32 devices in a mesh: gx: 2 (over x), gy: 4 (over z), gz: 4 (over y, core).
Axes of the slice: x: 2, y: 2, z: 4, core: 2. Of those that a mesh axis runs over, the one named last changes fastest.
Arguments:
- gas: float32 [64, 8, 32, 512], P(None, 'gx', 'gy', 'gz'), may hold values from 0 to 1
- droplet: float32 [32, 64, 4096], P(None, None, ('gx', 'gy', 'gz')), may hold values from 0 to 1
- owner: int32 [4096, 1], P(('gx', 'gy', 'gz')), may hold values from 0 to 15; in each aligned block of 128 rows (0 to 127, 128 to 255, ...) at most 16 rows name the same one
- cells: int32 [8, 4096], P(None, ('gx', 'gy', 'gz')), may hold values from 0 to 4095
- weights: float32 [8, 4096], P(None, ('gx', 'gy', 'gz')), may hold values from 0.1 to 1
- mass: float32 [4096], P(('gx', 'gy', 'gz')), may hold values from 0.25 to 4
- liquid_rate: float32 [64], replicated, may hold values from 0.05 to 0.45
- surface_rate: float32 [64], replicated, may hold values from 0.05 to 0.5
- gas_rate: float32 [64], replicated, may hold values from 0.04 to 0.16
Outputs:
- gas_next: float32 [64, 8, 32, 512], P(None, 'gx', 'gy', 'gz')
- droplet_next: float32 [32, 64, 4096], P(None, None, ('gx', 'gy', 'gz'))
The draws below stay inside these ranges and needn't reach their ends.
Inputs may be any that keep to these rules, and one draw needn't show every extreme that they name: `owner`: among the 128 parcels of one device at most 16 name the same gas device, and some gas device is named by exactly 16 of them.
All inputs are finite; a program needn't handle non-finite values.
Results may differ from the reference program's by a relative error of at most 0.00002.
Values sent between devices are 32-bit elements; how exact they have to be, the bound alone decides.
No kernel may reach another device: no remote copies, remote signals or barrier semaphores. Data moves between devices by JAX's collectives and lax.ppermute only.
A program may use at most 64 MiB of HBM per device.

```python
import math
import jax
import jax.numpy as jnp
import numpy as np

SPECIES = 64
NODES = 32
STENCIL = 8
DROP_STEPS = 4
GAS_STEPS = 2
CX = 4
CY = 8
CZ = 128
P_DEV = 128
CAP = 16
NX = 8
NY = 32
NZ = 512
PARCELS = 4096
N_GY = 4
N_GZ = 4


def with_ends(result, rng, least, largest):
    spot = [jax.random.randint(jax.random.fold_in(rng, axis), (), 0, length) for axis, length in enumerate(result.shape)]
    longest = result.shape.index(max(result.shape))
    beside = spot[:longest] + [(spot[longest] + 1) % result.shape[longest]] + spot[longest + 1:]
    return result.at[tuple(spot)].set(least).at[tuple(beside)].set(largest)


def shard_levels(own_key, extent, shards, smallest, largest):
    factor_of = 1.0
    for dim, shards_of in shards:
        draws = jax.random.uniform(jax.random.fold_in(jax.random.fold_in(own_key, 6), dim), (shards_of,), jnp.float32, smallest / len(shards), largest / len(shards))
        factor_of = factor_of * jnp.repeat(jnp.exp(draws), extent[dim] // shards_of).reshape((-1,) + (1,) * (len(extent) - 1 - dim))
    return factor_of


def routed_block(rng, own, number, rows, number_of, top, reach, skew):
    order = jax.random.permutation(rng, number_of)
    crowded, usual = shares(number_of, rows * top, reach, skew, True), shares(number_of, rows * top, reach, skew, False)
    places = jnp.arange(number_of)

    def named(sizes, turn):
        used = int((sizes > 0).sum())
        fixed = max(1, used // 4)
        passed = fixed + (places - fixed + turn * (used - fixed)) % max(1, number_of - fixed)
        return jnp.zeros((number_of,), jnp.int32).at[order[jnp.where(places < fixed, places, passed)]].set(jnp.asarray(sizes, jnp.int32))

    sizes = jnp.where(number % 4 == 0, named(crowded, number // 4), named(usual, number - number // 4 - 1))
    mixed = jax.random.permutation(jax.random.fold_in(own, 3), number_of)
    giver, sink = mixed[0:number_of // 2 * 2:2], mixed[1:number_of // 2 * 2:2]
    margin = jnp.minimum(sizes[giver] - 1, reach - sizes[sink]) // 2
    margin = jnp.where((giver == order[0]) | (sink == order[0]) | (sizes[sink] == 0), 0, jnp.maximum(margin, 0))
    passed = jax.random.randint(jax.random.fold_in(own, 4), (number_of // 2,), 0, 1 << 20) % (margin + 1)
    sizes = sizes.at[giver].add(-passed).at[sink].add(passed)
    items = jnp.searchsorted(jnp.cumsum(sizes), jnp.arange(rows * top), side="right").astype(jnp.int32)
    listing = items.reshape(top, rows).T
    listing = listing[jax.random.permutation(jax.random.fold_in(own, 1), rows)]
    turn = jax.random.randint(jax.random.fold_in(own, 2), (rows, 1), 0, top)
    return jnp.take_along_axis(listing, (jnp.arange(top)[None, :] + turn) % top, axis=1)


def shares(number_of, total, limit, lean, full):
    portions = [(1 << 20) // math.isqrt(grade ** lean) + 1 for grade in range(1, number_of + 1)]
    largest = limit if full else min(limit, max(-(-total // number_of), total * portions[0] // sum(portions)))
    least = 1 if total - largest >= number_of - 1 else 0
    counts, surplus = [largest] + [least] * (number_of - 1), total - largest - least * (number_of - 1)
    while surplus > 0:
        candidates = [i for i in range(1, number_of) if counts[i] < largest] or [i for i in range(1, number_of) if counts[i] < limit]
        whole, left = sum([portions[i] for i in candidates]), surplus
        for i in candidates:
            more = min(limit - counts[i], max(1, left * portions[i] // whole), surplus)
            counts[i] = counts[i] + more
            surplus = surplus - more
    return np.array(counts)


def setup_inputs(seed: int = 0) -> dict:
    key_list = jax.random.split(jax.random.key(seed), 10)
    gas = jnp.clip(1.0 * jax.random.uniform(key_list[0], (SPECIES, NX, NY, NZ), jnp.float32) ** shard_levels(key_list[0], (SPECIES, NX, NY, NZ), ((1, 2), (2, 4), (3, 4)), -0.2, 0.2), 0.0, 1.0)
    droplet = jnp.clip(1.0 * jax.random.uniform(key_list[1], (NODES, SPECIES, PARCELS), jnp.float32) ** shard_levels(key_list[1], (NODES, SPECIES, PARCELS), ((2, 32),), -0.2, 0.2), 0.0, 1.0)
    owner_keys = jax.random.split(jax.random.fold_in(key_list[2], 1), PARCELS // P_DEV)
    owner_turns = jax.random.permutation(jax.random.fold_in(key_list[2], 3), PARCELS // P_DEV)
    owner = jax.vmap(lambda own, number: routed_block(jax.random.fold_in(key_list[2], 2), own, number, P_DEV, N_GY * N_GZ, 1, CAP, 2))(owner_keys, owner_turns).reshape((PARCELS, 1))
    cells = with_ends(jax.random.randint(key_list[3], (STENCIL, PARCELS), 0, CX * CY * CZ), jax.random.fold_in(key_list[3], 1), 0, (CX * CY * CZ) - 1).astype(jnp.int32)
    weights = jnp.clip(0.1 + 0.9 * jax.random.uniform(key_list[4], (STENCIL, PARCELS), jnp.float32) ** shard_levels(key_list[4], (STENCIL, PARCELS), ((1, 32),), -0.2, 0.2), 0.1, 1.0)
    mass = jnp.clip(jnp.exp(math.log(4.0) - 2.7725887 * jax.random.uniform(key_list[5], (PARCELS,), jnp.float32) ** shard_levels(key_list[5], (PARCELS,), ((0, 32),), -0.2, 0.2)), 0.25, 4.0)
    liquid_rate = jnp.clip(jnp.exp(jax.random.uniform(key_list[6], (SPECIES,), jnp.float32, math.log(0.05), math.log(0.45))), 0.05, 0.45)
    surface_rate = jnp.clip(jnp.exp(jax.random.uniform(key_list[7], (SPECIES,), jnp.float32, math.log(0.05), math.log(0.5))), 0.05, 0.5)
    gas_rate = jnp.clip(jnp.exp(jax.random.uniform(key_list[8], (SPECIES,), jnp.float32, math.log(0.04), math.log(0.16))), 0.04, 0.16)
    return dict(gas=gas, droplet=droplet, owner=owner, cells=cells, weights=weights, mass=mass, liquid_rate=liquid_rate, surface_rate=surface_rate, gas_rate=gas_rate)


def droplet_steps(state, gas_at, liquid_rate, surface_rate):
    liquid_coef = liquid_rate[None, :, None]
    surface_coef = surface_rate[:, None]
    emitted = jnp.zeros(gas_at.shape, jnp.float32)
    for substep in range(DROP_STEPS):
        surface_flux = surface_coef * (state[-1] - gas_at)
        upper_node = jnp.concatenate([state[1:], state[-1:]], axis=0)
        lower_node = jnp.concatenate([state[1:2], state[:-1]], axis=0)
        state = state + liquid_coef * (upper_node - 2.0 * state + lower_node)
        state = state.at[-1].add(-surface_flux)
        emitted = emitted + surface_flux
    return state, emitted


def stencil_update(padded, field, gas_rate):
    beside = padded[:, 2:, 1:-1, 1:-1] + padded[:, :-2, 1:-1, 1:-1]
    beside = beside + padded[:, 1:-1, 2:, 1:-1] + padded[:, 1:-1, :-2, 1:-1]
    beside = beside + padded[:, 1:-1, 1:-1, 2:] + padded[:, 1:-1, 1:-1, :-2]
    return field + gas_rate[:, None, None, None] * (beside - 6.0 * field)


def reference(gas, droplet, owner, cells, weights, mass, liquid_rate, surface_rate, gas_rate):
    norm_wts = weights / jnp.sum(weights, axis=0, keepdims=True)
    parcel = jnp.arange(PARCELS, dtype=jnp.int32)
    slab_index = (parcel // P_DEV) // (N_GY * N_GZ)
    target = owner[:, 0]
    owner_row = target // N_GZ
    owner_col = target % N_GZ
    local_x = cells // (CY * CZ)
    local_y = (cells // CZ) % CY
    local_z = cells % CZ
    global_x = slab_index[None, :] * CX + local_x
    global_y = owner_row[None, :] * CY + local_y
    global_z = owner_col[None, :] * CZ + local_z
    global_cell = ((global_x * NY + global_y) * NZ + global_z).astype(jnp.int32)
    gasflat = gas.reshape(SPECIES, NX * NY * NZ)
    gas_at = jnp.zeros((SPECIES, PARCELS), jnp.float32)
    for corner in range(STENCIL):
        gas_at = gas_at + norm_wts[corner][None, :] * gasflat[:, global_cell[corner]]
    droplet_next, emitted = droplet_steps(droplet, gas_at, liquid_rate, surface_rate)
    source = mass[None, :] * emitted
    field = gas
    for substep in range(GAS_STEPS):
        padded = jnp.pad(field, ((0, 0), (1, 1), (1, 1), (1, 1)))
        field = stencil_update(padded, field, gas_rate)
    flat_out = field.reshape(SPECIES, NX * NY * NZ)
    for corner in range(STENCIL):
        flat_out = flat_out.at[:, global_cell[corner]].add(norm_wts[corner][None, :] * source)
    return flat_out.reshape(SPECIES, NX, NY, NZ), droplet_next
```

```python
import functools

import jax
import jax.numpy as jnp
from jax import lax
from jax.experimental import pallas as pl
from jax.experimental.pallas import tpu as pltpu
from jax.sharding import PartitionSpec as P

STENCIL = 8
DROP_STEPS = 4
GAS_STEPS = 2
LANES = 128
MIB = 1 << 20
NT = (((1,), (1,)), ((), ()))
HIGH = lax.Precision.HIGHEST
F32 = jnp.float32
BF16 = jnp.bfloat16


def iota(shape, dim):
    return lax.broadcasted_iota(jnp.int32, shape, dim)


def as_column(row):
    n = row.shape[1]
    return jnp.sum(jnp.where(iota((n, n), 0) == iota((n, n), 1), row, 0.0), axis=1, keepdims=True)


def split(value):
    scaled = value * 65537.0
    high = scaled - (scaled - value)
    return high.astype(BF16), (value - high).astype(BF16)


def surface_steps(nodes, gas_at, liquid, surface):
    emitted = None
    for step in range(DROP_STEPS):
        last = nodes[-1]
        flux = surface * (last - gas_at)
        emitted = flux if emitted is None else emitted + flux
        inner = [
            nodes[i] + liquid * (nodes[i + 1] - 2.0 * nodes[i] + nodes[i - 1])
            for i in range(1, len(nodes) - 1)
        ]
        if len(nodes) > 1:
            nodes = inner + [last + liquid * (nodes[-2] - last) - flux]
    return emitted


def surface_response(liquid, surface):
    zero = jnp.zeros_like(liquid)
    nodes = [zero] * (DROP_STEPS + 1)
    emitted = zero
    for step in range(DROP_STEPS):
        last = nodes[-1]
        flux = surface * (last - 1.0)
        emitted = emitted + flux
        inner = [
            nodes[i] + liquid * (nodes[i + 1] - 2.0 * nodes[i] + nodes[i - 1])
            for i in range(1, DROP_STEPS)
        ]
        nodes = [zero] + inner + [last + liquid * (nodes[-2] - last) - flux]
    return emitted, nodes[1:]


def pack_kernel(cap, tail, owner, cells, weights, mass, liquid, surface, send, slots):
    parcels = owner.shape[1]
    emitted = surface_steps(
        [tail[i] for i in range(DROP_STEPS)], 0.0, as_column(liquid[...]), as_column(surface[...])
    )
    wts = weights[...]
    norm = wts / jnp.sum(wts, axis=0, keepdims=True)
    mine = owner[...]
    column = jnp.transpose(jnp.broadcast_to(mine.astype(F32), (parcels, parcels)))
    earlier = (column == mine.astype(F32)) & (iota((parcels, parcels), 0) < iota((parcels, parcels), 1))
    rank = jnp.sum(jnp.where(earlier, 1.0, 0.0), axis=0, keepdims=True).astype(jnp.int32)
    slot = mine * cap + rank
    slots[...] = slot
    species = tail.shape[1]
    rest = jnp.zeros((LANES - species - 2 * STENCIL - 8, parcels), F32)
    values = jnp.concatenate(
        [
            mass[...] * emitted,
            cells[...].astype(F32),
            norm,
            jnp.broadcast_to(mass[...], (8, parcels)),
            rest,
        ],
        axis=0,
    )
    place = jnp.where(iota((send.shape[0], parcels), 0) == slot, 1.0, 0.0)
    send[...] = lax.dot_general(place, values, NT, precision=HIGH, preferred_element_type=F32)


def couple_kernel(cap, packed, rows, gas, liquid, surface, back, deposit, w_high, w_low, t_all):
    slots = rows.shape[0]
    species = liquid.shape[1]
    lines = gas.shape[0] // species
    table = jnp.transpose(rows[...])
    first = species
    cell = table[first : first + STENCIL]
    wts = table[first + STENCIL : first + 2 * STENCIL]
    mass = table[first + 2 * STENCIL : first + 2 * STENCIL + 1]
    cell_rows = [cell[k : k + 1] for k in range(STENCIL)]
    wts_rows = [wts[k : k + 1] for k in range(STENCIL)]
    whole = []
    for k in range(STENCIL):
        total = wts_rows[k]
        for other in range(STENCIL):
            if other != k:
                total = total + jnp.where(cell_rows[other] == cell_rows[k], wts_rows[other], 0.0)
        whole.append(total)
    line_of = jnp.floor(cell * (1.0 / LANES))
    lane_of = cell - LANES * line_of
    along = iota((LANES, slots), 0).astype(F32).astype(BF16)
    halves = [split(w) for w in whole]
    highs = [jnp.broadcast_to(h, (LANES, slots)) for h, _ in halves]
    lows = [jnp.broadcast_to(l, (LANES, slots)) for _, l in halves]

    @pl.loop(0, lines)
    def _(line):
        code = jnp.where(line_of == line.astype(F32), lane_of, -1.0).astype(BF16)
        high = jnp.zeros((LANES, slots), BF16)
        low = jnp.zeros((LANES, slots), BF16)
        for k in range(STENCIL):
            hit = jnp.broadcast_to(code[k : k + 1], (LANES, slots)) == along
            high = jnp.where(hit, highs[k], high)
            low = jnp.where(hit, lows[k], low)
        w_high[line] = high
        w_low[line] = low
        t_high, t_low = split(gas[pl.ds(line, species, stride=lines), :])
        t_all[line] = jnp.concatenate([t_high, t_low], axis=0)

    gathered = jnp.zeros((species, slots), F32)
    for line in range(lines):
        both = jnp.dot(t_all[line], w_high[line], preferred_element_type=F32)
        extra = jnp.dot(t_all[line, :species], w_low[line], preferred_element_type=F32)
        gathered = gathered + both[:species] + both[species:] + extra
    gas_rows = jnp.transpose(gathered)
    if packed:
        gas_rows = gas_rows.reshape(slots // cap, cap, species)
        gas_rows = jnp.concatenate([gas_rows[:, : cap // 2], gas_rows[:, cap // 2 :]], axis=2)
        back[...] = gas_rows.reshape(slots // 2, 2 * species)
    else:
        back[...] = jnp.concatenate([gas_rows, jnp.zeros((slots, LANES - species), F32)], axis=1)
    response, _ = surface_response(as_column(liquid[...]), as_column(surface[...]))
    source = table[:species] + mass * (response * gathered)
    s_high, s_low = split(source)
    s_all = jnp.concatenate([s_high, s_low], axis=0)
    for line in range(lines):
        both = lax.dot_general(s_all, w_high[line], NT, preferred_element_type=F32)
        extra = lax.dot_general(s_high, w_low[line], NT, preferred_element_type=F32)
        deposit[pl.ds(line, species, stride=lines), :] = both[:species] + both[species:] + extra


def droplet_kernel(state_in, liquid, surface, state_out):
    nodes, block, _ = state_in.shape
    species = liquid.shape[1]
    at = pl.program_id(0) * block + iota((block, species), 0)
    pick = at == iota((block, species), 1)
    liquid_col = jnp.sum(jnp.where(pick, liquid[...], 0.0), axis=1, keepdims=True)
    surface_col = jnp.sum(jnp.where(pick, surface[...], 0.0), axis=1, keepdims=True)
    state = state_in[...]
    for step in range(DROP_STEPS):
        upper = jnp.concatenate([state[1:], state[-1:]], axis=0)
        lower = jnp.concatenate([state[1:2], state[:-1]], axis=0)
        flux = surface_col * state[-1]
        state = state + liquid_col * (upper - 2.0 * state + lower)
        state = jnp.concatenate([state[:-1], (state[-1] - flux)[None]], axis=0)
    state_out[...] = state


def finish_kernel(cap, packed, tail, rows, slots, liquid, surface, out):
    species = liquid.shape[1]
    table = jnp.transpose(rows[...])
    count = rows.shape[0]
    parcels = slots.shape[1]
    at = iota((count, parcels), 0)
    slot = slots[...]
    if packed:
        half = cap // 2
        at = at // half * cap + at % half
        parts = [(table[:species], at), (table[species:], at + half)]
    else:
        parts = [(table[:species], at)]
    gas_at = jnp.zeros((species, parcels), F32)
    for values, index in parts:
        place = jnp.where(index == slot, 1.0, 0.0)
        gas_at = gas_at + jnp.dot(values, place, precision=HIGH, preferred_element_type=F32)
    _, response = surface_response(as_column(liquid[...]), as_column(surface[...]))
    for i in range(DROP_STEPS):
        out[i] = tail[i] + response[i] * gas_at


def with_halo(block, sides, width):
    for axis, dim in sides:
        count = lax.axis_size(axis)
        forward = [(i, i + 1) for i in range(count - 1)]
        backward = [(target, source) for source, target in forward]
        low = lax.ppermute(
            lax.slice_in_dim(block, block.shape[dim] - width, None, axis=dim), axis, forward
        )
        high = lax.ppermute(lax.slice_in_dim(block, 0, width, axis=dim), axis, backward)
        block = jnp.concatenate([low, block, high], axis=dim)
    return block


def stencil_update(padded, field, gas_rate):
    beside = padded[:, 2:, 1:-1, 1:-1] + padded[:, :-2, 1:-1, 1:-1]
    beside = beside + padded[:, 1:-1, 2:, 1:-1] + padded[:, 1:-1, :-2, 1:-1]
    beside = beside + padded[:, 1:-1, 1:-1, 2:] + padded[:, 1:-1, 1:-1, :-2]
    return field + gas_rate[:, None, None, None] * (beside - 6.0 * field)


def gas_step(field, gas_rate):
    padded = with_halo(field, (("gx", 1), ("gy", 2), ("gz", 3)), 1)
    return stencil_update(padded, field, gas_rate)


def full(shape):
    return pl.BlockSpec(shape, lambda *_: (0,) * len(shape))


def exchange(rows, group):
    width = rows.shape[1]
    chunks = rows.reshape(group, -1, width)
    chunks = lax.all_to_all(chunks, ("gy", "gz"), split_axis=0, concat_axis=0, tiled=True)
    return chunks.reshape(-1, width)


def on_device(gas, droplet, owner, cells, weights, mass, liquid_rate, surface_rate, gas_rate):
    group = lax.axis_size("gy") * lax.axis_size("gz")
    nodes, species, parcels = droplet.shape
    cap = 2 * parcels // group
    slots = group * cap
    packed = cap % 16 == 0
    lines = gas.shape[1] * gas.shape[2]
    flat = gas.reshape(species * lines, LANES)
    liquid = liquid_rate.reshape(1, species)
    surface = surface_rate.reshape(1, species)
    tail_block = nodes // DROP_STEPS - 1
    tail_spec = pl.BlockSpec((DROP_STEPS, species, parcels), lambda *_: (tail_block, 0, 0))
    rate_spec = full((1, species))

    send, slot = pl.pallas_call(
        functools.partial(pack_kernel, cap),
        grid=(1,),
        out_shape=(
            jax.ShapeDtypeStruct((slots, LANES), F32),
            jax.ShapeDtypeStruct((1, parcels), jnp.int32),
        ),
        in_specs=[
            tail_spec,
            full((1, parcels)),
            full((STENCIL, parcels)),
            full((STENCIL, parcels)),
            full((1, parcels)),
            rate_spec,
            rate_spec,
        ],
        out_specs=(full((slots, LANES)), full((1, parcels))),
        compiler_params=pltpu.CompilerParams(vmem_limit_bytes=16 * MIB),
        name="pack_parcels",
    )(droplet, owner.reshape(1, parcels), cells, weights, mass.reshape(1, parcels), liquid, surface)

    rows = exchange(send, group)

    back_rows = slots // 2 if packed else slots
    back, deposit = pl.pallas_call(
        functools.partial(couple_kernel, cap, packed),
        out_shape=(
            jax.ShapeDtypeStruct((back_rows, LANES), F32),
            jax.ShapeDtypeStruct((species * lines, LANES), F32),
        ),
        scratch_shapes=[
            pltpu.VMEM((lines, LANES, slots), BF16),
            pltpu.VMEM((lines, LANES, slots), BF16),
            pltpu.VMEM((lines, 2 * species, LANES), BF16),
        ],
        compiler_params=pltpu.CompilerParams(vmem_limit_bytes=32 * MIB),
        name="couple_gas",
    )(rows, flat, liquid, surface)

    returned = exchange(back, group)

    block = 16
    drop_spec = pl.BlockSpec((nodes, block, parcels), lambda i: (0, i, 0))
    evolved = pl.pallas_call(
        droplet_kernel,
        grid=(species // block,),
        out_shape=jax.ShapeDtypeStruct(droplet.shape, F32),
        in_specs=[drop_spec, rate_spec, rate_spec],
        out_specs=drop_spec,
        compiler_params=pltpu.CompilerParams(vmem_limit_bytes=16 * MIB),
        cost_estimate=pl.CostEstimate(flops=20 * droplet.size, bytes_accessed=8 * droplet.size, transcendentals=0),
        name="evolve_droplets",
    )(droplet, liquid, surface)

    droplet_next = pl.pallas_call(
        functools.partial(finish_kernel, cap, packed),
        grid=(1,),
        out_shape=jax.ShapeDtypeStruct(droplet.shape, F32),
        in_specs=[tail_spec, full((back_rows, LANES)), full((1, parcels)), rate_spec, rate_spec],
        out_specs=tail_spec,
        input_output_aliases={0: 0},
        compiler_params=pltpu.CompilerParams(vmem_limit_bytes=16 * MIB),
        name="finish_droplets",
    )(evolved, returned, slot, liquid, surface)

    field = gas
    for substep in range(GAS_STEPS):
        field = gas_step(field, gas_rate)
    return (field + deposit.reshape(gas.shape), droplet_next)


def solution(mesh):
    return jax.shard_map(
        on_device,
        mesh=mesh,
        in_specs=(
            P(None, "gx", "gy", "gz"),
            P(None, None, ("gx", "gy", "gz")),
            P(("gx", "gy", "gz"), None),
            P(None, ("gx", "gy", "gz")),
            P(None, ("gx", "gy", "gz")),
            P(("gx", "gy", "gz")),
            P(),
            P(),
            P(),
        ),
        out_specs=(P(None, "gx", "gy", "gz"), P(None, None, ("gx", "gy", "gz"))),
        check_vma=False,
    )
```

```python
import functools

import jax
import jax.numpy as jnp
from jax import lax
from jax.experimental import pallas as pl
from jax.experimental.pallas import tpu as pltpu
from jax.sharding import PartitionSpec as P

STENCIL = 8
DROP_STEPS = 4
GAS_STEPS = 2
LANES = 128
MIB = 1 << 20
NT = (((1,), (1,)), ((), ()))
HIGH = lax.Precision.HIGHEST
F32 = jnp.float32
BF16 = jnp.bfloat16


def iota(shape, dim):
    return lax.broadcasted_iota(jnp.int32, shape, dim)


def as_column(row):
    n = row.shape[1]
    return jnp.sum(jnp.where(iota((n, n), 0) == iota((n, n), 1), row, 0.0), axis=1, keepdims=True)


def split(value):
    scaled = value * 65537.0
    high = scaled - (scaled - value)
    return high.astype(BF16), (value - high).astype(BF16)


def surface_steps(nodes, gas_at, liquid, surface):
    emitted = None
    for step in range(DROP_STEPS):
        last = nodes[-1]
        flux = surface * (last - gas_at)
        emitted = flux if emitted is None else emitted + flux
        inner = [
            nodes[i] + liquid * (nodes[i + 1] - 2.0 * nodes[i] + nodes[i - 1])
            for i in range(1, len(nodes) - 1)
        ]
        if len(nodes) > 1:
            nodes = inner + [last + liquid * (nodes[-2] - last) - flux]
    return emitted


def surface_response(liquid, surface):
    zero = jnp.zeros_like(liquid)
    nodes = [zero] * (DROP_STEPS + 1)
    emitted = zero
    for step in range(DROP_STEPS):
        last = nodes[-1]
        flux = surface * (last - 1.0)
        emitted = emitted + flux
        inner = [
            nodes[i] + liquid * (nodes[i + 1] - 2.0 * nodes[i] + nodes[i - 1])
            for i in range(1, DROP_STEPS)
        ]
        nodes = [zero] + inner + [last + liquid * (nodes[-2] - last) - flux]
    return emitted, nodes[1:]


def pack_kernel(cap, tail, owner, cells, weights, mass, liquid, surface, send, slots):
    parcels = owner.shape[1]
    emitted = surface_steps(
        [tail[i] for i in range(DROP_STEPS)], 0.0, as_column(liquid[...]), as_column(surface[...])
    )
    wts = weights[...]
    norm = wts / jnp.sum(wts, axis=0, keepdims=True)
    mine = owner[...]
    column = jnp.transpose(jnp.broadcast_to(mine.astype(F32), (parcels, parcels)))
    earlier = (column == mine.astype(F32)) & (iota((parcels, parcels), 0) < iota((parcels, parcels), 1))
    rank = jnp.sum(jnp.where(earlier, 1.0, 0.0), axis=0, keepdims=True).astype(jnp.int32)
    slot = mine * cap + rank
    slots[...] = slot
    species = tail.shape[1]
    rest = jnp.zeros((LANES - species - 2 * STENCIL - 8, parcels), F32)
    values = jnp.concatenate(
        [
            mass[...] * emitted,
            cells[...].astype(F32),
            norm,
            jnp.broadcast_to(mass[...], (8, parcels)),
            rest,
        ],
        axis=0,
    )
    place = jnp.where(iota((send.shape[0], parcels), 0) == slot, 1.0, 0.0)
    send[...] = lax.dot_general(place, values, NT, precision=HIGH, preferred_element_type=F32)


def couple_kernel(cap, packed, rows, gas, liquid, surface, back, deposit, w_high, w_low, t_all):
    slots = rows.shape[0]
    species = liquid.shape[1]
    lines = gas.shape[0] // species
    table = jnp.transpose(rows[...])
    first = species
    cell = table[first : first + STENCIL]
    wts = table[first + STENCIL : first + 2 * STENCIL]
    mass = table[first + 2 * STENCIL : first + 2 * STENCIL + 1]
    cell_rows = [cell[k : k + 1] for k in range(STENCIL)]
    wts_rows = [wts[k : k + 1] for k in range(STENCIL)]
    whole = []
    for k in range(STENCIL):
        total = wts_rows[k]
        for other in range(STENCIL):
            if other != k:
                total = total + jnp.where(cell_rows[other] == cell_rows[k], wts_rows[other], 0.0)
        whole.append(total)
    line_of = jnp.floor(cell * (1.0 / LANES))
    lane_of = cell - LANES * line_of
    along = iota((LANES, slots), 0).astype(F32).astype(BF16)
    halves = [split(w) for w in whole]
    highs = [jnp.broadcast_to(h, (LANES, slots)) for h, _ in halves]
    lows = [jnp.broadcast_to(l, (LANES, slots)) for _, l in halves]

    @pl.loop(0, lines)
    def _(line):
        code = jnp.where(line_of == line.astype(F32), lane_of, -1.0).astype(BF16)
        high = jnp.zeros((LANES, slots), BF16)
        low = jnp.zeros((LANES, slots), BF16)
        for k in range(STENCIL):
            hit = jnp.broadcast_to(code[k : k + 1], (LANES, slots)) == along
            high = jnp.where(hit, highs[k], high)
            low = jnp.where(hit, lows[k], low)
        w_high[line] = high
        w_low[line] = low
        t_high, t_low = split(gas[pl.ds(line, species, stride=lines), :])
        t_all[line] = jnp.concatenate([t_high, t_low], axis=0)

    gathered = jnp.zeros((species, slots), F32)
    for line in range(lines):
        both = jnp.dot(t_all[line], w_high[line], preferred_element_type=F32)
        extra = jnp.dot(t_all[line, :species], w_low[line], preferred_element_type=F32)
        gathered = gathered + both[:species] + both[species:] + extra
    gas_rows = jnp.transpose(gathered)
    if packed:
        gas_rows = gas_rows.reshape(slots // cap, cap, species)
        gas_rows = jnp.concatenate([gas_rows[:, : cap // 2], gas_rows[:, cap // 2 :]], axis=2)
        back[...] = gas_rows.reshape(slots // 2, 2 * species)
    else:
        back[...] = jnp.concatenate([gas_rows, jnp.zeros((slots, LANES - species), F32)], axis=1)
    response, _ = surface_response(as_column(liquid[...]), as_column(surface[...]))
    source = table[:species] + mass * (response * gathered)
    s_high, s_low = split(source)
    s_all = jnp.concatenate([s_high, s_low], axis=0)
    for line in range(lines):
        both = lax.dot_general(s_all, w_high[line], NT, preferred_element_type=F32)
        extra = lax.dot_general(s_high, w_low[line], NT, preferred_element_type=F32)
        deposit[pl.ds(line, species, stride=lines), :] = both[:species] + both[species:] + extra


def droplet_kernel(state_in, liquid, surface, state_out):
    nodes, block, _ = state_in.shape
    species = liquid.shape[1]
    at = pl.program_id(0) * block + iota((block, species), 0)
    pick = at == iota((block, species), 1)
    liquid_col = jnp.sum(jnp.where(pick, liquid[...], 0.0), axis=1, keepdims=True)
    surface_col = jnp.sum(jnp.where(pick, surface[...], 0.0), axis=1, keepdims=True)
    state = state_in[...]
    for step in range(DROP_STEPS):
        upper = jnp.concatenate([state[1:], state[-1:]], axis=0)
        lower = jnp.concatenate([state[1:2], state[:-1]], axis=0)
        flux = surface_col * state[-1]
        state = state + liquid_col * (upper - 2.0 * state + lower)
        state = jnp.concatenate([state[:-1], (state[-1] - flux)[None]], axis=0)
    state_out[...] = state


def finish_kernel(cap, packed, tail, rows, slots, liquid, surface, out):
    species = liquid.shape[1]
    table = jnp.transpose(rows[...])
    count = rows.shape[0]
    parcels = slots.shape[1]
    at = iota((count, parcels), 0)
    slot = slots[...]
    if packed:
        half = cap // 2
        at = at // half * cap + at % half
        parts = [(table[:species], at), (table[species:], at + half)]
    else:
        parts = [(table[:species], at)]
    gas_at = jnp.zeros((species, parcels), F32)
    for values, index in parts:
        place = jnp.where(index == slot, 1.0, 0.0)
        gas_at = gas_at + jnp.dot(values, place, precision=HIGH, preferred_element_type=F32)
    _, response = surface_response(as_column(liquid[...]), as_column(surface[...]))
    for i in range(DROP_STEPS):
        out[i] = tail[i] + response[i] * gas_at


def place_on(axis):
    index, count = lax.axis_index(axis), lax.axis_size(axis)
    even = lax.rem(index, 2) == 0
    below = jnp.where(index > 0, 1.0, 0.0).astype(F32)
    above = jnp.where(index < count - 1, 1.0, 0.0).astype(F32)
    return even, below, above


def swaps(axis):
    count = lax.axis_size(axis)
    rounds = []
    for first in range(2):
        pairs = [(i, i + 1) for i in range(first, count - 1, 2)]
        if pairs:
            rounds.append(pairs + [(j, i) for i, j in pairs])
    return rounds


def swap_all(messages, axis):
    return [lax.ppermute(m, axis, pairs) for m, pairs in zip(messages, swaps(axis), strict=True)]


def low_high(even, first, second):
    if second is None:
        second = jnp.zeros_like(first)
    return jnp.where(even, second, first), jnp.where(even, first, second)


def beside_z(block):
    axis = block.ndim - 1
    lane = iota(block.shape, axis)
    before = jnp.where(lane == 0, 0.0, pltpu.roll(block, 1, axis))
    after = jnp.where(lane == LANES - 1, 0.0, pltpu.roll(block, LANES - 1, axis))
    return before + after


def beside_y(block, low, high):
    axis = block.ndim - 2
    size = block.shape[axis]
    row = iota(block.shape, axis)
    before = jnp.where(row == 0, low, pltpu.roll(block, 1, axis))
    after = jnp.where(row == size - 1, high, pltpu.roll(block, size - 1, axis))
    return before + after


def beside_x(block, low, high):
    before = jnp.concatenate([low[None], block[:-1]], axis=0)
    after = jnp.concatenate([block[1:], high[None]], axis=0)
    return before + after


def x_faces_kernel(gas, *refs):
    sends, sems = refs[:-1], refs[-1]
    even, _, _ = place_on("gx")
    top = gas.shape[1] - 2
    copies = []
    for turn, send in enumerate(sends):
        start = jnp.where(even == (turn == 0), top, 0)
        copies.append(pltpu.make_async_copy(gas.at[:, pl.ds(start, 2)], send, sems.at[turn]))
    for copy in copies:
        copy.start()
    for copy in copies:
        copy.wait()


def y_faces_kernel(size_x, size_y, turns_x, gas, *refs):
    xs, (send_a, send_b) = refs[:turns_x], refs[turns_x:]
    species = send_a.shape[1]
    lines = size_x * size_y
    even, _, _ = place_on("gy")
    even_x, _, _ = place_on("gx")
    for turn, send in enumerate((send_a, send_b)):
        up = even == (turn == 0)
        near = jnp.where(up, size_y - 1, 0)
        far = jnp.where(up, size_y - 2, 1)
        for x in range(size_x):
            send[x] = gas[pl.ds(x * size_y + near, species, stride=lines), :]
            send[size_x + x] = gas[pl.ds(x * size_y + far, species, stride=lines), :]
        edges = []
        for layer in (1, 0):
            parts = [x[pl.ds(layer * size_y + near, species, stride=2 * size_y), :] for x in xs]
            edges.append(low_high(even_x, parts[0], parts[1] if turns_x == 2 else None))
        send[2 * size_x] = edges[0][0]
        send[2 * size_x + 1] = edges[1][1]


def first_step_kernel(size_x, size_y, turns_x, gas, *refs):
    xs, refs = refs[:turns_x], refs[turns_x:]
    ya, yb, rate_s, rate, field, side_x, side_y, za, zb, y_low, y_high = refs
    species = rate.shape[1]
    lines = size_x * size_y
    even_x, below_x, above_x = place_on("gx")
    even_y, below_y, above_y = place_on("gy")
    even_z, _, _ = place_on("gz")
    for plane in range(2 * size_x + 2):
        y_low[plane], y_high[plane] = low_high(even_y, ya[plane], yb[plane])
    column = as_column(rate[...])
    for side, (halo, row, exists) in enumerate(((y_low, 0, below_y), (y_high, size_y - 1, above_y))):
        for x in range(size_x):
            near = halo[x]
            before = halo[x - 1] if x > 0 else halo[2 * size_x]
            after = halo[x + 1] if x < size_x - 1 else halo[2 * size_x + 1]
            own = gas[pl.ds(x * size_y + row, species, stride=lines), :]
            total = before + after + halo[size_x + x] + exists * own + beside_z(near)
            side_y[side, x] = near + column * (total - 6.0 * near)

    def x_halo(at):
        parts = [x[at] for x in xs]
        return low_high(even_x, parts[0], parts[1] if turns_x == 2 else None)

    @pl.loop(0, species, unroll=2)
    def _(s):
        r = rate_s[0, s]
        own = gas[pl.ds(s * lines, lines), :].reshape(size_x, size_y, LANES)
        layers = [x_halo(pl.ds((2 * s + i) * size_y, size_y)) for i in range(2)]
        low, low_far = layers[1][0], layers[0][0]
        high, high_far = layers[0][1], layers[1][1]
        here = pl.ds(s, 1)
        total = beside_x(own, low, high) + beside_z(own)
        total = total + beside_y(own, y_low[:size_x, here, :], y_high[:size_x, here, :])
        field[pl.ds(s * lines, lines), :] = (own + r * (total - 6.0 * own)).reshape(lines, LANES)
        sides = ((low, low_far, own[0], below_x), (high, high_far, own[-1], above_x))
        for side, (near, far, inner, exists) in enumerate(sides):
            edge = 2 * size_x + side
            total = far + exists * inner + beside_z(near)
            total = total + beside_y(near, y_low[edge, here, :], y_high[edge, here, :])
            side_x[side, s] = near + r * (total - 6.0 * near)

    low_rows, high_rows = [], []

    def add_columns(block):
        turned = jnp.transpose(block)
        low_rows.append(turned[:1])
        high_rows.append(turned[-1:])

    for ref in (gas, field):
        for i in range(species * lines // LANES):
            add_columns(ref[i * LANES : (i + 1) * LANES, :])
    per = LANES // size_y
    for side in range(2):
        for i in range(species // per):
            parts = []
            for x in xs:
                near = x[...].reshape(species, 2, size_y, LANES)[i * per : (i + 1) * per, 1 - side]
                parts.append(near.reshape(LANES, LANES))
            add_columns(low_high(even_x, parts[0], parts[1] if turns_x == 2 else None)[side])
    for halo in (y_low, y_high):
        for i in range(size_x * species // LANES):
            each = LANES // species
            add_columns(halo[i * each : (i + 1) * each].reshape(LANES, LANES))
    rest = jnp.zeros((za.shape[0] - len(low_rows), LANES), F32)
    low = jnp.concatenate(low_rows + [rest], axis=0)
    high = jnp.concatenate(high_rows + [rest], axis=0)
    za[...] = jnp.where(even_z, high, low)
    zb[...] = jnp.where(even_z, low, high)


def second_step_kernel(
    size_x, size_y, field, side_x, side_y, za, zb, za_in, zb_in, rate_s, rate, deposit, out, halo, halo_x, halo_y, halo_next
):
    species = rate.shape[1]
    lines = size_x * size_y
    even, below, above = place_on("gz")
    low, high = low_high(even, za_in[...], zb_in[...])
    own_low, own_high = low_high(even, za[...], zb[...])
    count = species * lines // LANES
    each = LANES // lines
    row, lane = iota((count, LANES), 0), iota((count, LANES), 1)
    rates = jnp.zeros((count, LANES), F32)
    for part in range(each):
        pick = iota((count, species), 1) == iota((count, species), 0) * each + part
        of_row = jnp.sum(jnp.where(pick, rate[...], 0.0), axis=1, keepdims=True)
        rates = jnp.where(lane // lines == part, of_row, rates)
    next_low = low[count : 2 * count] + below * rates * own_low[:count]
    next_high = high[count : 2 * count] + above * rates * own_high[:count]

    def spread(low_row, high_row):
        turned = iota((LANES, LANES), 0)
        rows = jnp.where(turned == 0, low_row, jnp.where(turned == LANES - 1, high_row, 0.0))
        return jnp.transpose(rows)

    for i in range(count):
        at = slice(i * LANES, (i + 1) * LANES)
        halo[at, :] = spread(low[i : i + 1], high[i : i + 1])
        halo_next[at, :] = spread(next_low[i : i + 1], next_high[i : i + 1])
    first = 2 * count
    for i in range(2 * species * size_y // LANES):
        halo_x[i * LANES : (i + 1) * LANES, :] = spread(low[first + i : first + i + 1], high[first + i : first + i + 1])
    first = first + 2 * species * size_y // LANES
    for i in range(2 * species * size_x // LANES):
        halo_y[i * LANES : (i + 1) * LANES, :] = spread(low[first + i : first + i + 1], high[first + i : first + i + 1])
    column = as_column(rate[...])
    for side in range(2):
        for x in range(size_x):
            at = pl.ds((side * size_x + x) * species, species)
            halo_y[at, :] = side_y[side, x] + column * halo_y[at, :]

    @pl.loop(0, species, unroll=2)
    def _(s):
        r = rate_s[0, s]
        at = pl.ds(s * lines, lines)
        now = (field[at, :] + r * halo[at, :]).reshape(size_x, size_y, LANES)
        x_low, x_high = [
            side_x[side, s] + r * halo_x[pl.ds((side * species + s) * size_y, size_y), :] for side in range(2)
        ]
        y_low, y_high = [
            jnp.concatenate(
                [halo_y[pl.ds((side * size_x + x) * species + s, 1), :][None] for x in range(size_x)], axis=0
            )
            for side in range(2)
        ]
        total = beside_x(now, x_low, x_high) + beside_y(now, y_low, y_high) + beside_z(now)
        total = total + halo_next[at, :].reshape(now.shape)
        result = now + r * (total - 6.0 * now)
        out[at, :] = result.reshape(lines, LANES) + deposit[at, :]


def full(shape):
    return pl.BlockSpec(shape, lambda *_: (0,) * len(shape))


def exchange(rows, group):
    width = rows.shape[1]
    chunks = rows.reshape(group, -1, width)
    chunks = lax.all_to_all(chunks, ("gy", "gz"), split_axis=0, concat_axis=0, tiled=True)
    return chunks.reshape(-1, width)


def on_device(gas, droplet, owner, cells, weights, mass, liquid_rate, surface_rate, gas_rate):
    group = lax.axis_size("gy") * lax.axis_size("gz")
    nodes, species, parcels = droplet.shape
    cap = 2 * parcels // group
    slots = group * cap
    packed = cap % 16 == 0
    lines = gas.shape[1] * gas.shape[2]
    flat = gas.reshape(species * lines, LANES)
    liquid = liquid_rate.reshape(1, species)
    surface = surface_rate.reshape(1, species)
    tail_block = nodes // DROP_STEPS - 1
    tail_spec = pl.BlockSpec((DROP_STEPS, species, parcels), lambda *_: (tail_block, 0, 0))
    rate_spec = full((1, species))

    send, slot = pl.pallas_call(
        functools.partial(pack_kernel, cap),
        grid=(1,),
        out_shape=(
            jax.ShapeDtypeStruct((slots, LANES), F32),
            jax.ShapeDtypeStruct((1, parcels), jnp.int32),
        ),
        in_specs=[
            tail_spec,
            full((1, parcels)),
            full((STENCIL, parcels)),
            full((STENCIL, parcels)),
            full((1, parcels)),
            rate_spec,
            rate_spec,
        ],
        out_specs=(full((slots, LANES)), full((1, parcels))),
        compiler_params=pltpu.CompilerParams(vmem_limit_bytes=4 * MIB),
        name="pack_parcels",
    )(droplet, owner.reshape(1, parcels), cells, weights, mass.reshape(1, parcels), liquid, surface)

    rows = exchange(send, group)

    back_rows = slots // 2 if packed else slots
    back, deposit = pl.pallas_call(
        functools.partial(couple_kernel, cap, packed),
        out_shape=(
            jax.ShapeDtypeStruct((back_rows, LANES), F32),
            jax.ShapeDtypeStruct((species * lines, LANES), F32),
        ),
        scratch_shapes=[
            pltpu.VMEM((lines, LANES, slots), BF16),
            pltpu.VMEM((lines, LANES, slots), BF16),
            pltpu.VMEM((lines, 2 * species, LANES), BF16),
        ],
        compiler_params=pltpu.CompilerParams(vmem_limit_bytes=12 * MIB),
        name="couple_gas",
    )(rows, flat, liquid, surface)

    returned = exchange(back, group)

    block = 16
    drop_spec = pl.BlockSpec((nodes, block, parcels), lambda i: (0, i, 0))
    evolved = pl.pallas_call(
        droplet_kernel,
        grid=(species // block,),
        out_shape=jax.ShapeDtypeStruct(droplet.shape, F32),
        in_specs=[drop_spec, rate_spec, rate_spec],
        out_specs=drop_spec,
        compiler_params=pltpu.CompilerParams(vmem_limit_bytes=8 * MIB),
        cost_estimate=pl.CostEstimate(flops=20 * droplet.size, bytes_accessed=8 * droplet.size, transcendentals=0),
        name="evolve_droplets",
    )(droplet, liquid, surface)

    droplet_next = pl.pallas_call(
        functools.partial(finish_kernel, cap, packed),
        grid=(1,),
        out_shape=jax.ShapeDtypeStruct(droplet.shape, F32),
        in_specs=[tail_spec, full((back_rows, LANES)), full((1, parcels)), rate_spec, rate_spec],
        out_specs=tail_spec,
        input_output_aliases={0: 0},
        compiler_params=pltpu.CompilerParams(vmem_limit_bytes=4 * MIB),
        name="finish_droplets",
    )(evolved, returned, slot, liquid, surface)

    size_x, size_y = gas.shape[1], gas.shape[2]
    rate = gas_rate.reshape(1, species)
    smem = pl.BlockSpec(memory_space=pltpu.SMEM)
    vmem = pl.BlockSpec(memory_space=pltpu.VMEM)
    turns_x = len(swaps("gx"))
    x_shape = jax.ShapeDtypeStruct((species, 2, size_y, LANES), F32)
    x_sends = pl.pallas_call(
        x_faces_kernel,
        out_shape=[x_shape] * turns_x,
        in_specs=[pl.BlockSpec(memory_space=pl.ANY)],
        out_specs=[vmem] * turns_x,
        scratch_shapes=[pltpu.SemaphoreType.DMA((2,))],
        compiler_params=pltpu.CompilerParams(vmem_limit_bytes=4 * MIB),
        name="x_faces",
    )(gas)
    x_halo = [x.reshape(-1, LANES) for x in swap_all(x_sends, "gx")]
    y_shape = (2 * size_x + 2, species, LANES)
    y_sends = pl.pallas_call(
        functools.partial(y_faces_kernel, size_x, size_y, turns_x),
        out_shape=[jax.ShapeDtypeStruct(y_shape, F32)] * 2,
        compiler_params=pltpu.CompilerParams(vmem_limit_bytes=6 * MIB),
        name="y_faces",
    )(flat, *x_halo)
    y_halo = swap_all(y_sends, "gy")
    z_shape = (48, LANES)
    field, side_x, side_y, *z_sends = pl.pallas_call(
        functools.partial(first_step_kernel, size_x, size_y, turns_x),
        out_shape=(
            jax.ShapeDtypeStruct(flat.shape, F32),
            jax.ShapeDtypeStruct((2, species, size_y, LANES), F32),
            jax.ShapeDtypeStruct((2, size_x, species, LANES), F32),
            jax.ShapeDtypeStruct(z_shape, F32),
            jax.ShapeDtypeStruct(z_shape, F32),
        ),
        in_specs=[vmem] * (turns_x + 3) + [smem, vmem],
        scratch_shapes=[pltpu.VMEM(y_shape, F32), pltpu.VMEM(y_shape, F32)],
        compiler_params=pltpu.CompilerParams(vmem_limit_bytes=10 * MIB),
        name="first_gas_step",
    )(flat, *x_halo, *y_halo, rate, rate)
    z_halo = swap_all(z_sends, "gz")
    gas_next = pl.pallas_call(
        functools.partial(second_step_kernel, size_x, size_y),
        out_shape=jax.ShapeDtypeStruct(flat.shape, F32),
        in_specs=[vmem] * 7 + [smem, vmem, vmem],
        scratch_shapes=[
            pltpu.VMEM(flat.shape, F32),
            pltpu.VMEM((2 * species * size_y, LANES), F32),
            pltpu.VMEM((2 * species * size_x, LANES), F32),
            pltpu.VMEM(flat.shape, F32),
        ],
        compiler_params=pltpu.CompilerParams(vmem_limit_bytes=10 * MIB),
        name="second_gas_step",
    )(field, side_x, side_y, *z_sends, *z_halo, rate, rate, deposit)
    return (gas_next.reshape(gas.shape), droplet_next)


def solution(mesh):
    return jax.shard_map(
        on_device,
        mesh=mesh,
        in_specs=(
            P(None, "gx", "gy", "gz"),
            P(None, None, ("gx", "gy", "gz")),
            P(("gx", "gy", "gz"), None),
            P(None, ("gx", "gy", "gz")),
            P(None, ("gx", "gy", "gz")),
            P(("gx", "gy", "gz")),
            P(),
            P(),
            P(),
        ),
        out_specs=(P(None, "gx", "gy", "gz"), P(None, None, ("gx", "gy", "gz"))),
        check_vma=False,
    )
```

```python
import functools

import jax
import jax.numpy as jnp
from jax import lax
from jax.experimental import pallas as pl
from jax.experimental.pallas import tpu as pltpu
from jax.sharding import PartitionSpec as P

STENCIL = 8
DROP_STEPS = 4
GAS_STEPS = 2
LANES = 128
GROUPS = 4
MIB = 1 << 20
NT = (((1,), (1,)), ((), ()))
HIGH = lax.Precision.HIGHEST
F32 = jnp.float32
BF16 = jnp.bfloat16


def iota(shape, dim):
    return lax.broadcasted_iota(jnp.int32, shape, dim)


def as_column(row):
    n = row.shape[1]
    return jnp.sum(jnp.where(iota((n, n), 0) == iota((n, n), 1), row, 0.0), axis=1, keepdims=True)


def leading(value):
    scaled = value * 65537.0
    return scaled - (scaled - value)


def split(value):
    high = leading(value)
    return high.astype(BF16), (value - high).astype(BF16)


def split_all(value):
    high = leading(value)
    rest = value - high
    middle = leading(rest)
    return high.astype(BF16), middle.astype(BF16), (rest - middle).astype(BF16)


def one_hot(hit):
    return jnp.where(hit, 1.0, 0.0).astype(BF16)


def surface_steps(nodes, gas_at, liquid, surface):
    emitted = None
    for step in range(DROP_STEPS):
        last = nodes[-1]
        flux = surface * (last - gas_at)
        emitted = flux if emitted is None else emitted + flux
        inner = [
            nodes[i] + liquid * (nodes[i + 1] - 2.0 * nodes[i] + nodes[i - 1])
            for i in range(1, len(nodes) - 1)
        ]
        if len(nodes) > 1:
            nodes = inner + [last + liquid * (nodes[-2] - last) - flux]
    return emitted


def surface_response(liquid, surface):
    zero = jnp.zeros_like(liquid)
    nodes = [zero] * (DROP_STEPS + 1)
    emitted = zero
    for step in range(DROP_STEPS):
        last = nodes[-1]
        flux = surface * (last - 1.0)
        emitted = emitted + flux
        inner = [
            nodes[i] + liquid * (nodes[i + 1] - 2.0 * nodes[i] + nodes[i - 1])
            for i in range(1, DROP_STEPS)
        ]
        nodes = [zero] + inner + [last + liquid * (nodes[-2] - last) - flux]
    return emitted, nodes[1:]


def pack_kernel(
    cap, droplet, gas, owner, cells, weights, mass, liquid, surface, send, slots, near_gas, tail, sems
):
    parcels = owner.shape[1]
    nodes, species = droplet.shape[0], droplet.shape[1]
    load_tail = pltpu.make_async_copy(droplet.at[pl.ds(nodes - DROP_STEPS, DROP_STEPS)], tail, sems.at[0])
    load_gas = pltpu.make_async_copy(gas, near_gas, sems.at[1])
    load_tail.start()
    load_gas.start()
    wts = weights[...]
    norm = wts / jnp.sum(wts, axis=0, keepdims=True)
    mine = owner[...]
    column = jnp.transpose(jnp.broadcast_to(mine.astype(F32), (parcels, parcels)))
    earlier = (column == mine.astype(F32)) & (iota((parcels, parcels), 0) < iota((parcels, parcels), 1))
    rank = jnp.sum(jnp.where(earlier, 1.0, 0.0), axis=0, keepdims=True).astype(jnp.int32)
    slot = mine * cap + rank
    slots[...] = slot
    place = one_hot(iota((send.shape[0], parcels), 0) == slot)
    rest = jnp.zeros((LANES - species - 2 * STENCIL - 8, parcels), F32)
    liquid_col, surface_col = as_column(liquid[...]), as_column(surface[...])
    load_tail.wait()
    emitted = surface_steps([tail[i] for i in range(DROP_STEPS)], 0.0, liquid_col, surface_col)
    values = jnp.concatenate(
        [
            mass[...] * emitted,
            cells[...].astype(F32),
            norm,
            jnp.broadcast_to(mass[...], (8, parcels)),
            rest,
        ],
        axis=0,
    )
    parts = jnp.concatenate(split_all(values), axis=0)
    placed = lax.dot_general(place, parts, NT, preferred_element_type=F32)
    send[...] = placed[:, :LANES] + placed[:, LANES : 2 * LANES] + placed[:, 2 * LANES :]
    load_gas.wait()


def faces_kernel(size_x, size_y, turns_x, near_gas, *sends):
    x_sends, y_sends = sends[:turns_x], sends[turns_x:]
    species = y_sends[0].shape[1]
    lines = size_x * size_y
    even_x, _, _ = place_on("gx")
    for turn, x_send in enumerate(x_sends):
        start = jnp.where(even_x == (turn == 0), size_x - 2, 0) * size_y

        @pl.loop(0, species, unroll=8)
        def _(s):
            x_send[pl.ds(s * 2 * size_y, 2 * size_y), :] = near_gas[pl.ds(s * lines + start, 2 * size_y), :]

    even_y, _, _ = place_on("gy")
    for turn, y_send in enumerate(y_sends):
        up = even_y == (turn == 0)
        near = jnp.where(up, size_y - 1, 0)
        far = jnp.where(up, size_y - 2, 1)
        for x in range(size_x):
            y_send[x] = near_gas[pl.ds(x * size_y + near, species, stride=lines), :]
            y_send[size_x + x] = near_gas[pl.ds(x * size_y + far, species, stride=lines), :]


def corner_kernel(size_x, ya, yb, *sends):
    even_x, _, _ = place_on("gx")
    even_y, _, _ = place_on("gy")
    for turn, send in enumerate(sends):
        x = jnp.where(even_x == (turn == 0), size_x - 1, 0)
        send[0], send[1] = low_high(even_y, ya[x], yb[x])


def couple_kernel(cap, packed, rows, gas, liquid, surface, back, deposit_out, deposit, w_high, w_low, sems):
    slots = rows.shape[0]
    species = liquid.shape[1]
    lines = gas.shape[0] // species
    table = jnp.transpose(rows[...])
    first = species
    cell = table[first : first + STENCIL]
    wts = table[first + STENCIL : first + 2 * STENCIL]
    mass = table[first + 2 * STENCIL : first + 2 * STENCIL + 1]
    cell_rows = [cell[k : k + 1] for k in range(STENCIL)]
    wts_rows = [wts[k : k + 1] for k in range(STENCIL)]
    whole = []
    for k in range(STENCIL):
        total = wts_rows[k]
        for other in range(STENCIL):
            if other != k:
                total = total + jnp.where(cell_rows[other] == cell_rows[k], wts_rows[other], 0.0)
        whole.append(total)
    tile = 16
    named = [jnp.broadcast_to(c.astype(jnp.int32), (tile, slots)).astype(jnp.int16) for c in cell_rows]
    halves = [split(w) for w in whole]
    highs = [jnp.broadcast_to(h, (tile, slots)) for h, _ in halves]
    lows = [jnp.broadcast_to(l, (tile, slots)) for _, l in halves]

    @pl.loop(0, lines, unroll=2)
    def _(line):
        for z in range(0, LANES, tile):
            along = (iota((tile, slots), 0) + (line * LANES + z)).astype(jnp.int16)
            high = jnp.zeros((tile, slots), BF16)
            low = jnp.zeros((tile, slots), BF16)
            for k in range(STENCIL):
                hit = named[k] == along
                high = jnp.where(hit, highs[k], high)
                low = jnp.where(hit, lows[k], low)
            w_high[line, z : z + tile] = high
            w_low[line, z : z + tile] = low

    gathered = jnp.zeros((species, slots), F32)
    for line in range(lines):
        t_high, t_low = split(gas[pl.ds(line, species, stride=lines), :])
        t_all = jnp.concatenate([t_high, t_low], axis=0)
        both = jnp.dot(t_all, w_high[line], preferred_element_type=F32)
        extra = jnp.dot(t_high, w_low[line], preferred_element_type=F32)
        gathered = gathered + both[:species] + both[species:] + extra
    gas_rows = jnp.transpose(gathered)
    if packed:
        gas_rows = gas_rows.reshape(slots // cap, cap, species)
        gas_rows = jnp.concatenate([gas_rows[:, : cap // 2], gas_rows[:, cap // 2 :]], axis=2)
        back[...] = gas_rows.reshape(slots // 2, 2 * species)
    else:
        back[...] = jnp.concatenate([gas_rows, jnp.zeros((slots, LANES - species), F32)], axis=1)
    response, _ = surface_response(as_column(liquid[...]), as_column(surface[...]))
    s_high, s_low = split(table[:species] + mass * (response * gathered))
    s_all = jnp.concatenate([s_high, s_low], axis=0)
    saves = []
    each = lines // GROUPS
    for line in range(lines):
        both = lax.dot_general(s_all, w_high[line], NT, preferred_element_type=F32)
        extra = lax.dot_general(s_high, w_low[line], NT, preferred_element_type=F32)
        deposit[line] = both[:species] + both[species:] + extra
        if line % each == each - 1:
            at = pl.ds(line + 1 - each, each)
            saves.append(pltpu.make_async_copy(deposit.at[at], deposit_out.at[at], sems.at[line // each]))
            saves[-1].start()
    for save in saves:
        save.wait()


def droplet_kernel(state_in, liquid, surface, state_out):
    nodes, species, _ = state_in.shape
    block = 8

    @pl.loop(0, species // block)
    def _(i):
        at = pl.ds(pl.multiple_of(i * block, block), block)
        pick = i * block + iota((block, species), 0) == iota((block, species), 1)
        liquid_col = jnp.sum(jnp.where(pick, liquid[...], 0.0), axis=1, keepdims=True)
        surface_col = jnp.sum(jnp.where(pick, surface[...], 0.0), axis=1, keepdims=True)
        wide = state_in.shape[2]
        rate = jnp.broadcast_to(liquid_col, (block, wide))
        keep = 1.0 - 2.0 * rate
        last_keep = jnp.broadcast_to(1.0 - liquid_col - surface_col, (block, wide))
        state = [state_in[node, at] for node in range(nodes)]
        for step in range(DROP_STEPS):
            state = (
                [keep * state[0] + (rate + rate) * state[1]]
                + [keep * state[n] + rate * (state[n - 1] + state[n + 1]) for n in range(1, nodes - 1)]
                + [last_keep * state[-1] + rate * state[-2]]
            )
        for node in range(nodes):
            state_out[node, at] = state[node]


def finish_kernel(cap, packed, tail, rows, slots, liquid, surface, out):
    species = liquid.shape[1]
    table = jnp.transpose(rows[...])
    count = rows.shape[0]
    parcels = slots.shape[1]
    at = iota((count, parcels), 0)
    slot = slots[...]
    if packed:
        half = cap // 2
        at = at // half * cap + at % half
        pairs = [(table[:species], at), (table[species:], at + half)]
    else:
        pairs = [(table[:species], at)]
    gas_at = jnp.zeros((species, parcels), F32)
    for values, index in pairs:
        parts = jnp.concatenate(split_all(values), axis=0)
        placed = jnp.dot(parts, one_hot(index == slot), preferred_element_type=F32)
        gas_at = gas_at + placed[:species] + placed[species : 2 * species] + placed[2 * species :]
    _, response = surface_response(as_column(liquid[...]), as_column(surface[...]))
    for i in range(DROP_STEPS):
        out[i] = tail[i] + response[i] * gas_at


def place_on(axis):
    index, count = lax.axis_index(axis), lax.axis_size(axis)
    even = lax.rem(index, 2) == 0
    below = jnp.where(index > 0, 1.0, 0.0).astype(F32)
    above = jnp.where(index < count - 1, 1.0, 0.0).astype(F32)
    return even, below, above


def swaps(axis):
    count = lax.axis_size(axis)
    rounds = []
    for first in range(2):
        pairs = [(i, i + 1) for i in range(first, count - 1, 2)]
        if pairs:
            rounds.append(pairs + [(j, i) for i, j in pairs])
    return rounds


def swap_all(messages, axis):
    return [lax.ppermute(m, axis, pairs) for m, pairs in zip(messages, swaps(axis), strict=True)]


def low_high(even, first, second):
    if second is None:
        second = jnp.zeros_like(first)
    return jnp.where(even, second, first), jnp.where(even, first, second)


def beside_z(block):
    axis = block.ndim - 1
    lane = iota(block.shape, axis)
    before = jnp.where(lane == 0, 0.0, pltpu.roll(block, 1, axis))
    after = jnp.where(lane == LANES - 1, 0.0, pltpu.roll(block, LANES - 1, axis))
    return before + after


def beside_y(block, low, high):
    axis = block.ndim - 2
    size = block.shape[axis]
    row = iota(block.shape, axis)
    before = jnp.where(row == 0, low, pltpu.roll(block, 1, axis))
    after = jnp.where(row == size - 1, high, pltpu.roll(block, size - 1, axis))
    return before + after


def beside_x(block, low, high):
    before = jnp.concatenate([low[None], block[:-1]], axis=0)
    after = jnp.concatenate([block[1:], high[None]], axis=0)
    return before + after


def first_step_kernel(size_x, size_y, turns_x, gas, *refs):
    xs, refs = refs[:turns_x], refs[turns_x:]
    corners, refs = refs[:turns_x], refs[turns_x:]
    ya, yb, rate_s, rate, _, field_out, side_x_out, side_y, za, zb, y_low, y_high, field, side_x, sems = refs
    species = rate.shape[1]
    lines = size_x * size_y
    even_x, below_x, above_x = place_on("gx")
    even_y, below_y, above_y = place_on("gy")
    even_z, _, _ = place_on("gz")
    for plane in range(2 * size_x):
        y_low[plane], y_high[plane] = low_high(even_y, ya[plane], yb[plane])
    for side, halo in enumerate((y_low, y_high)):
        parts = [corner[side] for corner in corners]
        edges = low_high(even_x, parts[0], parts[1] if turns_x == 2 else None)
        halo[2 * size_x], halo[2 * size_x + 1] = edges
    column = as_column(rate[...])
    for side, (halo, row, exists) in enumerate(((y_low, 0, below_y), (y_high, size_y - 1, above_y))):
        for x in range(size_x):
            near = halo[x]
            before = halo[x - 1] if x > 0 else halo[2 * size_x]
            after = halo[x + 1] if x < size_x - 1 else halo[2 * size_x + 1]
            own = gas[pl.ds(x * size_y + row, species, stride=lines), :]
            total = before + after + halo[size_x + x] + exists * own + beside_z(near)
            side_y[side, x] = near + column * (total - 6.0 * near)

    def x_halo(at):
        parts = [x[at] for x in xs]
        return low_high(even_x, parts[0], parts[1] if turns_x == 2 else None)

    @pl.loop(0, species, unroll=16)
    def _(s):
        r = rate_s[0, s]
        own = gas[pl.ds(s * lines, lines), :].reshape(size_x, size_y, LANES)
        layers = [x_halo(pl.ds((2 * s + i) * size_y, size_y)) for i in range(2)]
        low, low_far = layers[1][0], layers[0][0]
        high, high_far = layers[0][1], layers[1][1]
        here = pl.ds(s, 1)
        total = beside_x(own, low, high) + beside_z(own)
        total = total + beside_y(own, y_low[:size_x, here, :], y_high[:size_x, here, :])
        field[pl.ds(s * lines, lines), :] = (own + r * (total - 6.0 * own)).reshape(lines, LANES)
        sides = ((low, low_far, own[0], below_x), (high, high_far, own[-1], above_x))
        for side, (near, far, inner, exists) in enumerate(sides):
            edge = 2 * size_x + side
            total = far + exists * inner + beside_z(near)
            total = total + beside_y(near, y_low[edge, here, :], y_high[edge, here, :])
            side_x[side, s] = near + r * (total - 6.0 * near)

    saves = [
        pltpu.make_async_copy(field, field_out, sems.at[0]),
        pltpu.make_async_copy(side_x, side_x_out, sems.at[1]),
    ]
    for save in saves:
        save.start()
    low_rows, high_rows = [], []

    def add_columns(block):
        turned = jnp.transpose(block)
        low_rows.append(turned[:1])
        high_rows.append(turned[-1:])

    for ref in (gas, field):
        for i in range(species * lines // LANES):
            add_columns(ref[i * LANES : (i + 1) * LANES, :])
    per = LANES // size_y
    for side in range(2):
        for i in range(species // per):
            parts = []
            for x in xs:
                near = x[...].reshape(species, 2, size_y, LANES)[i * per : (i + 1) * per, 1 - side]
                parts.append(near.reshape(LANES, LANES))
            add_columns(low_high(even_x, parts[0], parts[1] if turns_x == 2 else None)[side])
    for halo in (y_low, y_high):
        for i in range(size_x * species // LANES):
            each = LANES // species
            add_columns(halo[i * each : (i + 1) * each].reshape(LANES, LANES))
    rest = jnp.zeros((za.shape[0] - len(low_rows), LANES), F32)
    low = jnp.concatenate(low_rows + [rest], axis=0)
    high = jnp.concatenate(high_rows + [rest], axis=0)
    za[...] = jnp.where(even_z, high, low)
    zb[...] = jnp.where(even_z, low, high)
    for save in saves:
        save.wait()


def second_step_kernel(
    size_x, size_y, field_in, side_x_in, side_y, za, zb, za_in, zb_in, rate_s, rate, deposit_in,
    out, halo, halo_x, halo_y, halo_next, field, side_x, deposit, sems,
):
    species = rate.shape[1]
    lines = size_x * size_y
    loads = [
        pltpu.make_async_copy(source, here, sems.at[i])
        for i, (source, here) in enumerate(((field_in, field), (side_x_in, side_x), (deposit_in, deposit)))
    ]
    for load in loads:
        load.start()
    even, below, above = place_on("gz")
    low, high = low_high(even, za_in[...], zb_in[...])
    own_low, own_high = low_high(even, za[...], zb[...])
    count = species * lines // LANES
    each = LANES // lines
    row, lane = iota((count, LANES), 0), iota((count, LANES), 1)
    rates = jnp.zeros((count, LANES), F32)
    for part in range(each):
        pick = iota((count, species), 1) == iota((count, species), 0) * each + part
        of_row = jnp.sum(jnp.where(pick, rate[...], 0.0), axis=1, keepdims=True)
        rates = jnp.where(lane // lines == part, of_row, rates)
    next_low = low[count : 2 * count] + below * rates * own_low[:count]
    next_high = high[count : 2 * count] + above * rates * own_high[:count]

    def spread(low_row, high_row):
        turned = iota((LANES, LANES), 0)
        rows = jnp.where(turned == 0, low_row, jnp.where(turned == LANES - 1, high_row, 0.0))
        return jnp.transpose(rows)

    for i in range(count):
        at = slice(i * LANES, (i + 1) * LANES)
        halo[at, :] = spread(low[i : i + 1], high[i : i + 1])
        halo_next[at, :] = spread(next_low[i : i + 1], next_high[i : i + 1])
    first = 2 * count
    for i in range(2 * species * size_y // LANES):
        halo_x[i * LANES : (i + 1) * LANES, :] = spread(low[first + i : first + i + 1], high[first + i : first + i + 1])
    first = first + 2 * species * size_y // LANES
    for i in range(2 * species * size_x // LANES):
        halo_y[i * LANES : (i + 1) * LANES, :] = spread(low[first + i : first + i + 1], high[first + i : first + i + 1])
    column = as_column(rate[...])
    for side in range(2):
        for x in range(size_x):
            at = pl.ds((side * size_x + x) * species, species)
            halo_y[at, :] = side_y[side, x] + column * halo_y[at, :]
    for load in loads:
        load.wait()

    @pl.loop(0, species, unroll=16)
    def _(s):
        r = rate_s[0, s]
        at = pl.ds(s * lines, lines)
        now = (field[at, :] + r * halo[at, :]).reshape(size_x, size_y, LANES)
        x_low, x_high = [
            side_x[side, s] + r * halo_x[pl.ds((side * species + s) * size_y, size_y), :] for side in range(2)
        ]
        y_low, y_high = [
            jnp.concatenate(
                [halo_y[pl.ds((side * size_x + x) * species + s, 1), :][None] for x in range(size_x)], axis=0
            )
            for side in range(2)
        ]
        total = beside_x(now, x_low, x_high) + beside_y(now, y_low, y_high) + beside_z(now)
        total = total + halo_next[at, :].reshape(now.shape)
        result = now + r * (total - 6.0 * now)
        out[at, :] = result.reshape(lines, LANES) + deposit[pl.ds(s, lines, stride=species), :]


def full(shape):
    return pl.BlockSpec(shape, lambda *_: (0,) * len(shape))


def lasts(microseconds):
    return pl.CostEstimate(flops=0, bytes_accessed=int(3.69e6 * microseconds), transcendentals=0)


def in_hbm(array):
    return pltpu.with_memory_space_constraint(array, pltpu.HBM)


def exchange(rows, group):
    width = rows.shape[1]
    chunks = rows.reshape(group, -1, width)
    chunks = lax.all_to_all(chunks, ("gy", "gz"), split_axis=0, concat_axis=0, tiled=True)
    return chunks.reshape(-1, width)


def on_device(gas, droplet, owner, cells, weights, mass, liquid_rate, surface_rate, gas_rate):
    group = lax.axis_size("gy") * lax.axis_size("gz")
    nodes, species, parcels = droplet.shape
    cap = 2 * parcels // group
    slots = group * cap
    packed = cap % 16 == 0
    lines = gas.shape[1] * gas.shape[2]
    flat = gas.reshape(species * lines, LANES)
    liquid = liquid_rate.reshape(1, species)
    surface = surface_rate.reshape(1, species)
    tail_block = nodes // DROP_STEPS - 1
    tail_spec = pl.BlockSpec((DROP_STEPS, species, parcels), lambda *_: (tail_block, 0, 0))
    rate_spec = full((1, species))
    size_x, size_y = gas.shape[1], gas.shape[2]
    rate = gas_rate.reshape(1, species)
    smem = pl.BlockSpec(memory_space=pltpu.SMEM)
    vmem = pl.BlockSpec(memory_space=pltpu.VMEM)
    hbm = pl.BlockSpec(memory_space=pl.ANY)
    whole = pl.BlockSpec()
    turns_x = len(swaps("gx"))
    x_shape = (species * 2 * size_y, LANES)
    y_shape = (2 * size_x, species, LANES)

    send, slot, near_gas = pl.pallas_call(
        functools.partial(pack_kernel, cap),
        grid=(1,),
        out_shape=[
            jax.ShapeDtypeStruct((slots, LANES), F32),
            jax.ShapeDtypeStruct((1, parcels), jnp.int32),
            pltpu.VMEM(flat.shape, F32),
        ],
        in_specs=[hbm, hbm, full((1, parcels)), full((STENCIL, parcels)), full((STENCIL, parcels)), full((1, parcels))]
        + [rate_spec] * 2,
        out_specs=[full((slots, LANES)), full((1, parcels)), vmem],
        scratch_shapes=[
            pltpu.VMEM((DROP_STEPS, species, parcels), F32),
            pltpu.SemaphoreType.DMA((2,)),
        ],
        compiler_params=pltpu.CompilerParams(vmem_limit_bytes=8 * MIB),
        cost_estimate=lasts(2.5),
        name="pack",
    )(
        in_hbm(droplet),
        in_hbm(flat),
        in_hbm(owner.reshape(1, parcels)),
        in_hbm(cells),
        in_hbm(weights),
        in_hbm(mass.reshape(1, parcels)),
        in_hbm(liquid),
        in_hbm(surface),
    )
    rows = exchange(send, group)

    faces = pl.pallas_call(
        functools.partial(faces_kernel, size_x, size_y, turns_x),
        out_shape=[jax.ShapeDtypeStruct(x_shape, F32)] * turns_x + [jax.ShapeDtypeStruct(y_shape, F32)] * 2,
        in_specs=[vmem],
        compiler_params=pltpu.CompilerParams(vmem_limit_bytes=4 * MIB),
        cost_estimate=lasts(0.6),
        name="faces",
    )(near_gas)
    x_halo = swap_all(faces[:turns_x], "gx")
    y_halo = swap_all(faces[turns_x:], "gy")

    evolved = pl.pallas_call(
        droplet_kernel,
        out_shape=jax.ShapeDtypeStruct(droplet.shape, F32),
        compiler_params=pltpu.CompilerParams(vmem_limit_bytes=8 * MIB),
        cost_estimate=lasts(2.0),
        name="evolve_droplets",
    )(droplet, liquid, surface)

    corners = pl.pallas_call(
        functools.partial(corner_kernel, size_x),
        out_shape=[jax.ShapeDtypeStruct((2, species, LANES), F32)] * turns_x,
        in_specs=[vmem] * 2,
        out_specs=[vmem] * turns_x,
        compiler_params=pltpu.CompilerParams(vmem_limit_bytes=4 * MIB),
        cost_estimate=lasts(0.3),
        name="corner_planes",
    )(*y_halo)
    corners = swap_all(corners, "gx")

    back_rows = slots // 2 if packed else slots
    w_shape = (lines, LANES, slots)
    deposit_shape = (lines, species, LANES)
    back, deposit = pl.pallas_call(
        functools.partial(couple_kernel, cap, packed),
        out_shape=[jax.ShapeDtypeStruct((back_rows, LANES), F32), pltpu.HBM(deposit_shape, F32)],
        in_specs=[vmem] * 2 + [whole] * 2,
        out_specs=[whole, hbm],
        scratch_shapes=[
            pltpu.VMEM(deposit_shape, F32),
            pltpu.VMEM(w_shape, BF16),
            pltpu.VMEM(w_shape, BF16),
            pltpu.SemaphoreType.DMA((GROUPS,)),
        ],
        compiler_params=pltpu.CompilerParams(vmem_limit_bytes=10 * MIB),
        cost_estimate=lasts(7.0),
        name="couple_gas",
    )(rows, near_gas, liquid, surface)

    returned = exchange(back, group)

    droplet_next = pl.pallas_call(
        functools.partial(finish_kernel, cap, packed),
        grid=(1,),
        out_shape=jax.ShapeDtypeStruct(droplet.shape, F32),
        in_specs=[tail_spec, full((back_rows, LANES)), full((1, parcels)), rate_spec, rate_spec],
        out_specs=tail_spec,
        input_output_aliases={0: 0},
        compiler_params=pltpu.CompilerParams(vmem_limit_bytes=4 * MIB),
        cost_estimate=lasts(1.8),
        name="finish_droplets",
    )(evolved, returned, slot, liquid, surface)

    z_shape = (48, LANES)
    full_y = (2 * size_x + 2, species, LANES)
    side_x_shape = (2, species, size_y, LANES)
    field, side_x, side_y, *z_sends = pl.pallas_call(
        functools.partial(first_step_kernel, size_x, size_y, turns_x),
        out_shape=[
            pltpu.HBM(flat.shape, F32),
            pltpu.HBM(side_x_shape, F32),
            jax.ShapeDtypeStruct((2, size_x, species, LANES), F32),
            jax.ShapeDtypeStruct(z_shape, F32),
            jax.ShapeDtypeStruct(z_shape, F32),
        ],
        in_specs=[vmem] * (2 * turns_x + 3) + [smem, whole, hbm],
        out_specs=[hbm] * 2 + [whole] * 3,
        scratch_shapes=[
            pltpu.VMEM(full_y, F32),
            pltpu.VMEM(full_y, F32),
            pltpu.VMEM(flat.shape, F32),
            pltpu.VMEM(side_x_shape, F32),
            pltpu.SemaphoreType.DMA((2,)),
        ],
        compiler_params=pltpu.CompilerParams(vmem_limit_bytes=8 * MIB),
        cost_estimate=lasts(3.8),
        name="first_gas_step",
    )(near_gas, *x_halo, *corners, *y_halo, rate, rate, in_hbm(evolved))
    z_halo = swap_all(z_sends, "gz")
    gas_next = pl.pallas_call(
        functools.partial(second_step_kernel, size_x, size_y),
        out_shape=jax.ShapeDtypeStruct(flat.shape, F32),
        in_specs=[hbm] * 2 + [whole] * 5 + [smem, whole, hbm],
        scratch_shapes=[
            pltpu.VMEM(flat.shape, F32),
            pltpu.VMEM((2 * species * size_y, LANES), F32),
            pltpu.VMEM((2 * species * size_x, LANES), F32),
            pltpu.VMEM(flat.shape, F32),
            pltpu.VMEM(flat.shape, F32),
            pltpu.VMEM(side_x_shape, F32),
            pltpu.VMEM(flat.shape, F32),
            pltpu.SemaphoreType.DMA((3,)),
        ],
        compiler_params=pltpu.CompilerParams(vmem_limit_bytes=10 * MIB),
        cost_estimate=lasts(5.0),
        name="second_gas_step",
    )(
        in_hbm(field),
        in_hbm(side_x),
        side_y,
        *z_sends,
        *z_halo,
        rate,
        rate,
        in_hbm(deposit.reshape(flat.shape)),
    )
    return (gas_next.reshape(gas.shape), droplet_next)


def solution(mesh):
    return jax.shard_map(
        on_device,
        mesh=mesh,
        in_specs=(
            P(None, "gx", "gy", "gz"),
            P(None, None, ("gx", "gy", "gz")),
            P(("gx", "gy", "gz"), None),
            P(None, ("gx", "gy", "gz")),
            P(None, ("gx", "gy", "gz")),
            P(("gx", "gy", "gz")),
            P(),
            P(),
            P(),
        ),
        out_specs=(P(None, "gx", "gy", "gz"), P(None, None, ("gx", "gy", "gz"))),
        check_vma=False,
    )
```

```python
import functools

import jax
import jax.numpy as jnp
from jax import lax
from jax.experimental import pallas as pl
from jax.experimental.pallas import tpu as pltpu
from jax.sharding import PartitionSpec as P

STENCIL = 8
DROP_STEPS = 4
GAS_STEPS = 2
LANES = 128
GROUPS = 4
MIB = 1 << 20
NT = (((1,), (1,)), ((), ()))
HIGH = lax.Precision.HIGHEST
F32 = jnp.float32
BF16 = jnp.bfloat16


def iota(shape, dim):
    return lax.broadcasted_iota(jnp.int32, shape, dim)


def as_column(row):
    n = row.shape[1]
    return jnp.sum(jnp.where(iota((n, n), 0) == iota((n, n), 1), row, 0.0), axis=1, keepdims=True)


def leading(value):
    scaled = value * 65537.0
    return scaled - (scaled - value)


def split(value):
    high = leading(value)
    return high.astype(BF16), (value - high).astype(BF16)


def split_all(value):
    high = leading(value)
    rest = value - high
    middle = leading(rest)
    return high.astype(BF16), middle.astype(BF16), (rest - middle).astype(BF16)


def one_hot(hit):
    return jnp.where(hit, 1.0, 0.0).astype(BF16)


def surface_steps(nodes, gas_at, liquid, surface):
    emitted = None
    for step in range(DROP_STEPS):
        last = nodes[-1]
        flux = surface * (last - gas_at)
        emitted = flux if emitted is None else emitted + flux
        inner = [
            nodes[i] + liquid * (nodes[i + 1] - 2.0 * nodes[i] + nodes[i - 1])
            for i in range(1, len(nodes) - 1)
        ]
        if len(nodes) > 1:
            nodes = inner + [last + liquid * (nodes[-2] - last) - flux]
    return emitted


def surface_response(liquid, surface):
    return surface_steps([jnp.zeros_like(liquid)] * DROP_STEPS, 1.0, liquid, surface)


def pack_kernel(
    cap, size_x, size_y, turns_x, droplet, gas, owner, cells, weights, mass, liquid, surface, send, slots, near_gas, *refs
):
    x_sends, (tail, sems) = refs[:turns_x], refs[turns_x:]
    parcels = owner.shape[1]
    nodes, species = droplet.shape[0], droplet.shape[1]
    load_tail = pltpu.make_async_copy(droplet.at[pl.ds(nodes - DROP_STEPS, DROP_STEPS)], tail, sems.at[0])
    lines = gas.shape[1]
    loads = [pltpu.make_async_copy(gas.at[:, line, :], near_gas.at[line], sems.at[1 + line]) for line in range(lines)]
    load_tail.start()
    for load in loads:
        load.start()
    wts = weights[...]
    norm = wts / jnp.sum(wts, axis=0, keepdims=True)
    mine = owner[...]
    column = jnp.transpose(jnp.broadcast_to(mine.astype(F32), (parcels, parcels)))
    earlier = (column == mine.astype(F32)) & (iota((parcels, parcels), 0) < iota((parcels, parcels), 1))
    rank = jnp.sum(jnp.where(earlier, 1.0, 0.0), axis=0, keepdims=True).astype(jnp.int32)
    slot = mine * cap + rank
    slots[...] = slot
    place = one_hot(iota((send.shape[0], parcels), 0) == slot)
    rest = jnp.zeros((LANES - species - 2 * STENCIL - 8, parcels), F32)
    liquid_col, surface_col = as_column(liquid[...]), as_column(surface[...])
    load_tail.wait()
    emitted = surface_steps([tail[i] for i in range(DROP_STEPS)], 0.0, liquid_col, surface_col)
    values = jnp.concatenate(
        [
            mass[...] * emitted,
            cells[...].astype(F32),
            norm,
            jnp.broadcast_to(mass[...], (8, parcels)),
            rest,
        ],
        axis=0,
    )
    for load in loads:
        load.wait()
    even_x, _, _ = place_on("gx")
    for turn, x_send in enumerate(x_sends):
        start = jnp.where(even_x == (turn == 0), size_x - 2, 0) * size_y
        for i in range(2 * size_y):
            x_send[i] = near_gas[start + i]
    parts = jnp.concatenate(split_all(values), axis=0)
    placed = lax.dot_general(place, parts, NT, preferred_element_type=F32)
    send[...] = placed[:, :LANES] + placed[:, LANES : 2 * LANES] + placed[:, 2 * LANES :]


def y_faces_kernel(size_x, size_y, near_gas, ya, yb):
    even_y, _, _ = place_on("gy")
    for turn, y_send in enumerate((ya, yb)):
        up = even_y == (turn == 0)
        near = jnp.where(up, size_y - 1, 0)
        far = jnp.where(up, size_y - 2, 1)
        for x in range(size_x):
            y_send[x] = near_gas[x * size_y + near]
            y_send[size_x + x] = near_gas[x * size_y + far]


def corner_kernel(size_x, ya, yb, *sends):
    even_x, _, _ = place_on("gx")
    even_y, _, _ = place_on("gy")
    for turn, send in enumerate(sends):
        x = jnp.where(even_x == (turn == 0), size_x - 1, 0)
        send[0], send[1] = low_high(even_y, ya[x], yb[x])


def couple_kernel(cap, packed, rows, gas, liquid, surface, back, deposit_out, deposit, w_high, w_low, sems):
    slots = rows.shape[0]
    species = liquid.shape[1]
    lines = gas.shape[0]
    table = jnp.transpose(rows[...])
    first = species
    cell = table[first : first + STENCIL]
    wts = table[first + STENCIL : first + 2 * STENCIL]
    mass = table[first + 2 * STENCIL : first + 2 * STENCIL + 1]
    whole = wts
    for shift in range(1, STENCIL):
        same = cell == pltpu.roll(cell, shift, 0)
        whole = whole + jnp.where(same, pltpu.roll(wts, shift, 0), 0.0)
    tile = 16
    cell = cell.astype(jnp.int32)
    high_rows, low_rows = split(whole)
    named = [jnp.broadcast_to(cell[k : k + 1], (tile, slots)).astype(jnp.int16) for k in range(STENCIL)]
    highs = [jnp.broadcast_to(high_rows[k : k + 1], (tile, slots)) for k in range(STENCIL)]
    lows = [jnp.broadcast_to(low_rows[k : k + 1], (tile, slots)) for k in range(STENCIL)]

    def pair(ref, line):
        return ref[line : line + 2].reshape(2 * LANES, slots)

    gathered = jnp.zeros((species, slots), F32)
    for line in range(0, lines, 2):
        for part in range(2):
            for z in range(0, LANES, tile):
                along = (iota((tile, slots), 0) + ((line + part) * LANES + z)).astype(jnp.int16)
                high = jnp.zeros((tile, slots), BF16)
                low = jnp.zeros((tile, slots), BF16)
                for k in range(STENCIL):
                    hit = named[k] == along
                    high = jnp.where(hit, highs[k], high)
                    low = jnp.where(hit, lows[k], low)
                w_high[line + part, z : z + tile] = high
                w_low[line + part, z : z + tile] = low
        t_high, t_low = split(jnp.concatenate([gas[line], gas[line + 1]], axis=1))
        t_all = jnp.concatenate([t_high, t_low], axis=0)
        both = jnp.dot(t_all, pair(w_high, line), preferred_element_type=F32)
        extra = jnp.dot(t_high, pair(w_low, line), preferred_element_type=F32)
        gathered = gathered + both[:species] + both[species:] + extra
    gas_rows = jnp.transpose(gathered)
    if packed:
        gas_rows = gas_rows.reshape(slots // cap, cap, species)
        gas_rows = jnp.concatenate([gas_rows[:, : cap // 2], gas_rows[:, cap // 2 :]], axis=2)
        back[...] = gas_rows.reshape(slots // 2, 2 * species)
    else:
        back[...] = jnp.concatenate([gas_rows, jnp.zeros((slots, LANES - species), F32)], axis=1)
    response = surface_response(as_column(liquid[...]), as_column(surface[...]))
    s_high, s_low = split(table[:species] + mass * (response * gathered))
    s_all = jnp.concatenate([s_high, s_low], axis=0)
    s_only = jnp.concatenate([s_high, jnp.zeros_like(s_low)], axis=0)
    saves = []
    each = lines // GROUPS
    for line in range(0, lines, 2):
        both = lax.dot_general(pair(w_high, line), s_all, NT, preferred_element_type=F32)
        both = both + lax.dot_general(pair(w_low, line), s_only, NT, preferred_element_type=F32)
        for i in range(2):
            turned = jnp.transpose(both[i * LANES : (i + 1) * LANES])
            deposit[line + i] = turned[:species] + turned[species:]
        if line % each == each - 2:
            at = pl.ds(line + 2 - each, each)
            saves.append(pltpu.make_async_copy(deposit.at[at], deposit_out.at[at], sems.at[line // each]))
            saves[-1].start()
    for save in saves:
        save.wait()


def droplet_kernel(
    cap, packed, droplet, rows, slots, liquid, surface, _, state_out, state_in, state_next, gas_at, load_sems, sems
):
    nodes, species, parcels = state_in.shape
    block = 8

    def load(i):
        at = pl.ds(i * block, block)
        return pltpu.make_async_copy(droplet.at[:, at], state_in.at[:, at], load_sems.at[i])

    for i in range(species // block):
        load(i).start()
    table = jnp.transpose(rows[...])
    count = rows.shape[0]
    at = iota((count, parcels), 0)
    slot = slots[...]
    if packed:
        half = cap // 2
        at = at // half * cap + at % half
        pairs = [(table[:species], at), (table[species:], at + half)]
    else:
        pairs = [(table[:species], at)]
    total = jnp.zeros((species, parcels), F32)
    for values, index in pairs:
        parts = jnp.concatenate(split_all(values), axis=0)
        placed = jnp.dot(parts, one_hot(index == slot), preferred_element_type=F32)
        total = total + placed[:species] + placed[species : 2 * species] + placed[2 * species :]
    gas_at[...] = total

    def save(i):
        at = pl.ds(i * block, block)
        return pltpu.make_async_copy(state_next.at[:, at], state_out.at[:, at], sems.at[i])

    @pl.loop(0, species // block)
    def _(i):
        at = pl.ds(pl.multiple_of(i * block, block), block)
        pick = i * block + iota((block, species), 0) == iota((block, species), 1)
        liquid_col = jnp.sum(jnp.where(pick, liquid[...], 0.0), axis=1, keepdims=True)
        surface_col = jnp.sum(jnp.where(pick, surface[...], 0.0), axis=1, keepdims=True)
        rate = jnp.broadcast_to(liquid_col, (block, parcels))
        keep = 1.0 - 2.0 * rate
        last_keep = jnp.broadcast_to(1.0 - liquid_col - surface_col, (block, parcels))
        from_gas = surface_col * gas_at[at, :]
        load(i).wait()
        state = [state_in[node, at] for node in range(nodes)]
        for step in range(DROP_STEPS):
            state = (
                [keep * state[0] + (rate + rate) * state[1]]
                + [keep * state[n] + rate * (state[n - 1] + state[n + 1]) for n in range(1, nodes - 1)]
                + [last_keep * state[-1] + rate * state[-2] + from_gas]
            )
        for node in range(nodes):
            state_next[node, at] = state[node]
        save(i).start()

    for i in range(species // block):
        save(i).wait()


def place_on(axis):
    index, count = lax.axis_index(axis), lax.axis_size(axis)
    even = lax.rem(index, 2) == 0
    below = jnp.where(index > 0, 1.0, 0.0).astype(F32)
    above = jnp.where(index < count - 1, 1.0, 0.0).astype(F32)
    return even, below, above


def swaps(axis, wrap=False):
    count = lax.axis_size(axis)
    rounds = []
    for first in range(2):
        pairs = [(i, i + 1) for i in range(first, count - 1, 2)]
        if wrap and first == 1 and count > 2 and count % 2 == 0:
            pairs.append((count - 1, 0))
        if pairs:
            rounds.append(pairs + [(j, i) for i, j in pairs])
    return rounds


def swap_all(messages, axis, wrap=False):
    return [lax.ppermute(m, axis, pairs) for m, pairs in zip(messages, swaps(axis, wrap), strict=True)]


def low_high(even, first, second):
    if second is None:
        second = jnp.zeros_like(first)
    return jnp.where(even, second, first), jnp.where(even, first, second)


def beside_z(block):
    axis = block.ndim - 1
    lane = iota(block.shape, axis)
    before = jnp.where(lane == 0, 0.0, pltpu.roll(block, 1, axis))
    after = jnp.where(lane == LANES - 1, 0.0, pltpu.roll(block, LANES - 1, axis))
    return before + after


def beside_xy(planes, x, y, x_low, x_high, y_low, y_high):
    size_x, size_y = len(planes), len(planes[0])
    total = planes[x - 1][y]() if x > 0 else x_low(y)
    total = total + (planes[x + 1][y]() if x < size_x - 1 else x_high(y))
    total = total + (planes[x][y - 1]() if y > 0 else y_low(x))
    return total + (planes[x][y + 1]() if y < size_y - 1 else y_high(x))


def plane_at(ref, index):
    return lambda: ref[index]


def wide_rates(rate, rows):
    column = as_column(rate[...])
    column = jnp.concatenate([column] * (rows // column.shape[0]), axis=0)
    return jnp.broadcast_to(column, (rows, LANES))


def columns_of(block):
    turned = jnp.transpose(block)
    return turned[:1], turned[-1:]


def first_step_kernel(size_x, size_y, turns_x, gas, *refs):
    xs, refs = refs[:turns_x], refs[turns_x:]
    (ya, yb, rate, field), refs = refs[:4], refs[4:]
    xs_out, (ya_out, yb_out, za, zb) = refs[:turns_x], refs[turns_x:]
    species = rate.shape[1]
    lines = size_x * size_y
    even_x, below_x, above_x = place_on("gx")
    even_y, below_y, above_y = place_on("gy")
    even_z, _, _ = place_on("gz")
    wide = wide_rates(rate, species)
    keep = 1.0 - 6.0 * wide
    planes = [[plane_at(gas, x * size_y + y) for y in range(size_y)] for x in range(size_x)]

    def from_x(side, y):
        near = [ref[(1 - side) * size_y + y] for ref in xs]
        return low_high(even_x, near[0], near[1] if turns_x == 2 else None)[side]

    def from_y(side, x):
        return low_high(even_y, ya[x], yb[x])[side]

    for x in range(size_x):
        for y in range(size_y):
            own = gas[x * size_y + y]
            total = beside_xy(
                planes,
                x,
                y,
                functools.partial(from_x, 0),
                functools.partial(from_x, 1),
                functools.partial(from_y, 0),
                functools.partial(from_y, 1),
            )
            field[x * size_y + y] = keep * own + wide * (total + beside_z(own))

    for turn, ref in enumerate(xs):
        up = even_x == (turn == 0)
        exists = jnp.where(up, above_x, below_x)
        near, far = jnp.where(up, 0, size_y), jnp.where(up, size_y, 0)
        inner = jnp.where(up, lines - size_y, 0)
        for y in range(size_y):
            own = ref[near + y]
            total = ref[far + y] + exists * gas[inner + y]
            if y > 0:
                total = total + ref[near + y - 1]
            if y < size_y - 1:
                total = total + ref[near + y + 1]
            xs_out[turn][far + y] = keep * own + wide * (total + beside_z(own))

    for turn, (ref, ref_out) in enumerate(((ya, ya_out), (yb, yb_out))):
        up = even_y == (turn == 0)
        exists = jnp.where(up, above_y, below_y)
        inner = jnp.where(up, size_y - 1, 0)
        for x in range(size_x):
            own = ref[x]
            total = ref[size_x + x] + exists * gas[x * size_y + inner]
            if x > 0:
                total = total + ref[x - 1]
            if x < size_x - 1:
                total = total + ref[x + 1]
            ref_out[size_x + x] = keep * own + wide * (total + beside_z(own))

    rows = []
    each = LANES // species
    for ref in (gas, field):
        rows += [columns_of(ref[i : i + each].reshape(LANES, LANES)) for i in range(0, lines, each)]
    for turn, ref in enumerate(xs):
        near = jnp.where(even_x == (turn == 0), 0, size_y)
        rows += [columns_of(ref[pl.ds(near + i, each)].reshape(LANES, LANES)) for i in range(0, size_y, each)]
    for ref in (ya, yb):
        rows += [columns_of(ref[i : i + each].reshape(LANES, LANES)) for i in range(0, size_x, each)]
    rest = [jnp.zeros((za.shape[0] - len(rows), LANES), F32)]
    low = jnp.concatenate([row[0] for row in rows] + rest, axis=0)
    high = jnp.concatenate([row[1] for row in rows] + rest, axis=0)
    za[...] = jnp.where(even_z, high, low)
    zb[...] = jnp.where(even_z, low, high)


def second_step_kernel(
    size_x, size_y, turns_x, field, *refs
):
    xs, refs = refs[:turns_x], refs[turns_x:]
    corners, refs = refs[:turns_x], refs[turns_x:]
    ya, yb, za, zb, za_in, zb_in, rate, deposit_in, out, now, now_x, now_y, result, deposit, sems = refs
    species = rate.shape[1]
    lines = size_x * size_y
    load = pltpu.make_async_copy(deposit_in, deposit, sems.at[lines])
    load.start()
    even_x, _, _ = place_on("gx")
    even_y, _, _ = place_on("gy")
    even, below, above = place_on("gz")
    each = LANES // species
    count = lines // each
    rates = jnp.concatenate([rate[...]] * each, axis=1)
    low, high = low_high(even, za_in[...], zb_in[...])
    low, high = jnp.where(below > 0.0, low, 0.0), jnp.where(above > 0.0, high, 0.0)
    own_low, own_high = low_high(even, za[...], zb[...])
    next_low = rates * (low[count : 2 * count] + below * rates * own_low[:count])
    next_high = rates * (high[count : 2 * count] + above * rates * own_high[:count])
    low, high = rates * low, rates * high

    def spread(low_row, high_row):
        turned = iota((LANES, LANES), 0)
        rows = jnp.where(turned == 0, low_row, jnp.where(turned == LANES - 1, high_row, 0.0))
        return jnp.transpose(rows)

    def row(i):
        return spread(low[i : i + 1], high[i : i + 1])

    def add_halo(target, source, start, count, first):
        for i in range(count):
            block = source[pl.ds(start + i * each, each)].reshape(LANES, LANES) + row(first + i)
            target[i * each : (i + 1) * each] = block.reshape(each, species, LANES)

    wide = wide_rates(rate, species)
    add_halo(now, field, 0, count, 0)
    first = 2 * count
    for turn, (ref, corner) in enumerate(zip(xs, corners, strict=True)):
        start = jnp.where(even_x == (turn == 0), size_y, 0)
        add_halo(now_x.at[turn], ref, start, size_y // each, first)
        first = first + size_y // each
        now_x[turn, 0] = now_x[turn, 0] + wide * corner[0]
        now_x[turn, size_y - 1] = now_x[turn, size_y - 1] + wide * corner[1]
    for turn, ref in enumerate((ya, yb)):
        add_halo(now_y.at[turn], ref, size_x, size_x // each, first)
        first = first + size_x // each
        edges = [jnp.where(even_y == (turn == 0), corner[1], corner[0]) for corner in corners]
        edges = low_high(even_x, edges[0], edges[1] if turns_x == 2 else None)
        now_y[turn, 0] = now_y[turn, 0] + wide * edges[0]
        now_y[turn, size_x - 1] = now_y[turn, size_x - 1] + wide * edges[1]

    keep = 1.0 - 6.0 * wide
    planes = [[plane_at(now, x * size_y + y) for y in range(size_y)] for x in range(size_x)]

    def from_x(side, y):
        return low_high(even_x, now_x[0, y], now_x[1, y] if turns_x == 2 else None)[side]

    def from_y(side, x):
        return low_high(even_y, now_y[0, x], now_y[1, x])[side]

    load.wait()
    saves = []
    for x in range(size_x):
        for y in range(size_y):
            line = x * size_y + y
            own = now[line]
            total = beside_xy(
                planes,
                x,
                y,
                functools.partial(from_x, 0),
                functools.partial(from_x, 1),
                functools.partial(from_y, 0),
                functools.partial(from_y, 1),
            )
            if line % each == 0:
                i = line // each
                ends = spread(next_low[i : i + 1], next_high[i : i + 1])
            part = ends[line % each * species : (line % each + 1) * species]
            result[line] = keep * own + wide * (total + beside_z(own)) + part + deposit[line]
            saves.append(pltpu.make_async_copy(result.at[line], out.at[:, line, :], sems.at[line]))
            saves[-1].start()
    for save in saves:
        save.wait()


def full(shape):
    return pl.BlockSpec(shape, lambda *_: (0,) * len(shape))


def lasts(microseconds):
    return pl.CostEstimate(flops=0, bytes_accessed=int(3.69e6 * microseconds), transcendentals=0)


def in_hbm(array):
    return pltpu.with_memory_space_constraint(array, pltpu.HBM)


def in_vmem(array):
    return pltpu.with_memory_space_constraint(array, pltpu.VMEM)


def exchange(rows, group):
    width = rows.shape[1]
    chunks = rows.reshape(group, -1, width)
    chunks = lax.all_to_all(chunks, ("gy", "gz"), split_axis=0, concat_axis=0, tiled=True)
    return chunks.reshape(-1, width)


def on_device(gas, droplet, owner, cells, weights, mass, liquid_rate, surface_rate, gas_rate):
    group = lax.axis_size("gy") * lax.axis_size("gz")
    nodes, species, parcels = droplet.shape
    cap = 2 * parcels // group
    slots = group * cap
    packed = cap % 16 == 0
    lines = gas.shape[1] * gas.shape[2]
    flat = gas.reshape(species, lines, LANES)
    planes = (lines, species, LANES)
    liquid = liquid_rate.reshape(1, species)
    surface = surface_rate.reshape(1, species)
    rate_spec = full((1, species))
    size_x, size_y = gas.shape[1], gas.shape[2]
    rate = gas_rate.reshape(1, species)
    vmem = pl.BlockSpec(memory_space=pltpu.VMEM)
    hbm = pl.BlockSpec(memory_space=pl.ANY)
    whole = pl.BlockSpec()
    turns_x = len(swaps("gx"))
    x_shape = (2 * size_y, species, LANES)
    y_shape = (2 * size_x, species, LANES)

    send, slot, near_gas, *x_faces = pl.pallas_call(
        functools.partial(pack_kernel, cap, size_x, size_y, turns_x),
        grid=(1,),
        out_shape=[
            pltpu.VMEM((slots, LANES), F32),
            jax.ShapeDtypeStruct((1, parcels), jnp.int32),
            pltpu.VMEM(planes, F32),
        ]
        + [pltpu.VMEM(x_shape, F32)] * turns_x,
        in_specs=[hbm, hbm, full((1, parcels)), full((STENCIL, parcels)), full((STENCIL, parcels)), full((1, parcels))]
        + [rate_spec] * 2,
        out_specs=[vmem, full((1, parcels)), vmem] + [vmem] * turns_x,
        scratch_shapes=[
            pltpu.VMEM((DROP_STEPS, species, parcels), F32),
            pltpu.SemaphoreType.DMA((1 + lines,)),
        ],
        compiler_params=pltpu.CompilerParams(vmem_limit_bytes=8 * MIB),
        cost_estimate=lasts(2.5),
        name="pack",
    )(
        in_hbm(droplet),
        in_hbm(flat),
        in_hbm(owner.reshape(1, parcels)),
        in_hbm(cells),
        in_hbm(weights),
        in_hbm(mass.reshape(1, parcels)),
        in_hbm(liquid),
        in_hbm(surface),
    )
    rows = exchange(send, group)

    x_halo = swap_all(x_faces, "gx")
    y_faces = pl.pallas_call(
        functools.partial(y_faces_kernel, size_x, size_y),
        out_shape=[pltpu.VMEM(y_shape, F32)] * 2,
        in_specs=[vmem],
        out_specs=[vmem] * 2,
        compiler_params=pltpu.CompilerParams(vmem_limit_bytes=4 * MIB),
        cost_estimate=lasts(0.6),
        name="y_faces",
    )(near_gas)
    y_halo = swap_all(y_faces, "gy")

    corners = pl.pallas_call(
        functools.partial(corner_kernel, size_x),
        out_shape=[jax.ShapeDtypeStruct((2, species, LANES), F32)] * turns_x,
        in_specs=[vmem] * 2,
        out_specs=[vmem] * turns_x,
        compiler_params=pltpu.CompilerParams(vmem_limit_bytes=4 * MIB),
        cost_estimate=lasts(0.3),
        name="corner_planes",
    )(*y_halo)
    corners = swap_all(corners, "gx")

    back_rows = slots // 2 if packed else slots
    w_shape = (lines, LANES, slots)
    back, deposit = pl.pallas_call(
        functools.partial(couple_kernel, cap, packed),
        out_shape=[pltpu.VMEM((back_rows, LANES), F32), pltpu.HBM(planes, F32)],
        in_specs=[vmem] * 2 + [whole] * 2,
        out_specs=[vmem, hbm],
        scratch_shapes=[
            pltpu.VMEM(planes, F32),
            pltpu.VMEM(w_shape, BF16),
            pltpu.VMEM(w_shape, BF16),
            pltpu.SemaphoreType.DMA((GROUPS,)),
        ],
        compiler_params=pltpu.CompilerParams(vmem_limit_bytes=10 * MIB),
        cost_estimate=lasts(7.0),
        name="couple_gas",
    )(rows, near_gas, liquid, surface)

    returned = exchange(back, group)

    z_shape = (48, LANES)
    halos = [in_vmem(halo) for halo in x_halo + y_halo]
    field, *stepped = pl.pallas_call(
        functools.partial(first_step_kernel, size_x, size_y, turns_x),
        out_shape=[pltpu.VMEM(planes, F32)]
        + [pltpu.VMEM(x_shape, F32)] * turns_x
        + [pltpu.VMEM(y_shape, F32)] * 2
        + [jax.ShapeDtypeStruct(z_shape, F32)] * 2,
        in_specs=[vmem] * (turns_x + 3) + [whole],
        out_specs=[vmem] * (turns_x + 3) + [whole] * 2,
        input_output_aliases={1 + i: 1 + i for i in range(turns_x + 2)},
        compiler_params=pltpu.CompilerParams(vmem_limit_bytes=8 * MIB),
        cost_estimate=lasts(1.6),
        name="first_gas_step",
    )(near_gas, *halos, rate)
    halos, z_sends = stepped[:-2], stepped[-2:]
    z_halo = swap_all(z_sends, "gz", wrap=True)
    gas_next = pl.pallas_call(
        functools.partial(second_step_kernel, size_x, size_y, turns_x),
        out_shape=jax.ShapeDtypeStruct(flat.shape, F32),
        in_specs=[vmem] * (2 * turns_x + 3) + [whole] * 5 + [hbm],
        out_specs=hbm,
        scratch_shapes=[
            pltpu.VMEM(planes, F32),
            pltpu.VMEM((turns_x, size_y, species, LANES), F32),
            pltpu.VMEM((2, size_x, species, LANES), F32),
            pltpu.VMEM(planes, F32),
            pltpu.VMEM(planes, F32),
            pltpu.SemaphoreType.DMA((lines + 1,)),
        ],
        compiler_params=pltpu.CompilerParams(vmem_limit_bytes=10 * MIB),
        cost_estimate=lasts(4.0),
        name="second_gas_step",
    )(field, *halos[:turns_x], *corners, *halos[turns_x:], *z_sends, *z_halo, rate, in_hbm(deposit))
    droplet_next = pl.pallas_call(
        functools.partial(droplet_kernel, cap, packed),
        out_shape=jax.ShapeDtypeStruct(droplet.shape, F32),
        in_specs=[hbm] + [whole] * 4 + [hbm],
        out_specs=hbm,
        scratch_shapes=[
            pltpu.VMEM(droplet.shape, F32),
            pltpu.VMEM(droplet.shape, F32),
            pltpu.VMEM((species, parcels), F32),
            pltpu.SemaphoreType.DMA((species // 8,)),
            pltpu.SemaphoreType.DMA((species // 8,)),
        ],
        compiler_params=pltpu.CompilerParams(vmem_limit_bytes=8 * MIB),
        cost_estimate=lasts(2.5),
        name="droplets",
    )(in_hbm(droplet), returned, slot, liquid, surface, in_hbm(gas_next))
    return (gas_next.reshape(gas.shape), droplet_next)


def solution(mesh):
    return jax.shard_map(
        on_device,
        mesh=mesh,
        in_specs=(
            P(None, "gx", "gy", "gz"),
            P(None, None, ("gx", "gy", "gz")),
            P(("gx", "gy", "gz"), None),
            P(None, ("gx", "gy", "gz")),
            P(None, ("gx", "gy", "gz")),
            P(("gx", "gy", "gz")),
            P(),
            P(),
            P(),
        ),
        out_specs=(P(None, "gx", "gy", "gz"), P(None, None, ("gx", "gy", "gz"))),
        check_vma=False,
    )
```

```python
import functools

import jax
import jax.numpy as jnp
from jax import lax
from jax.experimental import pallas as pl
from jax.experimental.pallas import tpu as pltpu
from jax.sharding import PartitionSpec as P

STENCIL = 8
DROP_STEPS = 4
GAS_STEPS = 2
LANES = 128
GROUPS = 4
MIB = 1 << 20
NT = (((1,), (1,)), ((), ()))
HIGH = lax.Precision.HIGHEST
F32 = jnp.float32
BF16 = jnp.bfloat16


def iota(shape, dim):
    return lax.broadcasted_iota(jnp.int32, shape, dim)


def as_column(row):
    n = row.shape[1]
    return jnp.sum(jnp.where(iota((n, n), 0) == iota((n, n), 1), row, 0.0), axis=1, keepdims=True)


def leading(value):
    scaled = value * 65537.0
    return scaled - (scaled - value)


def split(value):
    high = leading(value)
    return high.astype(BF16), (value - high).astype(BF16)


def split_all(value):
    high = leading(value)
    rest = value - high
    middle = leading(rest)
    return high.astype(BF16), middle.astype(BF16), (rest - middle).astype(BF16)


def one_hot(hit):
    return jnp.where(hit, 1.0, 0.0).astype(BF16)


def surface_steps(nodes, gas_at, liquid, surface):
    emitted = None
    for step in range(DROP_STEPS):
        last = nodes[-1]
        flux = surface * (last - gas_at)
        emitted = flux if emitted is None else emitted + flux
        inner = [
            nodes[i] + liquid * (nodes[i + 1] - 2.0 * nodes[i] + nodes[i - 1])
            for i in range(1, len(nodes) - 1)
        ]
        if len(nodes) > 1:
            nodes = inner + [last + liquid * (nodes[-2] - last) - flux]
    return emitted


def surface_response(liquid, surface):
    return surface_steps([jnp.zeros_like(liquid)] * DROP_STEPS, 1.0, liquid, surface)


def pack_kernel(cap, size_x, size_y, turns_x, droplet, gas, *refs):
    sources, (send, slots, near_gas), refs = refs[:6], refs[6:9], refs[9:]
    x_sends, refs = refs[:turns_x], refs[turns_x:]
    (owner, cells, weights, mass, liquid, surface), (tail, sems) = refs[:6], refs[6:]
    parcels = owner.shape[1]
    nodes, species = droplet.shape[0], droplet.shape[1]
    lines = gas.shape[1]
    pairs = list(zip(sources, refs[:6], strict=True))
    pairs.append((droplet.at[pl.ds(nodes - DROP_STEPS, DROP_STEPS)], tail))
    small = len(pairs)
    pairs += [(gas.at[:, line, :], near_gas.at[line]) for line in range(lines)]
    loads = [pltpu.make_async_copy(source, here, sems.at[i]) for i, (source, here) in enumerate(pairs)]
    for load in loads:
        load.start()
    for load in loads[: small - 1]:
        load.wait()
    wts = weights[...]
    norm = wts / jnp.sum(wts, axis=0, keepdims=True)
    mine = owner[...]
    column = jnp.transpose(jnp.broadcast_to(mine.astype(F32), (parcels, parcels)))
    earlier = (column == mine.astype(F32)) & (iota((parcels, parcels), 0) < iota((parcels, parcels), 1))
    rank = jnp.sum(jnp.where(earlier, 1.0, 0.0), axis=0, keepdims=True).astype(jnp.int32)
    slot = mine * cap + rank
    slots[...] = slot
    place = one_hot(iota((send.shape[0], parcels), 0) == slot)
    rest = jnp.zeros((LANES - species - 2 * STENCIL - 8, parcels), F32)
    liquid_col, surface_col = as_column(liquid[...]), as_column(surface[...])
    loads[small - 1].wait()
    emitted = surface_steps([tail[i] for i in range(DROP_STEPS)], 0.0, liquid_col, surface_col)
    values = jnp.concatenate(
        [
            mass[...] * emitted,
            cells[...].astype(F32),
            norm,
            jnp.broadcast_to(mass[...], (8, parcels)),
            rest,
        ],
        axis=0,
    )
    for load in loads[small:]:
        load.wait()
    even_x, _, _ = place_on("gx")
    for turn, x_send in enumerate(x_sends):
        start = jnp.where(even_x == (turn == 0), size_x - 2, 0) * size_y
        for i in range(2 * size_y):
            x_send[i] = near_gas[start + i]
    parts = jnp.concatenate(split_all(values), axis=0)
    placed = lax.dot_general(place, parts, NT, preferred_element_type=F32)
    send[...] = placed[:, :LANES] + placed[:, LANES : 2 * LANES] + placed[:, 2 * LANES :]


def y_faces_kernel(size_x, size_y, near_gas, ya, yb):
    even_y, _, _ = place_on("gy")
    for turn, y_send in enumerate((ya, yb)):
        up = even_y == (turn == 0)
        near = jnp.where(up, size_y - 1, 0)
        far = jnp.where(up, size_y - 2, 1)
        for x in range(size_x):
            y_send[x] = near_gas[x * size_y + near]
            y_send[size_x + x] = near_gas[x * size_y + far]


def corner_kernel(size_x, ya, yb, *sends):
    even_x, _, _ = place_on("gx")
    even_y, _, _ = place_on("gy")
    for turn, send in enumerate(sends):
        x = jnp.where(even_x == (turn == 0), size_x - 1, 0)
        send[0], send[1] = low_high(even_y, ya[x], yb[x])


def couple_kernel(cap, packed, rows, gas, liquid, surface, back, deposit_out, deposit, w_high, w_low, sems):
    slots = rows.shape[0]
    species = liquid.shape[1]
    lines = gas.shape[0]
    table = jnp.transpose(rows[...])
    first = species
    cell = table[first : first + STENCIL]
    wts = table[first + STENCIL : first + 2 * STENCIL]
    mass = table[first + 2 * STENCIL : first + 2 * STENCIL + 1]
    whole = wts
    for shift in range(1, STENCIL):
        same = cell == pltpu.roll(cell, shift, 0)
        whole = whole + jnp.where(same, pltpu.roll(wts, shift, 0), 0.0)
    tile = 16
    cell = cell.astype(jnp.int32)
    high_rows, low_rows = split(whole)
    named = [jnp.broadcast_to(cell[k : k + 1], (tile, slots)).astype(jnp.int16) for k in range(STENCIL)]
    highs = [jnp.broadcast_to(high_rows[k : k + 1], (tile, slots)) for k in range(STENCIL)]
    lows = [jnp.broadcast_to(low_rows[k : k + 1], (tile, slots)) for k in range(STENCIL)]

    def pair(ref, line):
        return ref[line : line + 2].reshape(2 * LANES, slots)

    gathered = jnp.zeros((species, slots), F32)
    for line in range(0, lines, 2):
        for part in range(2):
            for z in range(0, LANES, tile):
                along = (iota((tile, slots), 0) + ((line + part) * LANES + z)).astype(jnp.int16)
                high = jnp.zeros((tile, slots), BF16)
                low = jnp.zeros((tile, slots), BF16)
                for k in range(STENCIL):
                    hit = named[k] == along
                    high = jnp.where(hit, highs[k], high)
                    low = jnp.where(hit, lows[k], low)
                w_high[line + part, z : z + tile] = high
                w_low[line + part, z : z + tile] = low
        t_high, t_low = split(jnp.concatenate([gas[line], gas[line + 1]], axis=1))
        t_all = jnp.concatenate([t_high, t_low], axis=0)
        both = jnp.dot(t_all, pair(w_high, line), preferred_element_type=F32)
        extra = jnp.dot(t_high, pair(w_low, line), preferred_element_type=F32)
        gathered = gathered + both[:species] + both[species:] + extra
    gas_rows = jnp.transpose(gathered)
    if packed:
        gas_rows = gas_rows.reshape(slots // cap, cap, species)
        gas_rows = jnp.concatenate([gas_rows[:, : cap // 2], gas_rows[:, cap // 2 :]], axis=2)
        back[...] = gas_rows.reshape(slots // 2, 2 * species)
    else:
        back[...] = jnp.concatenate([gas_rows, jnp.zeros((slots, LANES - species), F32)], axis=1)
    response = surface_response(as_column(liquid[...]), as_column(surface[...]))
    s_high, s_low = split(table[:species] + mass * (response * gathered))
    s_all = jnp.concatenate([s_high, s_low], axis=0)
    s_only = jnp.concatenate([s_high, jnp.zeros_like(s_low)], axis=0)
    saves = []
    each = lines // GROUPS
    for line in range(0, lines, 2):
        both = lax.dot_general(pair(w_high, line), s_all, NT, preferred_element_type=F32)
        both = both + lax.dot_general(pair(w_low, line), s_only, NT, preferred_element_type=F32)
        for i in range(2):
            turned = jnp.transpose(both[i * LANES : (i + 1) * LANES])
            deposit[line + i] = turned[:species] + turned[species:]
        if line % each == each - 2:
            at = pl.ds(line + 2 - each, each)
            saves.append(pltpu.make_async_copy(deposit.at[at], deposit_out.at[at], sems.at[line // each]))
            saves[-1].start()
    for save in saves:
        save.wait()


def droplet_kernel(
    cap, packed, state_in, rows, slots, liquid, surface, _, state_out, state_next, gas_at, sems
):
    nodes, species, parcels = state_in.shape
    block = 8

    table = jnp.transpose(rows[...])
    count = rows.shape[0]
    at = iota((count, parcels), 0)
    slot = slots[...]
    if packed:
        half = cap // 2
        at = at // half * cap + at % half
        pairs = [(table[:species], at), (table[species:], at + half)]
    else:
        pairs = [(table[:species], at)]
    total = jnp.zeros((species, parcels), F32)
    for values, index in pairs:
        parts = jnp.concatenate(split_all(values), axis=0)
        placed = jnp.dot(parts, one_hot(index == slot), preferred_element_type=F32)
        total = total + placed[:species] + placed[species : 2 * species] + placed[2 * species :]
    gas_at[...] = total

    def save(i):
        at = pl.ds(i * block, block)
        return pltpu.make_async_copy(state_next.at[:, at], state_out.at[:, at], sems.at[i])

    @pl.loop(0, species // block, unroll=4)
    def _(i):
        at = pl.ds(pl.multiple_of(i * block, block), block)
        pick = i * block + iota((block, species), 0) == iota((block, species), 1)
        liquid_col = jnp.sum(jnp.where(pick, liquid[...], 0.0), axis=1, keepdims=True)
        surface_col = jnp.sum(jnp.where(pick, surface[...], 0.0), axis=1, keepdims=True)
        rate = jnp.broadcast_to(liquid_col, (block, parcels))
        keep = 1.0 - 2.0 * rate
        last_keep = jnp.broadcast_to(1.0 - liquid_col - surface_col, (block, parcels))
        from_gas = surface_col * gas_at[at, :]
        state = [state_in[node, at] for node in range(nodes)]
        for step in range(DROP_STEPS):
            state = (
                [keep * state[0] + (rate + rate) * state[1]]
                + [keep * state[n] + rate * (state[n - 1] + state[n + 1]) for n in range(1, nodes - 1)]
                + [last_keep * state[-1] + rate * state[-2] + from_gas]
            )
        for node in range(nodes):
            state_next[node, at] = state[node]
        save(i).start()

    for i in range(species // block):
        save(i).wait()


def place_on(axis):
    index, count = lax.axis_index(axis), lax.axis_size(axis)
    even = lax.rem(index, 2) == 0
    below = jnp.where(index > 0, 1.0, 0.0).astype(F32)
    above = jnp.where(index < count - 1, 1.0, 0.0).astype(F32)
    return even, below, above


def swaps(axis, wrap=False):
    count = lax.axis_size(axis)
    rounds = []
    for first in range(2):
        pairs = [(i, i + 1) for i in range(first, count - 1, 2)]
        if wrap and first == 1 and count > 2 and count % 2 == 0:
            pairs.append((count - 1, 0))
        if pairs:
            rounds.append(pairs + [(j, i) for i, j in pairs])
    return rounds


def swap_all(messages, axis, wrap=False):
    return [lax.ppermute(m, axis, pairs) for m, pairs in zip(messages, swaps(axis, wrap), strict=True)]


def low_high(even, first, second):
    if second is None:
        second = jnp.zeros_like(first)
    return jnp.where(even, second, first), jnp.where(even, first, second)


def beside_z(block):
    axis = block.ndim - 1
    lane = iota(block.shape, axis)
    before = jnp.where(lane == 0, 0.0, pltpu.roll(block, 1, axis))
    after = jnp.where(lane == LANES - 1, 0.0, pltpu.roll(block, LANES - 1, axis))
    return before + after


def beside_xy(planes, x, y, x_low, x_high, y_low, y_high):
    size_x, size_y = len(planes), len(planes[0])
    total = planes[x - 1][y]() if x > 0 else x_low(y)
    total = total + (planes[x + 1][y]() if x < size_x - 1 else x_high(y))
    total = total + (planes[x][y - 1]() if y > 0 else y_low(x))
    return total + (planes[x][y + 1]() if y < size_y - 1 else y_high(x))


def plane_at(ref, index):
    return lambda: ref[index]


def wide_rates(rate, rows):
    column = as_column(rate[...])
    column = jnp.concatenate([column] * (rows // column.shape[0]), axis=0)
    return jnp.broadcast_to(column, (rows, LANES))


def columns_of(block):
    turned = jnp.transpose(block)
    return turned[:1], turned[-1:]


def first_step_kernel(size_x, size_y, turns_x, gas, *refs):
    xs, refs = refs[:turns_x], refs[turns_x:]
    (ya, yb, rate, field), refs = refs[:4], refs[4:]
    xs_out, (ya_out, yb_out, za, zb) = refs[:turns_x], refs[turns_x:]
    species = rate.shape[1]
    lines = size_x * size_y
    even_x, below_x, above_x = place_on("gx")
    even_y, below_y, above_y = place_on("gy")
    even_z, _, _ = place_on("gz")
    wide = wide_rates(rate, species)
    keep = 1.0 - 6.0 * wide
    planes = [[plane_at(gas, x * size_y + y) for y in range(size_y)] for x in range(size_x)]

    def from_x(side, y):
        near = [ref[(1 - side) * size_y + y] for ref in xs]
        return low_high(even_x, near[0], near[1] if turns_x == 2 else None)[side]

    def from_y(side, x):
        return low_high(even_y, ya[x], yb[x])[side]

    for x in range(size_x):
        for y in range(size_y):
            own = gas[x * size_y + y]
            total = beside_xy(
                planes,
                x,
                y,
                functools.partial(from_x, 0),
                functools.partial(from_x, 1),
                functools.partial(from_y, 0),
                functools.partial(from_y, 1),
            )
            field[x * size_y + y] = keep * own + wide * (total + beside_z(own))

    for turn, ref in enumerate(xs):
        up = even_x == (turn == 0)
        exists = jnp.where(up, above_x, below_x)
        near, far = jnp.where(up, 0, size_y), jnp.where(up, size_y, 0)
        inner = jnp.where(up, lines - size_y, 0)
        for y in range(size_y):
            own = ref[near + y]
            total = ref[far + y] + exists * gas[inner + y]
            if y > 0:
                total = total + ref[near + y - 1]
            if y < size_y - 1:
                total = total + ref[near + y + 1]
            xs_out[turn][far + y] = keep * own + wide * (total + beside_z(own))

    for turn, (ref, ref_out) in enumerate(((ya, ya_out), (yb, yb_out))):
        up = even_y == (turn == 0)
        exists = jnp.where(up, above_y, below_y)
        inner = jnp.where(up, size_y - 1, 0)
        for x in range(size_x):
            own = ref[x]
            total = ref[size_x + x] + exists * gas[x * size_y + inner]
            if x > 0:
                total = total + ref[x - 1]
            if x < size_x - 1:
                total = total + ref[x + 1]
            ref_out[size_x + x] = keep * own + wide * (total + beside_z(own))

    rows = []
    each = LANES // species
    for ref in (gas, field):
        rows += [columns_of(ref[i : i + each].reshape(LANES, LANES)) for i in range(0, lines, each)]
    for turn, ref in enumerate(xs):
        near = jnp.where(even_x == (turn == 0), 0, size_y)
        rows += [columns_of(ref[pl.ds(near + i, each)].reshape(LANES, LANES)) for i in range(0, size_y, each)]
    for ref in (ya, yb):
        rows += [columns_of(ref[i : i + each].reshape(LANES, LANES)) for i in range(0, size_x, each)]
    rest = [jnp.zeros((za.shape[0] - len(rows), LANES), F32)]
    low = jnp.concatenate([row[0] for row in rows] + rest, axis=0)
    high = jnp.concatenate([row[1] for row in rows] + rest, axis=0)
    za[...] = jnp.where(even_z, high, low)
    zb[...] = jnp.where(even_z, low, high)


def second_step_kernel(
    size_x, size_y, turns_x, field, *refs
):
    xs, refs = refs[:turns_x], refs[turns_x:]
    corners, refs = refs[:turns_x], refs[turns_x:]
    ya, yb, za, zb, za_in, zb_in, rate, deposit, out, now, now_x, now_y, result, sems = refs
    species = rate.shape[1]
    lines = size_x * size_y
    even_x, _, _ = place_on("gx")
    even_y, _, _ = place_on("gy")
    even, below, above = place_on("gz")
    each = LANES // species
    count = lines // each
    rates = jnp.concatenate([rate[...]] * each, axis=1)
    low, high = low_high(even, za_in[...], zb_in[...])
    low, high = jnp.where(below > 0.0, low, 0.0), jnp.where(above > 0.0, high, 0.0)
    own_low, own_high = low_high(even, za[...], zb[...])
    next_low = rates * (low[count : 2 * count] + below * rates * own_low[:count])
    next_high = rates * (high[count : 2 * count] + above * rates * own_high[:count])
    low, high = rates * low, rates * high

    def spread(low_row, high_row):
        turned = iota((LANES, LANES), 0)
        rows = jnp.where(turned == 0, low_row, jnp.where(turned == LANES - 1, high_row, 0.0))
        return jnp.transpose(rows)

    def row(i):
        return spread(low[i : i + 1], high[i : i + 1])

    def add_halo(target, source, start, count, first):
        for i in range(count):
            block = source[pl.ds(start + i * each, each)].reshape(LANES, LANES) + row(first + i)
            target[i * each : (i + 1) * each] = block.reshape(each, species, LANES)

    wide = wide_rates(rate, species)
    add_halo(now, field, 0, count, 0)
    first = 2 * count
    for turn, (ref, corner) in enumerate(zip(xs, corners, strict=True)):
        start = jnp.where(even_x == (turn == 0), size_y, 0)
        add_halo(now_x.at[turn], ref, start, size_y // each, first)
        first = first + size_y // each
        now_x[turn, 0] = now_x[turn, 0] + wide * corner[0]
        now_x[turn, size_y - 1] = now_x[turn, size_y - 1] + wide * corner[1]
    for turn, ref in enumerate((ya, yb)):
        add_halo(now_y.at[turn], ref, size_x, size_x // each, first)
        first = first + size_x // each
        edges = [jnp.where(even_y == (turn == 0), corner[1], corner[0]) for corner in corners]
        edges = low_high(even_x, edges[0], edges[1] if turns_x == 2 else None)
        now_y[turn, 0] = now_y[turn, 0] + wide * edges[0]
        now_y[turn, size_x - 1] = now_y[turn, size_x - 1] + wide * edges[1]

    keep = 1.0 - 6.0 * wide
    planes = [[plane_at(now, x * size_y + y) for y in range(size_y)] for x in range(size_x)]

    def from_x(side, y):
        return low_high(even_x, now_x[0, y], now_x[1, y] if turns_x == 2 else None)[side]

    def from_y(side, x):
        return low_high(even_y, now_y[0, x], now_y[1, x])[side]

    saves = []
    for x in range(size_x):
        for y in range(size_y):
            line = x * size_y + y
            own = now[line]
            total = beside_xy(
                planes,
                x,
                y,
                functools.partial(from_x, 0),
                functools.partial(from_x, 1),
                functools.partial(from_y, 0),
                functools.partial(from_y, 1),
            )
            if line % each == 0:
                i = line // each
                ends = spread(next_low[i : i + 1], next_high[i : i + 1])
            part = ends[line % each * species : (line % each + 1) * species]
            result[line] = keep * own + wide * (total + beside_z(own)) + part + deposit[line]
            saves.append(pltpu.make_async_copy(result.at[line], out.at[:, line, :], sems.at[line]))
            saves[-1].start()
    for save in saves:
        save.wait()


def full(shape):
    return pl.BlockSpec(shape, lambda *_: (0,) * len(shape))


def lasts(microseconds):
    return pl.CostEstimate(flops=0, bytes_accessed=int(3.69e6 * microseconds), transcendentals=0)


def in_hbm(array):
    return pltpu.with_memory_space_constraint(array, pltpu.HBM)


def in_vmem(array):
    return pltpu.with_memory_space_constraint(array, pltpu.VMEM)


def exchange(rows, group):
    width = rows.shape[1]
    chunks = rows.reshape(group, -1, width)
    chunks = lax.all_to_all(chunks, ("gy", "gz"), split_axis=0, concat_axis=0, tiled=True)
    return chunks.reshape(-1, width)


def on_device(gas, droplet, owner, cells, weights, mass, liquid_rate, surface_rate, gas_rate):
    group = lax.axis_size("gy") * lax.axis_size("gz")
    nodes, species, parcels = droplet.shape
    cap = 2 * parcels // group
    slots = group * cap
    packed = cap % 16 == 0
    lines = gas.shape[1] * gas.shape[2]
    flat = gas.reshape(species, lines, LANES)
    planes = (lines, species, LANES)
    liquid = liquid_rate.reshape(1, species)
    surface = surface_rate.reshape(1, species)
    rate_spec = full((1, species))
    size_x, size_y = gas.shape[1], gas.shape[2]
    rate = gas_rate.reshape(1, species)
    vmem = pl.BlockSpec(memory_space=pltpu.VMEM)
    hbm = pl.BlockSpec(memory_space=pl.ANY)
    whole = pl.BlockSpec()
    turns_x = len(swaps("gx"))
    x_shape = (2 * size_y, species, LANES)
    y_shape = (2 * size_x, species, LANES)

    send, slot, near_gas, *x_faces = pl.pallas_call(
        functools.partial(pack_kernel, cap, size_x, size_y, turns_x),
        out_shape=[
            pltpu.VMEM((slots, LANES), F32),
            pltpu.VMEM((1, parcels), jnp.int32),
            pltpu.VMEM(planes, F32),
        ]
        + [pltpu.VMEM(x_shape, F32)] * turns_x,
        in_specs=[hbm] * 8,
        out_specs=[vmem] * (3 + turns_x),
        scratch_shapes=[
            pltpu.VMEM((1, parcels), jnp.int32),
            pltpu.VMEM((STENCIL, parcels), jnp.int32),
            pltpu.VMEM((STENCIL, parcels), F32),
            pltpu.VMEM((1, parcels), F32),
            pltpu.VMEM((1, species), F32),
            pltpu.VMEM((1, species), F32),
            pltpu.VMEM((DROP_STEPS, species, parcels), F32),
            pltpu.SemaphoreType.DMA((7 + lines,)),
        ],
        compiler_params=pltpu.CompilerParams(vmem_limit_bytes=8 * MIB),
        cost_estimate=lasts(2.5),
        name="pack",
    )(
        in_hbm(droplet),
        in_hbm(flat),
        in_hbm(owner.reshape(1, parcels)),
        in_hbm(cells),
        in_hbm(weights),
        in_hbm(mass.reshape(1, parcels)),
        in_hbm(liquid),
        in_hbm(surface),
    )
    rows = exchange(send, group)

    y_faces = pl.pallas_call(
        functools.partial(y_faces_kernel, size_x, size_y),
        out_shape=[pltpu.VMEM(y_shape, F32)] * 2,
        in_specs=[vmem],
        out_specs=[vmem] * 2,
        compiler_params=pltpu.CompilerParams(vmem_limit_bytes=4 * MIB),
        cost_estimate=lasts(0.6),
        name="y_faces",
    )(near_gas)
    y_halo = swap_all(y_faces, "gy")
    x_halo = swap_all(x_faces, "gx")

    corners = pl.pallas_call(
        functools.partial(corner_kernel, size_x),
        out_shape=[jax.ShapeDtypeStruct((2, species, LANES), F32)] * turns_x,
        in_specs=[vmem] * 2,
        out_specs=[vmem] * turns_x,
        compiler_params=pltpu.CompilerParams(vmem_limit_bytes=4 * MIB),
        cost_estimate=lasts(0.3),
        name="corner_planes",
    )(*y_halo)
    corners = swap_all(corners, "gx")

    back_rows = slots // 2 if packed else slots
    w_shape = (lines, LANES, slots)
    back, deposit = pl.pallas_call(
        functools.partial(couple_kernel, cap, packed),
        out_shape=[pltpu.VMEM((back_rows, LANES), F32), pltpu.HBM(planes, F32)],
        in_specs=[vmem] * 2 + [whole] * 2,
        out_specs=[vmem, hbm],
        scratch_shapes=[
            pltpu.VMEM(planes, F32),
            pltpu.VMEM(w_shape, BF16),
            pltpu.VMEM(w_shape, BF16),
            pltpu.SemaphoreType.DMA((GROUPS,)),
        ],
        compiler_params=pltpu.CompilerParams(vmem_limit_bytes=10 * MIB),
        cost_estimate=lasts(7.0),
        name="couple_gas",
    )(rows, near_gas, liquid, surface)

    returned = exchange(back, group)

    z_shape = (48, LANES)
    halos = [in_vmem(halo) for halo in x_halo + y_halo]
    field, *stepped = pl.pallas_call(
        functools.partial(first_step_kernel, size_x, size_y, turns_x),
        out_shape=[pltpu.VMEM(planes, F32)]
        + [pltpu.VMEM(x_shape, F32)] * turns_x
        + [pltpu.VMEM(y_shape, F32)] * 2
        + [jax.ShapeDtypeStruct(z_shape, F32)] * 2,
        in_specs=[vmem] * (turns_x + 3) + [whole],
        out_specs=[vmem] * (turns_x + 3) + [whole] * 2,
        input_output_aliases={1 + i: 1 + i for i in range(turns_x + 2)},
        compiler_params=pltpu.CompilerParams(vmem_limit_bytes=8 * MIB),
        cost_estimate=lasts(1.6),
        name="first_gas_step",
    )(near_gas, *halos, rate)
    halos, z_sends = stepped[:-2], stepped[-2:]
    z_halo = swap_all(z_sends, "gz", wrap=True)
    gas_next = pl.pallas_call(
        functools.partial(second_step_kernel, size_x, size_y, turns_x),
        out_shape=jax.ShapeDtypeStruct(flat.shape, F32),
        in_specs=[vmem] * (2 * turns_x + 3) + [whole] * 5 + [vmem],
        out_specs=hbm,
        scratch_shapes=[
            pltpu.VMEM(planes, F32),
            pltpu.VMEM((turns_x, size_y, species, LANES), F32),
            pltpu.VMEM((2, size_x, species, LANES), F32),
            pltpu.VMEM(planes, F32),
            pltpu.SemaphoreType.DMA((lines,)),
        ],
        compiler_params=pltpu.CompilerParams(vmem_limit_bytes=10 * MIB),
        cost_estimate=lasts(4.0),
        name="second_gas_step",
    )(field, *halos[:turns_x], *corners, *halos[turns_x:], *z_sends, *z_halo, rate, in_vmem(deposit))
    droplet_next = pl.pallas_call(
        functools.partial(droplet_kernel, cap, packed),
        out_shape=jax.ShapeDtypeStruct(droplet.shape, F32),
        in_specs=[whole] * 5 + [hbm],
        out_specs=hbm,
        scratch_shapes=[
            pltpu.VMEM(droplet.shape, F32),
            pltpu.VMEM((species, parcels), F32),
            pltpu.SemaphoreType.DMA((species // 8,)),
        ],
        compiler_params=pltpu.CompilerParams(vmem_limit_bytes=8 * MIB),
        cost_estimate=lasts(2.5),
        name="droplets",
    )(droplet, returned, slot, liquid, surface, in_hbm(gas_next))
    return (gas_next.reshape(gas.shape), droplet_next)


def solution(mesh):
    return jax.shard_map(
        on_device,
        mesh=mesh,
        in_specs=(
            P(None, "gx", "gy", "gz"),
            P(None, None, ("gx", "gy", "gz")),
            P(("gx", "gy", "gz"), None),
            P(None, ("gx", "gy", "gz")),
            P(None, ("gx", "gy", "gz")),
            P(("gx", "gy", "gz")),
            P(),
            P(),
            P(),
        ),
        out_specs=(P(None, "gx", "gy", "gz"), P(None, None, ("gx", "gy", "gz"))),
        check_vma=False,
    )
```

```python
import functools

import jax
import jax.numpy as jnp
from jax import lax
from jax.experimental import pallas as pl
from jax.experimental.pallas import tpu as pltpu
from jax.sharding import PartitionSpec as P

STENCIL = 8
DROP_STEPS = 4
GAS_STEPS = 2
LANES = 128
MIB = 1 << 20
NT = (((1,), (1,)), ((), ()))
HIGH = lax.Precision.HIGHEST
F32 = jnp.float32
BF16 = jnp.bfloat16


def iota(shape, dim):
    return lax.broadcasted_iota(jnp.int32, shape, dim)


def as_column(row):
    n = row.shape[1]
    return jnp.sum(jnp.where(iota((n, n), 0) == iota((n, n), 1), row, 0.0), axis=1, keepdims=True)


def leading(value):
    scaled = value * 65537.0
    return scaled - (scaled - value)


def split(value):
    high = leading(value)
    return high.astype(BF16), (value - high).astype(BF16)


def split_all(value):
    high = leading(value)
    rest = value - high
    middle = leading(rest)
    return high.astype(BF16), middle.astype(BF16), (rest - middle).astype(BF16)


def one_hot(hit):
    return jnp.where(hit, 1.0, 0.0).astype(BF16)


def surface_steps(nodes, gas_at, liquid, surface):
    emitted = None
    for step in range(DROP_STEPS):
        last = nodes[-1]
        flux = surface * (last - gas_at)
        emitted = flux if emitted is None else emitted + flux
        inner = [
            nodes[i] + liquid * (nodes[i + 1] - 2.0 * nodes[i] + nodes[i - 1])
            for i in range(1, len(nodes) - 1)
        ]
        if len(nodes) > 1:
            nodes = inner + [last + liquid * (nodes[-2] - last) - flux]
    return emitted


def surface_response(liquid, surface):
    return surface_steps([jnp.zeros_like(liquid)] * DROP_STEPS, 1.0, liquid, surface)


def pack_kernel(cap, size_x, size_y, turns_x, droplet, gas, *refs):
    sources, (send, slots, near_gas), refs = refs[:6], refs[6:9], refs[9:]
    x_sends, refs = refs[: 2 * turns_x], refs[2 * turns_x :]
    (owner, cells, weights, mass, liquid, surface), (tail, sems) = refs[:6], refs[6:]
    parcels = owner.shape[1]
    nodes, species = droplet.shape[0], droplet.shape[1]
    lines = gas.shape[1]
    pairs = list(zip(sources, refs[:6], strict=True))
    pairs.append((droplet.at[pl.ds(nodes - DROP_STEPS, DROP_STEPS)], tail))
    small = len(pairs)
    pairs += [(gas.at[:, line, :], near_gas.at[line]) for line in range(lines)]
    loads = [pltpu.make_async_copy(source, here, sems.at[i]) for i, (source, here) in enumerate(pairs)]
    for load in loads:
        load.start()
    for load in loads[: small - 1]:
        load.wait()
    wts = weights[...]
    norm = wts / jnp.sum(wts, axis=0, keepdims=True)
    mine = owner[...]
    column = jnp.transpose(jnp.broadcast_to(mine.astype(F32), (parcels, parcels)))
    earlier = (column == mine.astype(F32)) & (iota((parcels, parcels), 0) < iota((parcels, parcels), 1))
    rank = jnp.sum(jnp.where(earlier, 1.0, 0.0), axis=0, keepdims=True).astype(jnp.int32)
    slot = mine * cap + rank
    slots[...] = slot
    place = one_hot(iota((send.shape[0], parcels), 0) == slot)
    rest = jnp.zeros((LANES - species - 2 * STENCIL - 8, parcels), F32)
    liquid_col, surface_col = as_column(liquid[...]), as_column(surface[...])
    loads[small - 1].wait()
    emitted = surface_steps([tail[i] for i in range(DROP_STEPS)], 0.0, liquid_col, surface_col)
    values = jnp.concatenate(
        [
            mass[...] * emitted,
            cells[...].astype(F32),
            norm,
            jnp.broadcast_to(mass[...], (8, parcels)),
            rest,
        ],
        axis=0,
    )
    for load in loads[small:]:
        load.wait()
    even_x, _, _ = place_on("gx")
    for turn in range(turns_x):
        up = even_x == (turn == 0)
        near = jnp.where(up, size_x - 1, 0) * size_y
        far = jnp.where(up, size_x - 2, 1) * size_y
        for y in range(size_y):
            x_sends[turn][y] = near_gas[near + y]
            x_sends[turns_x + turn][y] = near_gas[far + y]
    parts = jnp.concatenate(split_all(values), axis=0)
    placed = lax.dot_general(place, parts, NT, preferred_element_type=F32)
    send[...] = placed[:, :LANES] + placed[:, LANES : 2 * LANES] + placed[:, 2 * LANES :]


def y_faces_kernel(size_x, size_y, near_gas, ya, yb):
    even_y, _, _ = place_on("gy")
    for turn, y_send in enumerate((ya, yb)):
        up = even_y == (turn == 0)
        near = jnp.where(up, size_y - 1, 0)
        far = jnp.where(up, size_y - 2, 1)
        for x in range(size_x):
            y_send[x] = near_gas[x * size_y + near]
            y_send[size_x + x] = near_gas[x * size_y + far]


def corner_kernel(size_x, ya, yb, *sends):
    even_x, _, _ = place_on("gx")
    even_y, _, _ = place_on("gy")
    for turn, send in enumerate(sends):
        x = jnp.where(even_x == (turn == 0), size_x - 1, 0)
        send[0], send[1] = low_high(even_y, ya[x], yb[x])


def couple_kernel(cap, packed, rows, gas, liquid, surface, back, deposit, w_high, w_low):
    slots = rows.shape[0]
    species = liquid.shape[1]
    lines = gas.shape[0]
    table = jnp.transpose(rows[...])
    first = species
    cell = table[first : first + STENCIL]
    wts = table[first + STENCIL : first + 2 * STENCIL]
    mass = table[first + 2 * STENCIL : first + 2 * STENCIL + 1]
    whole = wts
    for shift in range(1, STENCIL):
        same = cell == pltpu.roll(cell, shift, 0)
        whole = whole + jnp.where(same, pltpu.roll(wts, shift, 0), 0.0)
    tile = 16
    cell = cell.astype(jnp.int32)
    high_rows, low_rows = split(whole)
    named = [jnp.broadcast_to(cell[k : k + 1], (tile, slots)).astype(jnp.int16) for k in range(STENCIL)]
    highs = [jnp.broadcast_to(high_rows[k : k + 1], (tile, slots)) for k in range(STENCIL)]
    lows = [jnp.broadcast_to(low_rows[k : k + 1], (tile, slots)) for k in range(STENCIL)]

    def pair(ref, line):
        return ref[line : line + 2].reshape(2 * LANES, slots)

    gathered = jnp.zeros((species, slots), F32)
    for line in range(0, lines, 2):
        for part in range(2):
            for z in range(0, LANES, tile):
                along = (iota((tile, slots), 0) + ((line + part) * LANES + z)).astype(jnp.int16)
                high = jnp.zeros((tile, slots), BF16)
                low = jnp.zeros((tile, slots), BF16)
                for k in range(STENCIL):
                    hit = named[k] == along
                    high = jnp.where(hit, highs[k], high)
                    low = jnp.where(hit, lows[k], low)
                w_high[line + part, z : z + tile] = high
                w_low[line + part, z : z + tile] = low
        t_high, t_low = split(jnp.concatenate([gas[line], gas[line + 1]], axis=1))
        t_all = jnp.concatenate([t_high, t_low], axis=0)
        both = jnp.dot(t_all, pair(w_high, line), preferred_element_type=F32)
        extra = jnp.dot(t_high, pair(w_low, line), preferred_element_type=F32)
        gathered = gathered + both[:species] + both[species:] + extra
    gas_rows = jnp.transpose(gathered)
    if packed:
        gas_rows = gas_rows.reshape(slots // cap, cap, species)
        gas_rows = jnp.concatenate([gas_rows[:, : cap // 2], gas_rows[:, cap // 2 :]], axis=2)
        back[...] = gas_rows.reshape(slots // 2, 2 * species)
    else:
        back[...] = jnp.concatenate([gas_rows, jnp.zeros((slots, LANES - species), F32)], axis=1)
    response = surface_response(as_column(liquid[...]), as_column(surface[...]))
    s_high, s_low = split(table[:species] + mass * (response * gathered))
    s_all = jnp.concatenate([s_high, s_low], axis=0)
    s_only = jnp.concatenate([s_high, jnp.zeros_like(s_low)], axis=0)
    for line in range(0, lines, 2):
        both = lax.dot_general(pair(w_high, line), s_all, NT, preferred_element_type=F32)
        both = both + lax.dot_general(pair(w_low, line), s_only, NT, preferred_element_type=F32)
        for i in range(2):
            turned = jnp.transpose(both[i * LANES : (i + 1) * LANES])
            deposit[line + i] = turned[:species] + turned[species:]


def droplet_kernel(
    cap, packed, state_in, rows, slots, liquid, surface, _, state_out, state_next, gas_at, sems
):
    nodes, species, parcels = state_in.shape
    block = 8

    table = jnp.transpose(rows[...])
    count = rows.shape[0]
    at = iota((count, parcels), 0)
    slot = slots[...]
    if packed:
        half = cap // 2
        at = at // half * cap + at % half
        pairs = [(table[:species], at), (table[species:], at + half)]
    else:
        pairs = [(table[:species], at)]
    total = jnp.zeros((species, parcels), F32)
    for values, index in pairs:
        parts = jnp.concatenate(split_all(values), axis=0)
        placed = jnp.dot(parts, one_hot(index == slot), preferred_element_type=F32)
        total = total + placed[:species] + placed[species : 2 * species] + placed[2 * species :]
    gas_at[...] = total

    def save(i):
        at = pl.ds(i * block, block)
        return pltpu.make_async_copy(state_next.at[:, at], state_out.at[:, at], sems.at[i])

    @pl.loop(0, species // block, unroll=4)
    def _(i):
        at = pl.ds(pl.multiple_of(i * block, block), block)
        pick = i * block + iota((block, species), 0) == iota((block, species), 1)
        liquid_col = jnp.sum(jnp.where(pick, liquid[...], 0.0), axis=1, keepdims=True)
        surface_col = jnp.sum(jnp.where(pick, surface[...], 0.0), axis=1, keepdims=True)
        rate = jnp.broadcast_to(liquid_col, (block, parcels))
        keep = 1.0 - 2.0 * rate
        last_keep = jnp.broadcast_to(1.0 - liquid_col - surface_col, (block, parcels))
        from_gas = surface_col * gas_at[at, :]
        state = [state_in[node, at] for node in range(nodes)]
        for step in range(DROP_STEPS):
            state = (
                [keep * state[0] + (rate + rate) * state[1]]
                + [keep * state[n] + rate * (state[n - 1] + state[n + 1]) for n in range(1, nodes - 1)]
                + [last_keep * state[-1] + rate * state[-2] + from_gas]
            )
        for node in range(nodes):
            state_next[node, at] = state[node]
        save(i).start()

    for i in range(species // block):
        save(i).wait()


def place_on(axis):
    index, count = lax.axis_index(axis), lax.axis_size(axis)
    even = lax.rem(index, 2) == 0
    below = jnp.where(index > 0, 1.0, 0.0).astype(F32)
    above = jnp.where(index < count - 1, 1.0, 0.0).astype(F32)
    return even, below, above


def swaps(axis, wrap=False):
    count = lax.axis_size(axis)
    rounds = []
    for first in range(2):
        pairs = [(i, i + 1) for i in range(first, count - 1, 2)]
        if wrap and first == 1 and count > 2 and count % 2 == 0:
            pairs.append((count - 1, 0))
        if pairs:
            rounds.append(pairs + [(j, i) for i, j in pairs])
    return rounds


def swap_all(messages, axis, wrap=False):
    return [lax.ppermute(m, axis, pairs) for m, pairs in zip(messages, swaps(axis, wrap), strict=True)]


def low_high(even, first, second):
    if second is None:
        second = jnp.zeros_like(first)
    return jnp.where(even, second, first), jnp.where(even, first, second)


def beside_z(block):
    axis = block.ndim - 1
    lane = iota(block.shape, axis)
    before = jnp.where(lane == 0, 0.0, pltpu.roll(block, 1, axis))
    after = jnp.where(lane == LANES - 1, 0.0, pltpu.roll(block, LANES - 1, axis))
    return before + after


def beside_xy(planes, x, y, x_low, x_high, y_low, y_high):
    size_x, size_y = len(planes), len(planes[0])
    total = planes[x - 1][y]() if x > 0 else x_low(y)
    total = total + (planes[x + 1][y]() if x < size_x - 1 else x_high(y))
    total = total + (planes[x][y - 1]() if y > 0 else y_low(x))
    return total + (planes[x][y + 1]() if y < size_y - 1 else y_high(x))


def plane_at(ref, index):
    return lambda: ref[index]


def wide_rates(rate, rows):
    column = as_column(rate[...])
    column = jnp.concatenate([column] * (rows // column.shape[0]), axis=0)
    return jnp.broadcast_to(column, (rows, LANES))


def columns_of(block):
    turned = jnp.transpose(block)
    return turned[:1], turned[-1:]


def first_step_kernel(size_x, size_y, turns_x, gas, *refs):
    xs, refs = refs[:turns_x], refs[turns_x:]
    xs_far, refs = refs[:turns_x], refs[turns_x:]
    (ya, yb, rate, field), refs = refs[:4], refs[4:]
    xs_out, (ya_out, yb_out, za, zb) = refs[:turns_x], refs[turns_x:]
    species = rate.shape[1]
    lines = size_x * size_y
    even_x, below_x, above_x = place_on("gx")
    even_y, below_y, above_y = place_on("gy")
    even_z, _, _ = place_on("gz")
    wide = wide_rates(rate, species)
    keep = 1.0 - 6.0 * wide
    planes = [[plane_at(gas, x * size_y + y) for y in range(size_y)] for x in range(size_x)]

    def from_x(side, y):
        near = [ref[y] for ref in xs]
        return low_high(even_x, near[0], near[1] if turns_x == 2 else None)[side]

    def from_y(side, x):
        return low_high(even_y, ya[x], yb[x])[side]

    for x in range(size_x):
        for y in range(size_y):
            own = gas[x * size_y + y]
            total = beside_xy(
                planes,
                x,
                y,
                functools.partial(from_x, 0),
                functools.partial(from_x, 1),
                functools.partial(from_y, 0),
                functools.partial(from_y, 1),
            )
            field[x * size_y + y] = keep * own + wide * (total + beside_z(own))

    for turn, ref in enumerate(xs):
        up = even_x == (turn == 0)
        exists = jnp.where(up, above_x, below_x)
        inner = jnp.where(up, lines - size_y, 0)
        for y in range(size_y):
            own = ref[y]
            total = xs_far[turn][y] + exists * gas[inner + y]
            if y > 0:
                total = total + ref[y - 1]
            if y < size_y - 1:
                total = total + ref[y + 1]
            xs_out[turn][y] = keep * own + wide * (total + beside_z(own))

    for turn, (ref, ref_out) in enumerate(((ya, ya_out), (yb, yb_out))):
        up = even_y == (turn == 0)
        exists = jnp.where(up, above_y, below_y)
        inner = jnp.where(up, size_y - 1, 0)
        for x in range(size_x):
            own = ref[x]
            total = ref[size_x + x] + exists * gas[x * size_y + inner]
            if x > 0:
                total = total + ref[x - 1]
            if x < size_x - 1:
                total = total + ref[x + 1]
            ref_out[size_x + x] = keep * own + wide * (total + beside_z(own))

    rows = []
    each = LANES // species
    for ref in (gas, field):
        rows += [columns_of(ref[i : i + each].reshape(LANES, LANES)) for i in range(0, lines, each)]
    for ref in xs:
        rows += [columns_of(ref[i : i + each].reshape(LANES, LANES)) for i in range(0, size_y, each)]
    for ref in (ya, yb):
        rows += [columns_of(ref[i : i + each].reshape(LANES, LANES)) for i in range(0, size_x, each)]
    rest = [jnp.zeros((za.shape[0] - len(rows), LANES), F32)]
    low = jnp.concatenate([row[0] for row in rows] + rest, axis=0)
    high = jnp.concatenate([row[1] for row in rows] + rest, axis=0)
    za[...] = jnp.where(even_z, high, low)
    zb[...] = jnp.where(even_z, low, high)


def second_step_kernel(
    size_x, size_y, turns_x, field, *refs
):
    xs, refs = refs[:turns_x], refs[turns_x:]
    corners, refs = refs[:turns_x], refs[turns_x:]
    ya, yb, za, zb, za_in, zb_in, rate, deposit, out, now, now_x, now_y, result, sems = refs
    species = rate.shape[1]
    lines = size_x * size_y
    even_x, _, _ = place_on("gx")
    even_y, _, _ = place_on("gy")
    even, below, above = place_on("gz")
    each = LANES // species
    count = lines // each
    rates = jnp.concatenate([rate[...]] * each, axis=1)
    low, high = low_high(even, za_in[...], zb_in[...])
    low, high = jnp.where(below > 0.0, low, 0.0), jnp.where(above > 0.0, high, 0.0)
    own_low, own_high = low_high(even, za[...], zb[...])
    next_low = rates * (low[count : 2 * count] + below * rates * own_low[:count])
    next_high = rates * (high[count : 2 * count] + above * rates * own_high[:count])
    low, high = rates * low, rates * high

    def spread(low_row, high_row):
        turned = iota((LANES, LANES), 0)
        rows = jnp.where(turned == 0, low_row, jnp.where(turned == LANES - 1, high_row, 0.0))
        return jnp.transpose(rows)

    def row(i):
        return spread(low[i : i + 1], high[i : i + 1])

    def add_halo(target, source, start, count, first):
        for i in range(count):
            block = source[pl.ds(start + i * each, each)].reshape(LANES, LANES) + row(first + i)
            target[i * each : (i + 1) * each] = block.reshape(each, species, LANES)

    wide = wide_rates(rate, species)
    add_halo(now, field, 0, count, 0)
    first = 2 * count
    for turn, (ref, corner) in enumerate(zip(xs, corners, strict=True)):
        add_halo(now_x.at[turn], ref, 0, size_y // each, first)
        first = first + size_y // each
        now_x[turn, 0] = now_x[turn, 0] + wide * corner[0]
        now_x[turn, size_y - 1] = now_x[turn, size_y - 1] + wide * corner[1]
    for turn, ref in enumerate((ya, yb)):
        add_halo(now_y.at[turn], ref, size_x, size_x // each, first)
        first = first + size_x // each
        edges = [jnp.where(even_y == (turn == 0), corner[1], corner[0]) for corner in corners]
        edges = low_high(even_x, edges[0], edges[1] if turns_x == 2 else None)
        now_y[turn, 0] = now_y[turn, 0] + wide * edges[0]
        now_y[turn, size_x - 1] = now_y[turn, size_x - 1] + wide * edges[1]

    keep = 1.0 - 6.0 * wide
    planes = [[plane_at(now, x * size_y + y) for y in range(size_y)] for x in range(size_x)]

    def from_x(side, y):
        return low_high(even_x, now_x[0, y], now_x[1, y] if turns_x == 2 else None)[side]

    def from_y(side, x):
        return low_high(even_y, now_y[0, x], now_y[1, x])[side]

    saves = []
    for x in range(size_x):
        for y in range(size_y):
            line = x * size_y + y
            own = now[line]
            total = beside_xy(
                planes,
                x,
                y,
                functools.partial(from_x, 0),
                functools.partial(from_x, 1),
                functools.partial(from_y, 0),
                functools.partial(from_y, 1),
            )
            if line % each == 0:
                i = line // each
                ends = spread(next_low[i : i + 1], next_high[i : i + 1])
            part = ends[line % each * species : (line % each + 1) * species]
            result[line] = keep * own + wide * (total + beside_z(own)) + part + deposit[line]
            saves.append(pltpu.make_async_copy(result.at[line], out.at[:, line, :], sems.at[line]))
            saves[-1].start()
    for save in saves:
        save.wait()


def full(shape):
    return pl.BlockSpec(shape, lambda *_: (0,) * len(shape))


def lasts(microseconds):
    return pl.CostEstimate(flops=0, bytes_accessed=int(3.69e6 * microseconds), transcendentals=0)


def in_hbm(array):
    return pltpu.with_memory_space_constraint(array, pltpu.HBM)


def in_vmem(array):
    return pltpu.with_memory_space_constraint(array, pltpu.VMEM)


def exchange(rows, group):
    width = rows.shape[1]
    chunks = rows.reshape(group, -1, width)
    chunks = lax.all_to_all(chunks, ("gy", "gz"), split_axis=0, concat_axis=0, tiled=True)
    return chunks.reshape(-1, width)


def on_device(gas, droplet, owner, cells, weights, mass, liquid_rate, surface_rate, gas_rate):
    group = lax.axis_size("gy") * lax.axis_size("gz")
    nodes, species, parcels = droplet.shape
    cap = 2 * parcels // group
    slots = group * cap
    packed = cap % 16 == 0
    lines = gas.shape[1] * gas.shape[2]
    flat = gas.reshape(species, lines, LANES)
    planes = (lines, species, LANES)
    liquid = liquid_rate.reshape(1, species)
    surface = surface_rate.reshape(1, species)
    rate_spec = full((1, species))
    size_x, size_y = gas.shape[1], gas.shape[2]
    rate = gas_rate.reshape(1, species)
    vmem = pl.BlockSpec(memory_space=pltpu.VMEM)
    hbm = pl.BlockSpec(memory_space=pl.ANY)
    whole = pl.BlockSpec()
    turns_x = len(swaps("gx"))
    x_shape = (size_y, species, LANES)
    y_shape = (2 * size_x, species, LANES)

    send, slot, near_gas, *x_faces = pl.pallas_call(
        functools.partial(pack_kernel, cap, size_x, size_y, turns_x),
        out_shape=[
            pltpu.VMEM((slots, LANES), F32),
            pltpu.VMEM((1, parcels), jnp.int32),
            pltpu.VMEM(planes, F32),
        ]
        + [pltpu.VMEM(x_shape, F32)] * (2 * turns_x),
        in_specs=[hbm] * 8,
        out_specs=[vmem] * (3 + 2 * turns_x),
        scratch_shapes=[
            pltpu.VMEM((1, parcels), jnp.int32),
            pltpu.VMEM((STENCIL, parcels), jnp.int32),
            pltpu.VMEM((STENCIL, parcels), F32),
            pltpu.VMEM((1, parcels), F32),
            pltpu.VMEM((1, species), F32),
            pltpu.VMEM((1, species), F32),
            pltpu.VMEM((DROP_STEPS, species, parcels), F32),
            pltpu.SemaphoreType.DMA((7 + lines,)),
        ],
        compiler_params=pltpu.CompilerParams(vmem_limit_bytes=8 * MIB),
        cost_estimate=lasts(2.5),
        name="pack",
    )(
        in_hbm(droplet),
        in_hbm(flat),
        in_hbm(owner.reshape(1, parcels)),
        in_hbm(cells),
        in_hbm(weights),
        in_hbm(mass.reshape(1, parcels)),
        in_hbm(liquid),
        in_hbm(surface),
    )
    rows = exchange(send, group)

    y_faces = pl.pallas_call(
        functools.partial(y_faces_kernel, size_x, size_y),
        out_shape=[pltpu.VMEM(y_shape, F32)] * 2,
        in_specs=[vmem],
        out_specs=[vmem] * 2,
        compiler_params=pltpu.CompilerParams(vmem_limit_bytes=4 * MIB),
        cost_estimate=lasts(0.6),
        name="y_faces",
    )(near_gas)
    y_halo = swap_all(y_faces, "gy")
    x_near = swap_all(x_faces[:turns_x], "gx")
    x_far = swap_all(x_faces[turns_x:], "gx")

    corners = pl.pallas_call(
        functools.partial(corner_kernel, size_x),
        out_shape=[jax.ShapeDtypeStruct((2, species, LANES), F32)] * turns_x,
        in_specs=[vmem] * 2,
        out_specs=[vmem] * turns_x,
        compiler_params=pltpu.CompilerParams(vmem_limit_bytes=4 * MIB),
        cost_estimate=lasts(0.3),
        name="corner_planes",
    )(*y_halo)
    corners = swap_all(corners, "gx")

    back_rows = slots // 2 if packed else slots
    w_shape = (lines, LANES, slots)
    back, deposit = pl.pallas_call(
        functools.partial(couple_kernel, cap, packed),
        out_shape=[pltpu.VMEM((back_rows, LANES), F32), pltpu.VMEM(planes, F32)],
        in_specs=[vmem] * 2 + [whole] * 2,
        out_specs=[vmem, vmem],
        scratch_shapes=[
            pltpu.VMEM(w_shape, BF16),
            pltpu.VMEM(w_shape, BF16),
        ],
        compiler_params=pltpu.CompilerParams(vmem_limit_bytes=10 * MIB),
        cost_estimate=lasts(7.0),
        name="couple_gas",
    )(rows, near_gas, liquid, surface)

    returned = exchange(back, group)

    z_shape = (48, LANES)
    halos = [in_vmem(halo) for halo in x_near + x_far + y_halo]
    field, *stepped = pl.pallas_call(
        functools.partial(first_step_kernel, size_x, size_y, turns_x),
        out_shape=[pltpu.VMEM(planes, F32)]
        + [pltpu.VMEM(x_shape, F32)] * turns_x
        + [pltpu.VMEM(y_shape, F32)] * 2
        + [jax.ShapeDtypeStruct(z_shape, F32)] * 2,
        in_specs=[vmem] * (2 * turns_x + 3) + [whole],
        out_specs=[vmem] * (turns_x + 3) + [whole] * 2,
        input_output_aliases={1 + turns_x + i: 1 + i for i in range(turns_x + 2)},
        compiler_params=pltpu.CompilerParams(vmem_limit_bytes=8 * MIB),
        cost_estimate=lasts(1.6),
        name="first_gas_step",
    )(near_gas, *halos, rate)
    halos, z_sends = stepped[:-2], stepped[-2:]
    z_halo = swap_all(z_sends, "gz", wrap=True)
    gas_next = pl.pallas_call(
        functools.partial(second_step_kernel, size_x, size_y, turns_x),
        out_shape=jax.ShapeDtypeStruct(flat.shape, F32),
        in_specs=[vmem] * (2 * turns_x + 3) + [whole] * 5 + [vmem],
        out_specs=hbm,
        scratch_shapes=[
            pltpu.VMEM(planes, F32),
            pltpu.VMEM((turns_x, size_y, species, LANES), F32),
            pltpu.VMEM((2, size_x, species, LANES), F32),
            pltpu.VMEM(planes, F32),
            pltpu.SemaphoreType.DMA((lines,)),
        ],
        compiler_params=pltpu.CompilerParams(vmem_limit_bytes=10 * MIB),
        cost_estimate=lasts(4.0),
        name="second_gas_step",
    )(field, *halos[:turns_x], *corners, *halos[turns_x:], *z_sends, *z_halo, rate, in_vmem(deposit))
    droplet_next = pl.pallas_call(
        functools.partial(droplet_kernel, cap, packed),
        out_shape=jax.ShapeDtypeStruct(droplet.shape, F32),
        in_specs=[whole] * 5 + [hbm],
        out_specs=hbm,
        scratch_shapes=[
            pltpu.VMEM(droplet.shape, F32),
            pltpu.VMEM((species, parcels), F32),
            pltpu.SemaphoreType.DMA((species // 8,)),
        ],
        compiler_params=pltpu.CompilerParams(vmem_limit_bytes=8 * MIB),
        cost_estimate=lasts(2.5),
        name="droplets",
    )(droplet, returned, slot, liquid, surface, in_hbm(gas_next))
    return (gas_next.reshape(gas.shape), droplet_next)


def solution(mesh):
    return jax.shard_map(
        on_device,
        mesh=mesh,
        in_specs=(
            P(None, "gx", "gy", "gz"),
            P(None, None, ("gx", "gy", "gz")),
            P(("gx", "gy", "gz"), None),
            P(None, ("gx", "gy", "gz")),
            P(None, ("gx", "gy", "gz")),
            P(("gx", "gy", "gz")),
            P(),
            P(),
            P(),
        ),
        out_specs=(P(None, "gx", "gy", "gz"), P(None, None, ("gx", "gy", "gz"))),
        check_vma=False,
    )
```

```python
import functools

import jax
import jax.numpy as jnp
from jax import lax
from jax.experimental import pallas as pl
from jax.experimental.pallas import tpu as pltpu
from jax.sharding import PartitionSpec as P

STENCIL = 8
DROP_STEPS = 4
GAS_STEPS = 2
LANES = 128
MIB = 1 << 20
NT = (((1,), (1,)), ((), ()))
HIGH = lax.Precision.HIGHEST
F32 = jnp.float32
BF16 = jnp.bfloat16


def iota(shape, dim):
    return lax.broadcasted_iota(jnp.int32, shape, dim)


def as_column(row):
    n = row.shape[1]
    return jnp.sum(jnp.where(iota((n, n), 0) == iota((n, n), 1), row, 0.0), axis=1, keepdims=True)


def leading(value):
    scaled = value * 65537.0
    return scaled - (scaled - value)


def split(value):
    high = leading(value)
    return high.astype(BF16), (value - high).astype(BF16)


def split_all(value):
    high = leading(value)
    rest = value - high
    middle = leading(rest)
    return high.astype(BF16), middle.astype(BF16), (rest - middle).astype(BF16)


def one_hot(hit):
    return jnp.where(hit, 1.0, 0.0).astype(BF16)


def surface_steps(nodes, gas_at, liquid, surface):
    emitted = None
    for step in range(DROP_STEPS):
        last = nodes[-1]
        flux = surface * (last - gas_at)
        emitted = flux if emitted is None else emitted + flux
        inner = [
            nodes[i] + liquid * (nodes[i + 1] - 2.0 * nodes[i] + nodes[i - 1])
            for i in range(1, len(nodes) - 1)
        ]
        if len(nodes) > 1:
            nodes = inner + [last + liquid * (nodes[-2] - last) - flux]
    return emitted


def surface_response(liquid, surface):
    return surface_steps([jnp.zeros_like(liquid)] * DROP_STEPS, 1.0, liquid, surface)


def pack_kernel(cap, size_x, size_y, turns_x, droplet, gas, *refs):
    sources, (send, slots, near_gas), refs = refs[:6], refs[6:9], refs[9:]
    x_sends, refs = refs[: 2 * turns_x], refs[2 * turns_x :]
    (owner, cells, weights, mass, liquid, surface), (tail, sems) = refs[:6], refs[6:]
    parcels = owner.shape[1]
    nodes, species = droplet.shape[0], droplet.shape[1]
    lines = gas.shape[1]
    pairs = list(zip(sources, refs[:6], strict=True))
    pairs.append((droplet.at[pl.ds(nodes - DROP_STEPS, DROP_STEPS)], tail))
    small = len(pairs)
    pairs += [(gas.at[:, line, :], near_gas.at[line]) for line in range(lines)]
    loads = [pltpu.make_async_copy(source, here, sems.at[i]) for i, (source, here) in enumerate(pairs)]
    for load in loads:
        load.start()
    for load in loads[: small - 1]:
        load.wait()
    wts = weights[...]
    norm = wts / jnp.sum(wts, axis=0, keepdims=True)
    mine = owner[...]
    column = jnp.transpose(jnp.broadcast_to(mine.astype(F32), (parcels, parcels)))
    earlier = (column == mine.astype(F32)) & (iota((parcels, parcels), 0) < iota((parcels, parcels), 1))
    rank = jnp.sum(jnp.where(earlier, 1.0, 0.0), axis=0, keepdims=True).astype(jnp.int32)
    slot = mine * cap + rank
    slots[...] = slot
    place = one_hot(iota((send.shape[0], parcels), 0) == slot)
    rest = jnp.zeros((LANES - species - 2 * STENCIL - 8, parcels), F32)
    liquid_col, surface_col = as_column(liquid[...]), as_column(surface[...])
    loads[small - 1].wait()
    emitted = surface_steps([tail[i] for i in range(DROP_STEPS)], 0.0, liquid_col, surface_col)
    values = jnp.concatenate(
        [
            mass[...] * emitted,
            cells[...].astype(F32),
            norm,
            jnp.broadcast_to(mass[...], (8, parcels)),
            rest,
        ],
        axis=0,
    )
    for load in loads[small:]:
        load.wait()
    even_x, _, _ = place_on("gx")
    for turn in range(turns_x):
        up = even_x == (turn == 0)
        near = jnp.where(up, size_x - 1, 0) * size_y
        far = jnp.where(up, size_x - 2, 1) * size_y
        for y in range(size_y):
            x_sends[turn][y] = near_gas[near + y]
            x_sends[turns_x + turn][y] = near_gas[far + y]
    parts = jnp.concatenate(split_all(values), axis=0)
    placed = lax.dot_general(place, parts, NT, preferred_element_type=F32)
    send[...] = placed[:, :LANES] + placed[:, LANES : 2 * LANES] + placed[:, 2 * LANES :]


def y_faces_kernel(size_x, size_y, near_gas, ya, yb):
    even_y, _, _ = place_on("gy")
    for turn, y_send in enumerate((ya, yb)):
        up = even_y == (turn == 0)
        near = jnp.where(up, size_y - 1, 0)
        far = jnp.where(up, size_y - 2, 1)
        for x in range(size_x):
            y_send[x] = near_gas[x * size_y + near]
            y_send[size_x + x] = near_gas[x * size_y + far]


def corner_kernel(size_x, ya, yb, *sends):
    even_x, _, _ = place_on("gx")
    even_y, below_y, above_y = place_on("gy")
    for turn, send in enumerate(sends):
        x = jnp.where(even_x == (turn == 0), size_x - 1, 0)
        send[0], send[1] = low_high(even_y, ya[x], second_round(even_y, below_y, above_y, yb[x]))


def couple_kernel(cap, packed, rows, gas, liquid, surface, back, deposit, w_high, w_low):
    slots = rows.shape[0]
    species = liquid.shape[1]
    lines = gas.shape[0]
    table = jnp.transpose(rows[...])
    first = species
    cell = table[first : first + STENCIL]
    wts = table[first + STENCIL : first + 2 * STENCIL]
    mass = table[first + 2 * STENCIL : first + 2 * STENCIL + 1]
    whole = wts
    for shift in range(1, STENCIL):
        same = cell == pltpu.roll(cell, shift, 0)
        whole = whole + jnp.where(same, pltpu.roll(wts, shift, 0), 0.0)
    tile = 16
    cell = cell.astype(jnp.int32)
    high_rows, low_rows = split(whole)
    named = [jnp.broadcast_to(cell[k : k + 1], (tile, slots)).astype(jnp.int16) for k in range(STENCIL)]
    highs = [jnp.broadcast_to(high_rows[k : k + 1], (tile, slots)) for k in range(STENCIL)]
    lows = [jnp.broadcast_to(low_rows[k : k + 1], (tile, slots)) for k in range(STENCIL)]

    def pair(ref, line):
        return ref[line : line + 2].reshape(2 * LANES, slots)

    gathered = jnp.zeros((species, slots), F32)
    for line in range(0, lines, 2):
        for part in range(2):
            for z in range(0, LANES, tile):
                along = (iota((tile, slots), 0) + ((line + part) * LANES + z)).astype(jnp.int16)
                high = jnp.zeros((tile, slots), BF16)
                low = jnp.zeros((tile, slots), BF16)
                for k in range(STENCIL):
                    hit = named[k] == along
                    high = jnp.where(hit, highs[k], high)
                    low = jnp.where(hit, lows[k], low)
                w_high[line + part, z : z + tile] = high
                w_low[line + part, z : z + tile] = low
        t_high, t_low = split(jnp.concatenate([gas[line], gas[line + 1]], axis=1))
        t_all = jnp.concatenate([t_high, t_low], axis=0)
        both = jnp.dot(t_all, pair(w_high, line), preferred_element_type=F32)
        extra = jnp.dot(t_high, pair(w_low, line), preferred_element_type=F32)
        gathered = gathered + both[:species] + both[species:] + extra
    gas_rows = jnp.transpose(gathered)
    if packed:
        gas_rows = gas_rows.reshape(slots // cap, cap, species)
        gas_rows = jnp.concatenate([gas_rows[:, : cap // 2], gas_rows[:, cap // 2 :]], axis=2)
        back[...] = gas_rows.reshape(slots // 2, 2 * species)
    else:
        back[...] = jnp.concatenate([gas_rows, jnp.zeros((slots, LANES - species), F32)], axis=1)
    response = surface_response(as_column(liquid[...]), as_column(surface[...]))
    s_high, s_low = split(table[:species] + mass * (response * gathered))
    s_all = jnp.concatenate([s_high, s_low], axis=0)
    s_only = jnp.concatenate([s_high, jnp.zeros_like(s_low)], axis=0)
    for line in range(0, lines, 2):
        both = lax.dot_general(pair(w_high, line), s_all, NT, preferred_element_type=F32)
        both = both + lax.dot_general(pair(w_low, line), s_only, NT, preferred_element_type=F32)
        for i in range(2):
            turned = jnp.transpose(both[i * LANES : (i + 1) * LANES])
            deposit[line + i] = turned[:species] + turned[species:]


def droplet_kernel(
    cap, packed, state_in, rows, slots, liquid, surface, _, state_out, state_next, gas_at, sems
):
    nodes, species, parcels = state_in.shape
    block = 8

    table = jnp.transpose(rows[...])
    count = rows.shape[0]
    at = iota((count, parcels), 0)
    slot = slots[...]
    if packed:
        half = cap // 2
        at = at // half * cap + at % half
        pairs = [(table[:species], at), (table[species:], at + half)]
    else:
        pairs = [(table[:species], at)]
    total = jnp.zeros((species, parcels), F32)
    for values, index in pairs:
        parts = jnp.concatenate(split_all(values), axis=0)
        placed = jnp.dot(parts, one_hot(index == slot), preferred_element_type=F32)
        total = total + placed[:species] + placed[species : 2 * species] + placed[2 * species :]
    gas_at[...] = total

    def save(i):
        at = pl.ds(i * block, block)
        return pltpu.make_async_copy(state_next.at[:, at], state_out.at[:, at], sems.at[i])

    @pl.loop(0, species // block, unroll=4)
    def _(i):
        at = pl.ds(pl.multiple_of(i * block, block), block)
        pick = i * block + iota((block, species), 0) == iota((block, species), 1)
        liquid_col = jnp.sum(jnp.where(pick, liquid[...], 0.0), axis=1, keepdims=True)
        surface_col = jnp.sum(jnp.where(pick, surface[...], 0.0), axis=1, keepdims=True)
        rate = jnp.broadcast_to(liquid_col, (block, parcels))
        keep = 1.0 - 2.0 * rate
        last_keep = jnp.broadcast_to(1.0 - liquid_col - surface_col, (block, parcels))
        from_gas = surface_col * gas_at[at, :]
        state = [state_in[node, at] for node in range(nodes)]
        for step in range(DROP_STEPS):
            state = (
                [keep * state[0] + (rate + rate) * state[1]]
                + [keep * state[n] + rate * (state[n - 1] + state[n + 1]) for n in range(1, nodes - 1)]
                + [last_keep * state[-1] + rate * state[-2] + from_gas]
            )
        for node in range(nodes):
            state_next[node, at] = state[node]
        save(i).start()

    for i in range(species // block):
        save(i).wait()


def place_on(axis):
    index, count = lax.axis_index(axis), lax.axis_size(axis)
    even = lax.rem(index, 2) == 0
    below = jnp.where(index > 0, 1.0, 0.0).astype(F32)
    above = jnp.where(index < count - 1, 1.0, 0.0).astype(F32)
    return even, below, above


def swaps(axis, closed=False, spare=None):
    count = lax.axis_size(axis)
    across = 1 if spare is None else lax.axis_size(spare)
    rounds = []
    for first in range(2):
        pairs = [(i * across + j, (i + 1) * across + j) for i in range(first, count - 1, 2) for j in range(across)]
        if closed and first == 1 and count > 2 and count % 2 == 0:
            if spare is None:
                pairs.append((count - 1, 0))
            elif across % 2 == 0:
                pairs += [(i * across + j, i * across + j + 1) for i in (0, count - 1) for j in range(0, across, 2)]
        if pairs:
            rounds.append(pairs + [(j, i) for i, j in pairs])
    return rounds


def swap_all(messages, axis, closed=False, spare=None):
    axes = axis if spare is None else (axis, spare)
    return [lax.ppermute(m, axes, pairs) for m, pairs in zip(messages, swaps(axis, closed, spare), strict=True)]


def second_round(even, below, above, block):
    return jnp.where(jnp.where(even, below, above) > 0.0, block, 0.0)


def low_high(even, first, second):
    if second is None:
        second = jnp.zeros_like(first)
    return jnp.where(even, second, first), jnp.where(even, first, second)


def beside_z(block):
    axis = block.ndim - 1
    lane = iota(block.shape, axis)
    before = jnp.where(lane == 0, 0.0, pltpu.roll(block, 1, axis))
    after = jnp.where(lane == LANES - 1, 0.0, pltpu.roll(block, LANES - 1, axis))
    return before + after


def beside_xy(planes, x, y, x_low, x_high, y_low, y_high):
    size_x, size_y = len(planes), len(planes[0])
    total = planes[x - 1][y]() if x > 0 else x_low(y)
    total = total + (planes[x + 1][y]() if x < size_x - 1 else x_high(y))
    total = total + (planes[x][y - 1]() if y > 0 else y_low(x))
    return total + (planes[x][y + 1]() if y < size_y - 1 else y_high(x))


def plane_at(ref, index):
    return lambda: ref[index]


def wide_rates(rate, rows):
    column = as_column(rate[...])
    column = jnp.concatenate([column] * (rows // column.shape[0]), axis=0)
    return jnp.broadcast_to(column, (rows, LANES))


def columns_of(block):
    turned = jnp.transpose(block)
    return turned[:1], turned[-1:]


def first_step_kernel(size_x, size_y, turns_x, gas, *refs):
    xs, refs = refs[:turns_x], refs[turns_x:]
    xs_far, refs = refs[:turns_x], refs[turns_x:]
    (ya, yb, rate, field), refs = refs[:4], refs[4:]
    xs_out, (ya_out, yb_out, za, zb) = refs[:turns_x], refs[turns_x:]
    species = rate.shape[1]
    lines = size_x * size_y
    even_x, below_x, above_x = place_on("gx")
    even_y, below_y, above_y = place_on("gy")
    even_z, _, _ = place_on("gz")
    wide = wide_rates(rate, species)
    keep = 1.0 - 6.0 * wide
    planes = [[plane_at(gas, x * size_y + y) for y in range(size_y)] for x in range(size_x)]

    def from_x(side, y):
        near = [ref[y] for ref in xs]
        return low_high(even_x, near[0], near[1] if turns_x == 2 else None)[side]

    def from_y(side, x):
        return low_high(even_y, ya[x], second_round(even_y, below_y, above_y, yb[x]))[side]

    for x in range(size_x):
        for y in range(size_y):
            own = gas[x * size_y + y]
            total = beside_xy(
                planes,
                x,
                y,
                functools.partial(from_x, 0),
                functools.partial(from_x, 1),
                functools.partial(from_y, 0),
                functools.partial(from_y, 1),
            )
            field[x * size_y + y] = keep * own + wide * (total + beside_z(own))

    for turn, ref in enumerate(xs):
        up = even_x == (turn == 0)
        exists = jnp.where(up, above_x, below_x)
        inner = jnp.where(up, lines - size_y, 0)
        for y in range(size_y):
            own = ref[y]
            total = xs_far[turn][y] + exists * gas[inner + y]
            if y > 0:
                total = total + ref[y - 1]
            if y < size_y - 1:
                total = total + ref[y + 1]
            xs_out[turn][y] = keep * own + wide * (total + beside_z(own))

    for turn, (ref, ref_out) in enumerate(((ya, ya_out), (yb, yb_out))):
        up = even_y == (turn == 0)
        exists = jnp.where(up, above_y, below_y)
        inner = jnp.where(up, size_y - 1, 0)
        for x in range(size_x):
            own = ref[x]
            total = ref[size_x + x] + exists * gas[x * size_y + inner]
            if x > 0:
                total = total + ref[x - 1]
            if x < size_x - 1:
                total = total + ref[x + 1]
            ref_out[size_x + x] = keep * own + wide * (total + beside_z(own))

    rows = []
    each = LANES // species
    for ref in (gas, field):
        rows += [columns_of(ref[i : i + each].reshape(LANES, LANES)) for i in range(0, lines, each)]
    for ref in xs:
        rows += [columns_of(ref[i : i + each].reshape(LANES, LANES)) for i in range(0, size_y, each)]
    for ref in (ya, yb):
        rows += [columns_of(ref[i : i + each].reshape(LANES, LANES)) for i in range(0, size_x, each)]
    rest = [jnp.zeros((za.shape[0] - len(rows), LANES), F32)]
    low = jnp.concatenate([row[0] for row in rows] + rest, axis=0)
    high = jnp.concatenate([row[1] for row in rows] + rest, axis=0)
    za[...] = jnp.where(even_z, high, low)
    zb[...] = jnp.where(even_z, low, high)


def second_step_kernel(size_x, size_y, turns_x, field, *refs):
    xs, (ya, yb, rate, deposit, out) = refs[:turns_x], refs[turns_x:]
    species = rate.shape[1]
    even_x, _, _ = place_on("gx")
    even_y, below_y, above_y = place_on("gy")
    wide = wide_rates(rate, species)
    keep = 1.0 - 6.0 * wide
    planes = [[plane_at(field, x * size_y + y) for y in range(size_y)] for x in range(size_x)]

    def from_x(side, y):
        return low_high(even_x, xs[0][y], xs[1][y] if turns_x == 2 else None)[side]

    def from_y(side, x):
        second = second_round(even_y, below_y, above_y, yb[size_x + x])
        return low_high(even_y, ya[size_x + x], second)[side]

    for x in range(size_x):
        for y in range(size_y):
            line = x * size_y + y
            own = field[line]
            total = beside_xy(
                planes,
                x,
                y,
                functools.partial(from_x, 0),
                functools.partial(from_x, 1),
                functools.partial(from_y, 0),
                functools.partial(from_y, 1),
            )
            out[line] = keep * own + wide * (total + beside_z(own)) + deposit[line]


def close_kernel(size_x, size_y, turns_x, partial, *refs):
    corners, (za, zb, za_in, zb_in, rate, out, result, sems) = refs[:turns_x], refs[turns_x:]
    species = rate.shape[1]
    lines = size_x * size_y
    each = LANES // species
    count, rows_x, rows_y = lines // each, size_y // each, size_x // each
    even_x, _, _ = place_on("gx")
    even_y, below_y, above_y = place_on("gy")
    even, below, above = place_on("gz")
    rates = jnp.concatenate([rate[...]] * each, axis=1)
    keep = 1.0 - 6.0 * rates
    incoming = low_high(even, za_in[...], zb_in[...])
    leaving = low_high(even, za[...], zb[...])
    row, lane = iota((count, LANES), 0), iota((count, LANES), 1)
    first_place = (lane < species) & (row % rows_x == 0)
    last_place = (lane >= LANES - species) & (row % rows_x == rows_x - 1)
    blank = jnp.zeros((rows_x - 1, LANES), F32)
    outer, inner = [], []
    for column, own, exists in zip(incoming, leaving, (below, above), strict=True):
        column = rates * jnp.where(exists > 0.0, column, 0.0)
        main, partly = column[:count], column[count : 2 * count]
        at = 2 * count
        sides = [column[at + i * rows_x : at + (i + 1) * rows_x] for i in range(turns_x)]
        x_low, x_high = low_high(even_x, sides[0], sides[1] if turns_x == 2 else None)
        at = at + turns_x * rows_x
        sides = [column[at + i * rows_y : at + (i + 1) * rows_y] for i in range(2)]
        y_low, y_high = low_high(even_y, sides[0], second_round(even_y, below_y, above_y, sides[1]))
        low_rows, high_rows = [], []
        for x in range(size_x):
            i, part = x // each, x % each
            low_row, high_row = y_low[i : i + 1], y_high[i : i + 1]
            if part > 0:
                low_row = pltpu.roll(low_row, LANES - part * species, 1)
            if part < each - 1:
                high_row = pltpu.roll(high_row, (each - 1 - part) * species, 1)
            low_rows += [low_row, blank]
            high_rows += [blank, high_row]
        ahead = pltpu.roll(main, LANES - species, 1)
        after = jnp.where(lane >= LANES - species, jnp.concatenate([ahead[1:], ahead[-1:]], axis=0), ahead)
        after = jnp.where(last_place, jnp.concatenate(high_rows, axis=0), after)
        behind = pltpu.roll(main, species, 1)
        before = jnp.where(lane < species, jnp.concatenate([behind[:1], behind[:-1]], axis=0), behind)
        before = jnp.where(first_place, jnp.concatenate(low_rows, axis=0), before)
        total = before + after + jnp.concatenate([x_low, main[:-rows_x]], axis=0)
        total = total + jnp.concatenate([main[rows_x:], x_high], axis=0)
        outer.append(keep * main + rates * total + partly + exists * rates * rates * own[:count])
        inner.append(rates * main)

    wide = wide_rates(rate, species)
    twice = 2.0 * wide * wide
    edge = {}
    for i, y in enumerate((0, size_y - 1)):
        planes = low_high(even_x, corners[0][i], corners[1][i] if turns_x == 2 else None)
        edge[y], edge[lines - size_y + y] = planes
    turned = iota((LANES, LANES), 0)
    saves = []
    for i in range(count):
        at = slice(i, i + 1)
        block = jnp.where(turned == 0, outer[0][at], jnp.where(turned == 1, inner[0][at], 0.0))
        block = jnp.where(turned == LANES - 2, inner[1][at], block)
        block = jnp.transpose(jnp.where(turned == LANES - 1, outer[1][at], block))
        for part in range(each):
            line = i * each + part
            total = partial[line] + block[part * species : (part + 1) * species]
            if line in edge:
                total = total + twice * edge[line]
            result[line] = total
            saves.append(pltpu.make_async_copy(result.at[line], out.at[:, line, :], sems.at[line]))
            saves[-1].start()
    for save in saves:
        save.wait()


def full(shape):
    return pl.BlockSpec(shape, lambda *_: (0,) * len(shape))


def lasts(microseconds):
    return pl.CostEstimate(flops=0, bytes_accessed=int(3.69e6 * microseconds), transcendentals=0)


def in_hbm(array):
    return pltpu.with_memory_space_constraint(array, pltpu.HBM)


def in_vmem(array):
    return pltpu.with_memory_space_constraint(array, pltpu.VMEM)


def exchange(rows, group):
    width = rows.shape[1]
    chunks = rows.reshape(group, -1, width)
    chunks = lax.all_to_all(chunks, ("gy", "gz"), split_axis=0, concat_axis=0, tiled=True)
    return chunks.reshape(-1, width)


def on_device(gas, droplet, owner, cells, weights, mass, liquid_rate, surface_rate, gas_rate):
    group = lax.axis_size("gy") * lax.axis_size("gz")
    nodes, species, parcels = droplet.shape
    cap = 2 * parcels // group
    slots = group * cap
    packed = cap % 16 == 0
    lines = gas.shape[1] * gas.shape[2]
    flat = gas.reshape(species, lines, LANES)
    planes = (lines, species, LANES)
    liquid = liquid_rate.reshape(1, species)
    surface = surface_rate.reshape(1, species)
    rate_spec = full((1, species))
    size_x, size_y = gas.shape[1], gas.shape[2]
    rate = gas_rate.reshape(1, species)
    vmem = pl.BlockSpec(memory_space=pltpu.VMEM)
    hbm = pl.BlockSpec(memory_space=pl.ANY)
    whole = pl.BlockSpec()
    turns_x = len(swaps("gx"))
    x_shape = (size_y, species, LANES)
    y_shape = (2 * size_x, species, LANES)

    send, slot, near_gas, *x_faces = pl.pallas_call(
        functools.partial(pack_kernel, cap, size_x, size_y, turns_x),
        out_shape=[
            pltpu.VMEM((slots, LANES), F32),
            pltpu.VMEM((1, parcels), jnp.int32),
            pltpu.VMEM(planes, F32),
        ]
        + [pltpu.VMEM(x_shape, F32)] * (2 * turns_x),
        in_specs=[hbm] * 8,
        out_specs=[vmem] * (3 + 2 * turns_x),
        scratch_shapes=[
            pltpu.VMEM((1, parcels), jnp.int32),
            pltpu.VMEM((STENCIL, parcels), jnp.int32),
            pltpu.VMEM((STENCIL, parcels), F32),
            pltpu.VMEM((1, parcels), F32),
            pltpu.VMEM((1, species), F32),
            pltpu.VMEM((1, species), F32),
            pltpu.VMEM((DROP_STEPS, species, parcels), F32),
            pltpu.SemaphoreType.DMA((7 + lines,)),
        ],
        compiler_params=pltpu.CompilerParams(vmem_limit_bytes=8 * MIB),
        cost_estimate=lasts(2.5),
        name="pack",
    )(
        in_hbm(droplet),
        in_hbm(flat),
        in_hbm(owner.reshape(1, parcels)),
        in_hbm(cells),
        in_hbm(weights),
        in_hbm(mass.reshape(1, parcels)),
        in_hbm(liquid),
        in_hbm(surface),
    )
    rows = exchange(send, group)

    y_faces = pl.pallas_call(
        functools.partial(y_faces_kernel, size_x, size_y),
        out_shape=[pltpu.VMEM(y_shape, F32)] * 2,
        in_specs=[vmem],
        out_specs=[vmem] * 2,
        compiler_params=pltpu.CompilerParams(vmem_limit_bytes=4 * MIB),
        cost_estimate=lasts(0.6),
        name="y_faces",
    )(near_gas)
    y_halo = swap_all(y_faces, "gy", closed=True, spare="gz")
    x_near = swap_all(x_faces[:turns_x], "gx")
    x_far = swap_all(x_faces[turns_x:], "gx")

    corners = pl.pallas_call(
        functools.partial(corner_kernel, size_x),
        out_shape=[jax.ShapeDtypeStruct((2, species, LANES), F32)] * turns_x,
        in_specs=[vmem] * 2,
        out_specs=[vmem] * turns_x,
        compiler_params=pltpu.CompilerParams(vmem_limit_bytes=4 * MIB),
        cost_estimate=lasts(0.3),
        name="corner_planes",
    )(*y_halo)
    corners = swap_all(corners, "gx")

    back_rows = slots // 2 if packed else slots
    w_shape = (lines, LANES, slots)
    back, deposit = pl.pallas_call(
        functools.partial(couple_kernel, cap, packed),
        out_shape=[pltpu.VMEM((back_rows, LANES), F32), pltpu.VMEM(planes, F32)],
        in_specs=[vmem] * 2 + [whole] * 2,
        out_specs=[vmem, vmem],
        scratch_shapes=[
            pltpu.VMEM(w_shape, BF16),
            pltpu.VMEM(w_shape, BF16),
        ],
        compiler_params=pltpu.CompilerParams(vmem_limit_bytes=10 * MIB),
        cost_estimate=lasts(7.0),
        name="couple_gas",
    )(rows, near_gas, liquid, surface)

    returned = exchange(back, group)

    z_shape = (48, LANES)
    halos = [in_vmem(halo) for halo in x_near + x_far + y_halo]
    field, *stepped = pl.pallas_call(
        functools.partial(first_step_kernel, size_x, size_y, turns_x),
        out_shape=[pltpu.VMEM(planes, F32)]
        + [pltpu.VMEM(x_shape, F32)] * turns_x
        + [pltpu.VMEM(y_shape, F32)] * 2
        + [jax.ShapeDtypeStruct(z_shape, F32)] * 2,
        in_specs=[vmem] * (2 * turns_x + 3) + [whole],
        out_specs=[vmem] * (turns_x + 3) + [whole] * 2,
        input_output_aliases={1 + turns_x + i: 1 + i for i in range(turns_x + 2)},
        compiler_params=pltpu.CompilerParams(vmem_limit_bytes=8 * MIB),
        cost_estimate=lasts(1.6),
        name="first_gas_step",
    )(near_gas, *halos, rate)
    halos, z_sends = stepped[:-2], stepped[-2:]
    z_halo = swap_all(z_sends, "gz", closed=True)
    partial = pl.pallas_call(
        functools.partial(second_step_kernel, size_x, size_y, turns_x),
        out_shape=pltpu.VMEM(planes, F32),
        in_specs=[vmem] * (turns_x + 3) + [whole, vmem],
        out_specs=vmem,
        compiler_params=pltpu.CompilerParams(vmem_limit_bytes=4 * MIB),
        cost_estimate=lasts(1.3),
        name="second_gas_step",
    )(field, *halos, rate, in_vmem(deposit))
    gas_next = pl.pallas_call(
        functools.partial(close_kernel, size_x, size_y, turns_x),
        out_shape=jax.ShapeDtypeStruct(flat.shape, F32),
        in_specs=[vmem] * (1 + turns_x) + [whole] * 5,
        out_specs=hbm,
        scratch_shapes=[pltpu.VMEM(planes, F32), pltpu.SemaphoreType.DMA((lines,))],
        compiler_params=pltpu.CompilerParams(vmem_limit_bytes=6 * MIB),
        cost_estimate=lasts(1.5),
        name="close_gas_step",
    )(in_vmem(partial), *corners, *z_sends, *z_halo, rate)
    droplet_next = pl.pallas_call(
        functools.partial(droplet_kernel, cap, packed),
        out_shape=jax.ShapeDtypeStruct(droplet.shape, F32),
        in_specs=[whole] * 5 + [hbm],
        out_specs=hbm,
        scratch_shapes=[
            pltpu.VMEM(droplet.shape, F32),
            pltpu.VMEM((species, parcels), F32),
            pltpu.SemaphoreType.DMA((species // 8,)),
        ],
        compiler_params=pltpu.CompilerParams(vmem_limit_bytes=8 * MIB),
        cost_estimate=lasts(2.5),
        name="droplets",
    )(droplet, returned, slot, liquid, surface, in_hbm(gas_next))
    return (gas_next.reshape(gas.shape), droplet_next)


def solution(mesh):
    return jax.shard_map(
        on_device,
        mesh=mesh,
        in_specs=(
            P(None, "gx", "gy", "gz"),
            P(None, None, ("gx", "gy", "gz")),
            P(("gx", "gy", "gz"), None),
            P(None, ("gx", "gy", "gz")),
            P(None, ("gx", "gy", "gz")),
            P(("gx", "gy", "gz")),
            P(),
            P(),
            P(),
        ),
        out_specs=(P(None, "gx", "gy", "gz"), P(None, None, ("gx", "gy", "gz"))),
        check_vma=False,
    )
```

```python
import functools

import jax
import jax.numpy as jnp
from jax import lax
from jax.experimental import pallas as pl
from jax.experimental.pallas import tpu as pltpu
from jax.sharding import PartitionSpec as P

STENCIL = 8
DROP_STEPS = 4
GAS_STEPS = 2
LANES = 128
MIB = 1 << 20
NT = (((1,), (1,)), ((), ()))
HIGH = lax.Precision.HIGHEST
F32 = jnp.float32
BF16 = jnp.bfloat16


def iota(shape, dim):
    return lax.broadcasted_iota(jnp.int32, shape, dim)


def as_column(row):
    n = row.shape[1]
    return jnp.sum(jnp.where(iota((n, n), 0) == iota((n, n), 1), row, 0.0), axis=1, keepdims=True)


def leading(value):
    scaled = value * 65537.0
    return scaled - (scaled - value)


def split(value):
    high = leading(value)
    return high.astype(BF16), (value - high).astype(BF16)


def split_all(value):
    high = leading(value)
    rest = value - high
    middle = leading(rest)
    return high.astype(BF16), middle.astype(BF16), (rest - middle).astype(BF16)


def one_hot(hit):
    return jnp.where(hit, 1.0, 0.0).astype(BF16)


def surface_steps(nodes, gas_at, liquid, surface):
    emitted = None
    for step in range(DROP_STEPS):
        last = nodes[-1]
        flux = surface * (last - gas_at)
        emitted = flux if emitted is None else emitted + flux
        inner = [
            nodes[i] + liquid * (nodes[i + 1] - 2.0 * nodes[i] + nodes[i - 1])
            for i in range(1, len(nodes) - 1)
        ]
        if len(nodes) > 1:
            nodes = inner + [last + liquid * (nodes[-2] - last) - flux]
    return emitted


def surface_response(liquid, surface):
    return surface_steps([jnp.zeros_like(liquid)] * DROP_STEPS, 1.0, liquid, surface)


def pack_kernel(cap, size_x, size_y, turns_x, droplet, gas, *refs):
    sources, (send, slots, near_gas), refs = refs[:6], refs[6:9], refs[9:]
    x_sends, refs = refs[: 2 * turns_x], refs[2 * turns_x :]
    (owner, cells, weights, mass, liquid, surface), (tail, sems) = refs[:6], refs[6:]
    parcels = owner.shape[1]
    nodes, species = droplet.shape[0], droplet.shape[1]
    lines = gas.shape[1]
    pairs = list(zip(sources, refs[:6], strict=True))
    pairs.append((droplet.at[pl.ds(nodes - DROP_STEPS, DROP_STEPS)], tail))
    small = len(pairs)
    pairs += [(gas.at[:, line, :], near_gas.at[line]) for line in range(lines)]
    loads = [pltpu.make_async_copy(source, here, sems.at[i]) for i, (source, here) in enumerate(pairs)]
    for load in loads:
        load.start()
    for load in loads[: small - 1]:
        load.wait()
    wts = weights[...]
    norm = wts / jnp.sum(wts, axis=0, keepdims=True)
    mine = owner[...]
    column = jnp.transpose(jnp.broadcast_to(mine.astype(F32), (parcels, parcels)))
    earlier = (column == mine.astype(F32)) & (iota((parcels, parcels), 0) < iota((parcels, parcels), 1))
    rank = jnp.sum(jnp.where(earlier, 1.0, 0.0), axis=0, keepdims=True).astype(jnp.int32)
    slot = mine * cap + rank
    slots[...] = slot
    place = one_hot(iota((send.shape[0], parcels), 0) == slot)
    rest = jnp.zeros((LANES - species - 2 * STENCIL - 8, parcels), F32)
    liquid_col, surface_col = as_column(liquid[...]), as_column(surface[...])
    loads[small - 1].wait()
    emitted = surface_steps([tail[i] for i in range(DROP_STEPS)], 0.0, liquid_col, surface_col)
    values = jnp.concatenate(
        [
            mass[...] * emitted,
            cells[...].astype(F32),
            norm,
            jnp.broadcast_to(mass[...], (8, parcels)),
            rest,
        ],
        axis=0,
    )
    for load in loads[small:]:
        load.wait()
    even_x, _, _ = place_on("gx")
    for turn in range(turns_x):
        up = even_x == (turn == 0)
        near = jnp.where(up, size_x - 1, 0) * size_y
        far = jnp.where(up, size_x - 2, 1) * size_y
        for y in range(size_y):
            x_sends[turn][y] = near_gas[near + y]
            x_sends[turns_x + turn][y] = near_gas[far + y]
    parts = jnp.concatenate(split_all(values), axis=0)
    placed = lax.dot_general(place, parts, NT, preferred_element_type=F32)
    send[...] = placed[:, :LANES] + placed[:, LANES : 2 * LANES] + placed[:, 2 * LANES :]


def y_faces_kernel(size_x, size_y, near_gas, ya, yb):
    even_y, _, _ = place_on("gy")
    for turn, y_send in enumerate((ya, yb)):
        up = even_y == (turn == 0)
        near = jnp.where(up, size_y - 1, 0)
        far = jnp.where(up, size_y - 2, 1)
        for x in range(size_x):
            y_send[x] = near_gas[x * size_y + near]
            y_send[size_x + x] = near_gas[x * size_y + far]


def corner_kernel(size_x, ya, yb, *sends):
    even_x, _, _ = place_on("gx")
    even_y, below_y, above_y = place_on("gy")
    for turn, send in enumerate(sends):
        x = jnp.where(even_x == (turn == 0), size_x - 1, 0)
        send[0], send[1] = low_high(even_y, ya[x], second_round(even_y, below_y, above_y, yb[x]))


def couple_kernel(cap, packed, rows, gas, liquid, surface, back, deposit, w_high, w_low):
    slots = rows.shape[0]
    species = liquid.shape[1]
    lines = gas.shape[0]
    table = jnp.transpose(rows[...])
    first = species
    cell = table[first : first + STENCIL]
    wts = table[first + STENCIL : first + 2 * STENCIL]
    mass = table[first + 2 * STENCIL : first + 2 * STENCIL + 1]
    whole = wts
    for shift in range(1, STENCIL):
        same = cell == pltpu.roll(cell, shift, 0)
        whole = whole + jnp.where(same, pltpu.roll(wts, shift, 0), 0.0)
    tile = 16
    cell = cell.astype(jnp.int32)
    high_rows, low_rows = split(whole)
    named = [jnp.broadcast_to(cell[k : k + 1], (tile, slots)).astype(jnp.int16) for k in range(STENCIL)]
    highs = [jnp.broadcast_to(high_rows[k : k + 1], (tile, slots)) for k in range(STENCIL)]
    lows = [jnp.broadcast_to(low_rows[k : k + 1], (tile, slots)) for k in range(STENCIL)]

    def pair(ref, line):
        return ref[line : line + 2].reshape(2 * LANES, slots)

    gathered = jnp.zeros((species, slots), F32)
    for line in range(0, lines, 2):
        for part in range(2):
            for z in range(0, LANES, tile):
                along = (iota((tile, slots), 0) + ((line + part) * LANES + z)).astype(jnp.int16)
                high = jnp.zeros((tile, slots), BF16)
                low = jnp.zeros((tile, slots), BF16)
                for k in range(STENCIL):
                    hit = named[k] == along
                    high = jnp.where(hit, highs[k], high)
                    low = jnp.where(hit, lows[k], low)
                w_high[line + part, z : z + tile] = high
                w_low[line + part, z : z + tile] = low
        t_high, t_low = split(jnp.concatenate([gas[line], gas[line + 1]], axis=1))
        t_all = jnp.concatenate([t_high, t_low], axis=0)
        both = jnp.dot(t_all, pair(w_high, line), preferred_element_type=F32)
        extra = jnp.dot(t_high, pair(w_low, line), preferred_element_type=F32)
        gathered = gathered + both[:species] + both[species:] + extra
    gas_rows = jnp.transpose(gathered)
    if packed:
        gas_rows = gas_rows.reshape(slots // cap, cap, species)
        gas_rows = jnp.concatenate([gas_rows[:, : cap // 2], gas_rows[:, cap // 2 :]], axis=2)
        back[...] = gas_rows.reshape(slots // 2, 2 * species)
    else:
        back[...] = jnp.concatenate([gas_rows, jnp.zeros((slots, LANES - species), F32)], axis=1)
    response = surface_response(as_column(liquid[...]), as_column(surface[...]))
    s_high, s_low = split(table[:species] + mass * (response * gathered))
    s_all = jnp.concatenate([s_high, s_low], axis=0)
    s_only = jnp.concatenate([s_high, jnp.zeros_like(s_low)], axis=0)
    for line in range(0, lines, 2):
        both = lax.dot_general(pair(w_high, line), s_all, NT, preferred_element_type=F32)
        both = both + lax.dot_general(pair(w_low, line), s_only, NT, preferred_element_type=F32)
        for i in range(2):
            turned = jnp.transpose(both[i * LANES : (i + 1) * LANES])
            deposit[line + i] = turned[:species] + turned[species:]


def droplet_kernel(
    cap, packed, state_in, rows, slots, liquid, surface, _, state_out, state_next, gas_at, sems
):
    nodes, species, parcels = state_in.shape
    block = 8

    table = jnp.transpose(rows[...])
    count = rows.shape[0]
    at = iota((count, parcels), 0)
    slot = slots[...]
    if packed:
        half = cap // 2
        at = at // half * cap + at % half
        pairs = [(table[:species], at), (table[species:], at + half)]
    else:
        pairs = [(table[:species], at)]
    total = jnp.zeros((species, parcels), F32)
    for values, index in pairs:
        parts = jnp.concatenate(split_all(values), axis=0)
        placed = jnp.dot(parts, one_hot(index == slot), preferred_element_type=F32)
        total = total + placed[:species] + placed[species : 2 * species] + placed[2 * species :]
    gas_at[...] = total

    def save(i):
        at = pl.ds(i * block, block)
        return pltpu.make_async_copy(state_next.at[:, at], state_out.at[:, at], sems.at[i])

    @pl.loop(0, species // block, unroll=4)
    def _(i):
        at = pl.ds(pl.multiple_of(i * block, block), block)
        pick = i * block + iota((block, species), 0) == iota((block, species), 1)
        liquid_col = jnp.sum(jnp.where(pick, liquid[...], 0.0), axis=1, keepdims=True)
        surface_col = jnp.sum(jnp.where(pick, surface[...], 0.0), axis=1, keepdims=True)
        rate = jnp.broadcast_to(liquid_col, (block, parcels))
        keep = 1.0 - 2.0 * rate
        last_keep = jnp.broadcast_to(1.0 - liquid_col - surface_col, (block, parcels))
        from_gas = surface_col * gas_at[at, :]
        state = [state_in[node, at] for node in range(nodes)]
        for step in range(DROP_STEPS):
            state = (
                [keep * state[0] + (rate + rate) * state[1]]
                + [keep * state[n] + rate * (state[n - 1] + state[n + 1]) for n in range(1, nodes - 1)]
                + [last_keep * state[-1] + rate * state[-2] + from_gas]
            )
        for node in range(nodes):
            state_next[node, at] = state[node]
        save(i).start()

    for i in range(species // block):
        save(i).wait()


def place_on(axis):
    index, count = lax.axis_index(axis), lax.axis_size(axis)
    even = lax.rem(index, 2) == 0
    below = jnp.where(index > 0, 1.0, 0.0).astype(F32)
    above = jnp.where(index < count - 1, 1.0, 0.0).astype(F32)
    return even, below, above


def swaps(axis, closed=False, spare=None):
    count = lax.axis_size(axis)
    across = 1 if spare is None else lax.axis_size(spare)
    rounds = []
    for first in range(2):
        pairs = [(i * across + j, (i + 1) * across + j) for i in range(first, count - 1, 2) for j in range(across)]
        if closed and first == 1 and count > 2 and count % 2 == 0:
            if spare is None:
                pairs.append((count - 1, 0))
            elif across % 2 == 0:
                pairs += [(i * across + j, i * across + j + 1) for i in (0, count - 1) for j in range(0, across, 2)]
        if pairs:
            rounds.append(pairs + [(j, i) for i, j in pairs])
    return rounds


def swap_all(messages, axis, closed=False, spare=None):
    axes = axis if spare is None else (axis, spare)
    return [lax.ppermute(m, axes, pairs) for m, pairs in zip(messages, swaps(axis, closed, spare), strict=True)]


def second_round(even, below, above, block):
    return jnp.where(jnp.where(even, below, above) > 0.0, block, 0.0)


def low_high(even, first, second):
    if second is None:
        second = jnp.zeros_like(first)
    return jnp.where(even, second, first), jnp.where(even, first, second)


def beside_z(block):
    axis = block.ndim - 1
    lane = iota(block.shape, axis)
    before = jnp.where(lane == 0, 0.0, pltpu.roll(block, 1, axis))
    after = jnp.where(lane == LANES - 1, 0.0, pltpu.roll(block, LANES - 1, axis))
    return before + after


def beside_xy(planes, x, y, x_low, x_high, y_low, y_high):
    size_x, size_y = len(planes), len(planes[0])
    total = planes[x - 1][y]() if x > 0 else x_low(y)
    total = total + (planes[x + 1][y]() if x < size_x - 1 else x_high(y))
    total = total + (planes[x][y - 1]() if y > 0 else y_low(x))
    return total + (planes[x][y + 1]() if y < size_y - 1 else y_high(x))


def plane_at(ref, index):
    return lambda: ref[index]


def wide_rates(rate, rows):
    column = as_column(rate[...])
    column = jnp.concatenate([column] * (rows // column.shape[0]), axis=0)
    return jnp.broadcast_to(column, (rows, LANES))


def beside_in_rows(size_x, size_y, main, x_low, x_high, y_low, y_high):
    count = main.shape[0]
    each = size_x * size_y // count
    species = LANES // each
    rows_x = size_y // each
    row, lane = iota((count, LANES), 0), iota((count, LANES), 1)
    first_place = (lane < species) & (row % rows_x == 0)
    last_place = (lane >= LANES - species) & (row % rows_x == rows_x - 1)
    blank = jnp.zeros((rows_x - 1, LANES), F32)
    low_rows, high_rows = [], []
    for x in range(size_x):
        i, part = x // each, x % each
        low_row, high_row = y_low[i : i + 1], y_high[i : i + 1]
        if part > 0:
            low_row = pltpu.roll(low_row, LANES - part * species, 1)
        if part < each - 1:
            high_row = pltpu.roll(high_row, (each - 1 - part) * species, 1)
        low_rows += [low_row, blank]
        high_rows += [blank, high_row]
    ahead = pltpu.roll(main, LANES - species, 1)
    after = jnp.where(lane >= LANES - species, jnp.concatenate([ahead[1:], ahead[-1:]], axis=0), ahead)
    after = jnp.where(last_place, jnp.concatenate(high_rows, axis=0), after)
    behind = pltpu.roll(main, species, 1)
    before = jnp.where(lane < species, jnp.concatenate([behind[:1], behind[:-1]], axis=0), behind)
    before = jnp.where(first_place, jnp.concatenate(low_rows, axis=0), before)
    total = before + after + jnp.concatenate([x_low, main[:-rows_x]], axis=0)
    return total + jnp.concatenate([main[rows_x:], x_high], axis=0)


def z_message_kernel(size_x, size_y, turns_x, gas, *refs):
    xs, (ya, yb, rate, za, zb) = refs[:turns_x], refs[turns_x:]
    species = rate.shape[1]
    lines = size_x * size_y
    each = LANES // species
    rates = jnp.concatenate([rate[...]] * each, axis=1)
    keep = 1.0 - 6.0 * rates
    even_x, _, _ = place_on("gx")
    even_y, below_y, above_y = place_on("gy")
    even_z, _, _ = place_on("gz")

    def columns(ref):
        turned = [jnp.transpose(ref[i : i + each].reshape(LANES, LANES)) for i in range(0, ref.shape[0], each)]
        return [jnp.concatenate([t[z : z + 1] for t in turned], axis=0) for z in (0, 1, LANES - 1, LANES - 2)]

    main = columns(gas)
    x_sides = [columns(x) for x in xs]
    y_sides = [columns(y.at[:size_x]) for y in (ya, yb)]
    messages = []
    for side in range(2):
        own, inner = main[2 * side], main[2 * side + 1]
        from_x = [columns_of_x[2 * side] for columns_of_x in x_sides]
        from_y = [columns_of_y[2 * side] for columns_of_y in y_sides]
        x_low, x_high = low_high(even_x, from_x[0], from_x[1] if turns_x == 2 else None)
        y_low, y_high = low_high(even_y, from_y[0], second_round(even_y, below_y, above_y, from_y[1]))
        total = inner + beside_in_rows(size_x, size_y, own, x_low, x_high, y_low, y_high)
        parts = [own, keep * own + rates * total] + from_x + from_y
        filled = sum(part.shape[0] for part in parts)
        parts.append(jnp.zeros((za.shape[0] - filled, LANES), F32))
        messages.append(jnp.concatenate(parts, axis=0))
    low, high = messages
    za[...] = jnp.where(even_z, high, low)
    zb[...] = jnp.where(even_z, low, high)


def steps_kernel(size_x, size_y, turns_x, gas, *refs):
    xs, refs = refs[:turns_x], refs[turns_x:]
    xs_far, refs = refs[:turns_x], refs[turns_x:]
    ya, yb, rate, deposit, out, field, side_x, side_y = refs
    species = rate.shape[1]
    lines = size_x * size_y
    even_x, below_x, above_x = place_on("gx")
    even_y, below_y, above_y = place_on("gy")
    wide = wide_rates(rate, species)
    keep = 1.0 - 6.0 * wide

    def step(source, x_halos, y_halos, store):
        planes = [[plane_at(source, x * size_y + y) for y in range(size_y)] for x in range(size_x)]

        def from_x(side, y):
            return low_high(even_x, x_halos[0][y], x_halos[1][y] if turns_x == 2 else None)[side]

        def from_y(side, x):
            return low_high(even_y, y_halos[0][x], second_round(even_y, below_y, above_y, y_halos[1][x]))[side]

        for x in range(size_x):
            for y in range(size_y):
                own = source[x * size_y + y]
                total = beside_xy(
                    planes,
                    x,
                    y,
                    functools.partial(from_x, 0),
                    functools.partial(from_x, 1),
                    functools.partial(from_y, 0),
                    functools.partial(from_y, 1),
                )
                store(x * size_y + y, keep * own + wide * (total + beside_z(own)))

    def store_field(line, value):
        field[line] = value

    step(gas, xs, (ya, yb), store_field)
    for turn, ref in enumerate(xs):
        up = even_x == (turn == 0)
        exists = jnp.where(up, above_x, below_x)
        inner = jnp.where(up, lines - size_y, 0)
        for y in range(size_y):
            own = ref[y]
            total = xs_far[turn][y] + exists * gas[inner + y]
            if y > 0:
                total = total + ref[y - 1]
            if y < size_y - 1:
                total = total + ref[y + 1]
            side_x[turn, y] = keep * own + wide * (total + beside_z(own))

    for turn, ref in enumerate((ya, yb)):
        up = even_y == (turn == 0)
        exists = jnp.where(up, above_y, below_y)
        inner = jnp.where(up, size_y - 1, 0)
        for x in range(size_x):
            own = ref[x]
            total = ref[size_x + x] + exists * gas[x * size_y + inner]
            if x > 0:
                total = total + ref[x - 1]
            if x < size_x - 1:
                total = total + ref[x + 1]
            side_y[turn, x] = keep * own + wide * (total + beside_z(own))

    def store_result(line, value):
        out[line] = value + deposit[line]

    step(field, [side_x.at[turn] for turn in range(turns_x)], [side_y.at[turn] for turn in range(2)], store_result)


def close_kernel(size_x, size_y, turns_x, partial, *refs):
    corners, (za, zb, za_in, zb_in, rate, out, result, sems) = refs[:turns_x], refs[turns_x:]
    species = rate.shape[1]
    lines = size_x * size_y
    each = LANES // species
    count, rows_x, rows_y = lines // each, size_y // each, size_x // each
    even_x, _, _ = place_on("gx")
    even_y, below_y, above_y = place_on("gy")
    even, below, above = place_on("gz")
    rates = jnp.concatenate([rate[...]] * each, axis=1)
    keep = 1.0 - 6.0 * rates
    incoming = low_high(even, za_in[...], zb_in[...])
    leaving = low_high(even, za[...], zb[...])
    outer, inner = [], []
    for column, own, exists in zip(incoming, leaving, (below, above), strict=True):
        column = rates * jnp.where(exists > 0.0, column, 0.0)
        main, partly = column[:count], column[count : 2 * count]
        at = 2 * count
        sides = [column[at + i * rows_x : at + (i + 1) * rows_x] for i in range(turns_x)]
        x_low, x_high = low_high(even_x, sides[0], sides[1] if turns_x == 2 else None)
        at = at + turns_x * rows_x
        sides = [column[at + i * rows_y : at + (i + 1) * rows_y] for i in range(2)]
        y_low, y_high = low_high(even_y, sides[0], second_round(even_y, below_y, above_y, sides[1]))
        total = beside_in_rows(size_x, size_y, main, x_low, x_high, y_low, y_high)
        outer.append(keep * main + rates * total + partly + exists * rates * rates * own[:count])
        inner.append(rates * main)

    wide = wide_rates(rate, species)
    twice = 2.0 * wide * wide
    edge = {}
    for i, y in enumerate((0, size_y - 1)):
        planes = low_high(even_x, corners[0][i], corners[1][i] if turns_x == 2 else None)
        edge[y], edge[lines - size_y + y] = planes
    turned = iota((LANES, LANES), 0)
    saves = []
    for i in range(count):
        at = slice(i, i + 1)
        block = jnp.where(turned == 0, outer[0][at], jnp.where(turned == 1, inner[0][at], 0.0))
        block = jnp.where(turned == LANES - 2, inner[1][at], block)
        block = jnp.transpose(jnp.where(turned == LANES - 1, outer[1][at], block))
        for part in range(each):
            line = i * each + part
            total = partial[line] + block[part * species : (part + 1) * species]
            if line in edge:
                total = total + twice * edge[line]
            result[line] = total
            saves.append(pltpu.make_async_copy(result.at[line], out.at[:, line, :], sems.at[line]))
            saves[-1].start()
    for save in saves:
        save.wait()


def full(shape):
    return pl.BlockSpec(shape, lambda *_: (0,) * len(shape))


def lasts(microseconds):
    return pl.CostEstimate(flops=0, bytes_accessed=int(3.69e6 * microseconds), transcendentals=0)


def in_hbm(array):
    return pltpu.with_memory_space_constraint(array, pltpu.HBM)


def in_vmem(array):
    return pltpu.with_memory_space_constraint(array, pltpu.VMEM)


def exchange(rows, group):
    width = rows.shape[1]
    chunks = rows.reshape(group, -1, width)
    chunks = lax.all_to_all(chunks, ("gy", "gz"), split_axis=0, concat_axis=0, tiled=True)
    return chunks.reshape(-1, width)


def on_device(gas, droplet, owner, cells, weights, mass, liquid_rate, surface_rate, gas_rate):
    group = lax.axis_size("gy") * lax.axis_size("gz")
    nodes, species, parcels = droplet.shape
    cap = 2 * parcels // group
    slots = group * cap
    packed = cap % 16 == 0
    lines = gas.shape[1] * gas.shape[2]
    flat = gas.reshape(species, lines, LANES)
    planes = (lines, species, LANES)
    liquid = liquid_rate.reshape(1, species)
    surface = surface_rate.reshape(1, species)
    rate_spec = full((1, species))
    size_x, size_y = gas.shape[1], gas.shape[2]
    rate = gas_rate.reshape(1, species)
    vmem = pl.BlockSpec(memory_space=pltpu.VMEM)
    hbm = pl.BlockSpec(memory_space=pl.ANY)
    whole = pl.BlockSpec()
    turns_x = len(swaps("gx"))
    x_shape = (size_y, species, LANES)
    y_shape = (2 * size_x, species, LANES)

    send, slot, near_gas, *x_faces = pl.pallas_call(
        functools.partial(pack_kernel, cap, size_x, size_y, turns_x),
        out_shape=[
            pltpu.VMEM((slots, LANES), F32),
            pltpu.VMEM((1, parcels), jnp.int32),
            pltpu.VMEM(planes, F32),
        ]
        + [pltpu.VMEM(x_shape, F32)] * (2 * turns_x),
        in_specs=[hbm] * 8,
        out_specs=[vmem] * (3 + 2 * turns_x),
        scratch_shapes=[
            pltpu.VMEM((1, parcels), jnp.int32),
            pltpu.VMEM((STENCIL, parcels), jnp.int32),
            pltpu.VMEM((STENCIL, parcels), F32),
            pltpu.VMEM((1, parcels), F32),
            pltpu.VMEM((1, species), F32),
            pltpu.VMEM((1, species), F32),
            pltpu.VMEM((DROP_STEPS, species, parcels), F32),
            pltpu.SemaphoreType.DMA((7 + lines,)),
        ],
        compiler_params=pltpu.CompilerParams(vmem_limit_bytes=8 * MIB),
        cost_estimate=lasts(2.5),
        name="pack",
    )(
        in_hbm(droplet),
        in_hbm(flat),
        in_hbm(owner.reshape(1, parcels)),
        in_hbm(cells),
        in_hbm(weights),
        in_hbm(mass.reshape(1, parcels)),
        in_hbm(liquid),
        in_hbm(surface),
    )
    rows = exchange(send, group)

    y_faces = pl.pallas_call(
        functools.partial(y_faces_kernel, size_x, size_y),
        out_shape=[pltpu.VMEM(y_shape, F32)] * 2,
        in_specs=[vmem],
        out_specs=[vmem] * 2,
        compiler_params=pltpu.CompilerParams(vmem_limit_bytes=4 * MIB),
        cost_estimate=lasts(0.6),
        name="y_faces",
    )(near_gas)
    y_halo = swap_all(y_faces, "gy", closed=True, spare="gz")
    x_near = swap_all(x_faces[:turns_x], "gx")
    x_far = swap_all(x_faces[turns_x:], "gx")

    corners = pl.pallas_call(
        functools.partial(corner_kernel, size_x),
        out_shape=[jax.ShapeDtypeStruct((2, species, LANES), F32)] * turns_x,
        in_specs=[vmem] * 2,
        out_specs=[vmem] * turns_x,
        compiler_params=pltpu.CompilerParams(vmem_limit_bytes=4 * MIB),
        cost_estimate=lasts(0.3),
        name="corner_planes",
    )(*y_halo)
    corners = swap_all(corners, "gx")

    back_rows = slots // 2 if packed else slots
    w_shape = (lines, LANES, slots)
    back, deposit = pl.pallas_call(
        functools.partial(couple_kernel, cap, packed),
        out_shape=[pltpu.VMEM((back_rows, LANES), F32), pltpu.VMEM(planes, F32)],
        in_specs=[vmem] * 2 + [whole] * 2,
        out_specs=[vmem, vmem],
        scratch_shapes=[
            pltpu.VMEM(w_shape, BF16),
            pltpu.VMEM(w_shape, BF16),
        ],
        compiler_params=pltpu.CompilerParams(vmem_limit_bytes=10 * MIB),
        cost_estimate=lasts(7.0),
        name="couple_gas",
    )(rows, near_gas, liquid, surface)

    returned = exchange(back, group)

    z_shape = (48, LANES)
    x_near, x_far, y_halo = [[in_vmem(halo) for halo in halos] for halos in (x_near, x_far, y_halo)]
    z_sends = pl.pallas_call(
        functools.partial(z_message_kernel, size_x, size_y, turns_x),
        out_shape=[jax.ShapeDtypeStruct(z_shape, F32)] * 2,
        in_specs=[vmem] * (turns_x + 3) + [whole],
        compiler_params=pltpu.CompilerParams(vmem_limit_bytes=4 * MIB),
        cost_estimate=lasts(0.6),
        name="z_message",
    )(near_gas, *x_near, *y_halo, rate)
    z_halo = swap_all(z_sends, "gz", closed=True)
    partial = pl.pallas_call(
        functools.partial(steps_kernel, size_x, size_y, turns_x),
        out_shape=pltpu.VMEM(planes, F32),
        in_specs=[vmem] * (2 * turns_x + 3) + [whole, vmem],
        out_specs=vmem,
        scratch_shapes=[
            pltpu.VMEM(planes, F32),
            pltpu.VMEM((turns_x, size_y, species, LANES), F32),
            pltpu.VMEM((2, size_x, species, LANES), F32),
        ],
        compiler_params=pltpu.CompilerParams(vmem_limit_bytes=6 * MIB),
        cost_estimate=lasts(2.2),
        name="gas_steps",
    )(near_gas, *x_near, *x_far, *y_halo, rate, in_vmem(deposit))
    gas_next = pl.pallas_call(
        functools.partial(close_kernel, size_x, size_y, turns_x),
        out_shape=jax.ShapeDtypeStruct(flat.shape, F32),
        in_specs=[vmem] * (1 + turns_x) + [whole] * 5,
        out_specs=hbm,
        scratch_shapes=[pltpu.VMEM(planes, F32), pltpu.SemaphoreType.DMA((lines,))],
        compiler_params=pltpu.CompilerParams(vmem_limit_bytes=6 * MIB),
        cost_estimate=lasts(1.5),
        name="close_gas_step",
    )(in_vmem(partial), *corners, *z_sends, *z_halo, rate)
    droplet_next = pl.pallas_call(
        functools.partial(droplet_kernel, cap, packed),
        out_shape=jax.ShapeDtypeStruct(droplet.shape, F32),
        in_specs=[whole] * 5 + [hbm],
        out_specs=hbm,
        scratch_shapes=[
            pltpu.VMEM(droplet.shape, F32),
            pltpu.VMEM((species, parcels), F32),
            pltpu.SemaphoreType.DMA((species // 8,)),
        ],
        compiler_params=pltpu.CompilerParams(vmem_limit_bytes=8 * MIB),
        cost_estimate=lasts(2.5),
        name="droplets",
    )(droplet, returned, slot, liquid, surface, in_hbm(gas_next))
    return (gas_next.reshape(gas.shape), droplet_next)


def solution(mesh):
    return jax.shard_map(
        on_device,
        mesh=mesh,
        in_specs=(
            P(None, "gx", "gy", "gz"),
            P(None, None, ("gx", "gy", "gz")),
            P(("gx", "gy", "gz"), None),
            P(None, ("gx", "gy", "gz")),
            P(None, ("gx", "gy", "gz")),
            P(("gx", "gy", "gz")),
            P(),
            P(),
            P(),
        ),
        out_specs=(P(None, "gx", "gy", "gz"), P(None, None, ("gx", "gy", "gz"))),
        check_vma=False,
    )
```

```python
import functools

import jax
import jax.numpy as jnp
from jax import lax
from jax.experimental import pallas as pl
from jax.experimental.pallas import tpu as pltpu
from jax.sharding import PartitionSpec as P

STENCIL = 8
DROP_STEPS = 4
GAS_STEPS = 2
LANES = 128
MIB = 1 << 20
NT = (((1,), (1,)), ((), ()))
HIGH = lax.Precision.HIGHEST
F32 = jnp.float32
BF16 = jnp.bfloat16


def iota(shape, dim):
    return lax.broadcasted_iota(jnp.int32, shape, dim)


def as_column(row):
    n = row.shape[1]
    return jnp.sum(jnp.where(iota((n, n), 0) == iota((n, n), 1), row, 0.0), axis=1, keepdims=True)


def leading(value):
    scaled = value * 65537.0
    return scaled - (scaled - value)


def split(value):
    high = leading(value)
    return high.astype(BF16), (value - high).astype(BF16)


def split_all(value):
    high = leading(value)
    rest = value - high
    middle = leading(rest)
    return high.astype(BF16), middle.astype(BF16), (rest - middle).astype(BF16)


def one_hot(hit):
    return jnp.where(hit, 1.0, 0.0).astype(BF16)


def surface_steps(nodes, gas_at, liquid, surface):
    emitted = None
    for step in range(DROP_STEPS):
        last = nodes[-1]
        flux = surface * (last - gas_at)
        emitted = flux if emitted is None else emitted + flux
        inner = [
            nodes[i] + liquid * (nodes[i + 1] - 2.0 * nodes[i] + nodes[i - 1])
            for i in range(1, len(nodes) - 1)
        ]
        if len(nodes) > 1:
            nodes = inner + [last + liquid * (nodes[-2] - last) - flux]
    return emitted


def surface_response(liquid, surface):
    return surface_steps([jnp.zeros_like(liquid)] * DROP_STEPS, 1.0, liquid, surface)


def pack_kernel(cap, size_x, size_y, turns_x, droplet, gas, *refs):
    sources, (send, slots, near_gas), refs = refs[:6], refs[6:9], refs[9:]
    x_sends, refs = refs[: 2 * turns_x], refs[2 * turns_x :]
    (owner, cells, weights, mass, liquid, surface), (tail, sems) = refs[:6], refs[6:]
    parcels = owner.shape[1]
    nodes, species = droplet.shape[0], droplet.shape[1]
    lines = gas.shape[1]
    pairs = list(zip(sources, refs[:6], strict=True))
    pairs.append((droplet.at[pl.ds(nodes - DROP_STEPS, DROP_STEPS)], tail))
    small = len(pairs)
    pairs += [(gas.at[:, line, :], near_gas.at[line]) for line in range(lines)]
    loads = [pltpu.make_async_copy(source, here, sems.at[i]) for i, (source, here) in enumerate(pairs)]
    for load in loads:
        load.start()
    for load in loads[: small - 1]:
        load.wait()
    wts = weights[...]
    norm = wts / jnp.sum(wts, axis=0, keepdims=True)
    mine = owner[...]
    column = jnp.transpose(jnp.broadcast_to(mine.astype(F32), (parcels, parcels)))
    earlier = (column == mine.astype(F32)) & (iota((parcels, parcels), 0) < iota((parcels, parcels), 1))
    rank = jnp.sum(jnp.where(earlier, 1.0, 0.0), axis=0, keepdims=True).astype(jnp.int32)
    slot = mine * cap + rank
    slots[...] = slot
    place = one_hot(iota((send.shape[0], parcels), 0) == slot)
    rest = jnp.zeros((LANES - species - 2 * STENCIL - 8, parcels), F32)
    liquid_col, surface_col = as_column(liquid[...]), as_column(surface[...])
    loads[small - 1].wait()
    emitted = surface_steps([tail[i] for i in range(DROP_STEPS)], 0.0, liquid_col, surface_col)
    values = jnp.concatenate(
        [
            mass[...] * emitted,
            cells[...].astype(F32),
            norm,
            jnp.broadcast_to(mass[...], (8, parcels)),
            rest,
        ],
        axis=0,
    )
    for load in loads[small:]:
        load.wait()
    even_x, _, _ = place_on("gx")
    for turn in range(turns_x):
        up = even_x == (turn == 0)
        near = jnp.where(up, size_x - 1, 0) * size_y
        far = jnp.where(up, size_x - 2, 1) * size_y
        for y in range(size_y):
            x_sends[turn][y] = near_gas[near + y]
            x_sends[turns_x + turn][y] = near_gas[far + y]
    parts = jnp.concatenate(split_all(values), axis=0)
    placed = lax.dot_general(place, parts, NT, preferred_element_type=F32)
    send[...] = placed[:, :LANES] + placed[:, LANES : 2 * LANES] + placed[:, 2 * LANES :]


def y_faces_kernel(size_x, size_y, near_gas, ya, yb):
    even_y, _, _ = place_on("gy")
    for turn, y_send in enumerate((ya, yb)):
        up = even_y == (turn == 0)
        near = jnp.where(up, size_y - 1, 0)
        far = jnp.where(up, size_y - 2, 1)
        for x in range(size_x):
            y_send[x] = near_gas[x * size_y + near]
            y_send[size_x + x] = near_gas[x * size_y + far]


def corner_kernel(size_x, ya, yb, *sends):
    even_x, _, _ = place_on("gx")
    even_y, below_y, above_y = place_on("gy")
    for turn, send in enumerate(sends):
        x = jnp.where(even_x == (turn == 0), size_x - 1, 0)
        send[0], send[1] = low_high(even_y, ya[x], second_round(even_y, below_y, above_y, yb[x]))


def couple_kernel(cap, packed, rows, gas, liquid, surface, back_out, deposit, w_high, w_low, back, sems):
    slots = rows.shape[0]
    species = liquid.shape[1]
    lines = gas.shape[0]
    table = jnp.transpose(rows[...])
    first = species
    cell = table[first : first + STENCIL]
    wts = table[first + STENCIL : first + 2 * STENCIL]
    mass = table[first + 2 * STENCIL : first + 2 * STENCIL + 1]
    whole = wts
    for shift in range(1, STENCIL):
        same = cell == pltpu.roll(cell, shift, 0)
        whole = whole + jnp.where(same, pltpu.roll(wts, shift, 0), 0.0)
    tile = 16
    cell = cell.astype(jnp.int32)
    high_rows, low_rows = split(whole)
    named = [jnp.broadcast_to(cell[k : k + 1], (tile, slots)).astype(jnp.int16) for k in range(STENCIL)]
    first_cells = iota((tile, slots), 0).astype(jnp.int16)
    highs = [jnp.broadcast_to(high_rows[k : k + 1], (tile, slots)) for k in range(STENCIL)]
    lows = [jnp.broadcast_to(low_rows[k : k + 1], (tile, slots)) for k in range(STENCIL)]

    def pair(ref, line):
        return ref[line : line + 2].reshape(2 * LANES, slots)

    gathered = jnp.zeros((species, slots), F32)
    for line in range(0, lines, 2):
        for part in range(2):
            for z in range(0, LANES, tile):
                along = first_cells + jnp.int16((line + part) * LANES + z)
                high = jnp.zeros((tile, slots), BF16)
                low = jnp.zeros((tile, slots), BF16)
                for k in range(STENCIL):
                    hit = named[k] == along
                    high = jnp.where(hit, highs[k], high)
                    low = jnp.where(hit, lows[k], low)
                w_high[line + part, z : z + tile] = high
                w_low[line + part, z : z + tile] = low
        t_high, t_low = split(jnp.concatenate([gas[line], gas[line + 1]], axis=1))
        t_all = jnp.concatenate([t_high, t_low], axis=0)
        both = jnp.dot(t_all, pair(w_high, line), preferred_element_type=F32)
        extra = jnp.dot(t_high, pair(w_low, line), preferred_element_type=F32)
        gathered = gathered + both[:species] + both[species:] + extra
    gas_rows = jnp.transpose(gathered)
    if packed:
        gas_rows = gas_rows.reshape(slots // cap, cap, species)
        gas_rows = jnp.concatenate([gas_rows[:, : cap // 2], gas_rows[:, cap // 2 :]], axis=2)
        back[...] = gas_rows.reshape(slots // 2, 2 * species)
    else:
        back[...] = jnp.concatenate([gas_rows, jnp.zeros((slots, LANES - species), F32)], axis=1)
    save = pltpu.make_async_copy(back, back_out, sems.at[0])
    save.start()
    response = surface_response(as_column(liquid[...]), as_column(surface[...]))
    s_high, s_low = split(table[:species] + mass * (response * gathered))
    s_all = jnp.concatenate([s_high, s_low], axis=0)
    s_only = jnp.concatenate([s_high, jnp.zeros_like(s_low)], axis=0)
    for line in range(0, lines, 2):
        both = lax.dot_general(pair(w_high, line), s_all, NT, preferred_element_type=F32)
        both = both + lax.dot_general(pair(w_low, line), s_only, NT, preferred_element_type=F32)
        for i in range(2):
            turned = jnp.transpose(both[i * LANES : (i + 1) * LANES])
            deposit[line + i] = turned[:species] + turned[species:]
    save.wait()


def droplet_kernel(
    cap, packed, state_in, rows, slots, liquid, surface, _, state_out, state_next, gas_at, sems
):
    nodes, species, parcels = state_in.shape
    block = 8

    table = jnp.transpose(rows[...])
    count = rows.shape[0]
    at = iota((count, parcels), 0)
    slot = slots[...]
    if packed:
        half = cap // 2
        at = at // half * cap + at % half
        pairs = [(table[:species], at), (table[species:], at + half)]
    else:
        pairs = [(table[:species], at)]
    total = jnp.zeros((species, parcels), F32)
    for values, index in pairs:
        parts = jnp.concatenate(split_all(values), axis=0)
        placed = jnp.dot(parts, one_hot(index == slot), preferred_element_type=F32)
        total = total + placed[:species] + placed[species : 2 * species] + placed[2 * species :]
    gas_at[...] = total

    def save(i):
        at = pl.ds(i * block, block)
        return pltpu.make_async_copy(state_next.at[:, at], state_out.at[:, at], sems.at[i])

    @pl.loop(0, species // block, unroll=8)
    def _(i):
        at = pl.ds(pl.multiple_of(i * block, block), block)
        pick = i * block + iota((block, species), 0) == iota((block, species), 1)
        liquid_col = jnp.sum(jnp.where(pick, liquid[...], 0.0), axis=1, keepdims=True)
        surface_col = jnp.sum(jnp.where(pick, surface[...], 0.0), axis=1, keepdims=True)
        rate = jnp.broadcast_to(liquid_col, (block, parcels))
        keep = 1.0 - 2.0 * rate
        last_keep = jnp.broadcast_to(1.0 - liquid_col - surface_col, (block, parcels))
        from_gas = surface_col * gas_at[at, :]
        state = [state_in[node, at] for node in range(nodes)]
        for step in range(DROP_STEPS):
            state = (
                [keep * state[0] + (rate + rate) * state[1]]
                + [keep * state[n] + rate * (state[n - 1] + state[n + 1]) for n in range(1, nodes - 1)]
                + [last_keep * state[-1] + rate * state[-2] + from_gas]
            )
        for node in range(nodes):
            state_next[node, at] = state[node]
        save(i).start()

    for i in range(species // block):
        save(i).wait()


def place_on(axis):
    index, count = lax.axis_index(axis), lax.axis_size(axis)
    even = lax.rem(index, 2) == 0
    below = jnp.where(index > 0, 1.0, 0.0).astype(F32)
    above = jnp.where(index < count - 1, 1.0, 0.0).astype(F32)
    return even, below, above


def swaps(axis, closed=False, spare=None):
    count = lax.axis_size(axis)
    across = 1 if spare is None else lax.axis_size(spare)
    rounds = []
    for first in range(2):
        pairs = [(i * across + j, (i + 1) * across + j) for i in range(first, count - 1, 2) for j in range(across)]
        if closed and first == 1 and count > 2 and count % 2 == 0:
            if spare is None:
                pairs.append((count - 1, 0))
            elif across % 2 == 0:
                pairs += [(i * across + j, i * across + j + 1) for i in (0, count - 1) for j in range(0, across, 2)]
        if pairs:
            rounds.append(pairs + [(j, i) for i, j in pairs])
    return rounds


def swap_all(messages, axis, closed=False, spare=None):
    axes = axis if spare is None else (axis, spare)
    return [lax.ppermute(m, axes, pairs) for m, pairs in zip(messages, swaps(axis, closed, spare), strict=True)]


def second_round(even, below, above, block):
    return jnp.where(jnp.where(even, below, above) > 0.0, block, 0.0)


def low_high(even, first, second):
    if second is None:
        second = jnp.zeros_like(first)
    return jnp.where(even, second, first), jnp.where(even, first, second)


def beside_z(block):
    axis = block.ndim - 1
    lane = iota(block.shape, axis)
    before = jnp.where(lane == 0, 0.0, pltpu.roll(block, 1, axis))
    after = jnp.where(lane == LANES - 1, 0.0, pltpu.roll(block, LANES - 1, axis))
    return before + after


def beside_xy(planes, x, y, x_low, x_high, y_low, y_high):
    size_x, size_y = len(planes), len(planes[0])
    total = planes[x - 1][y]() if x > 0 else x_low(y)
    total = total + (planes[x + 1][y]() if x < size_x - 1 else x_high(y))
    total = total + (planes[x][y - 1]() if y > 0 else y_low(x))
    return total + (planes[x][y + 1]() if y < size_y - 1 else y_high(x))


def plane_at(ref, index):
    return lambda: ref[index]


def wide_rates(rate, rows):
    column = as_column(rate[...])
    column = jnp.concatenate([column] * (rows // column.shape[0]), axis=0)
    return jnp.broadcast_to(column, (rows, LANES))


def beside_in_rows(size_x, size_y, main, x_low, x_high, y_low, y_high):
    count = main.shape[0]
    each = size_x * size_y // count
    species = LANES // each
    rows_x = size_y // each
    row, lane = iota((count, LANES), 0), iota((count, LANES), 1)
    first_place = (lane < species) & (row % rows_x == 0)
    last_place = (lane >= LANES - species) & (row % rows_x == rows_x - 1)
    blank = jnp.zeros((rows_x - 1, LANES), F32)
    low_rows, high_rows = [], []
    for x in range(size_x):
        i, part = x // each, x % each
        low_row, high_row = y_low[i : i + 1], y_high[i : i + 1]
        if part > 0:
            low_row = pltpu.roll(low_row, LANES - part * species, 1)
        if part < each - 1:
            high_row = pltpu.roll(high_row, (each - 1 - part) * species, 1)
        low_rows += [low_row, blank]
        high_rows += [blank, high_row]
    ahead = pltpu.roll(main, LANES - species, 1)
    after = jnp.where(lane >= LANES - species, jnp.concatenate([ahead[1:], ahead[-1:]], axis=0), ahead)
    after = jnp.where(last_place, jnp.concatenate(high_rows, axis=0), after)
    behind = pltpu.roll(main, species, 1)
    before = jnp.where(lane < species, jnp.concatenate([behind[:1], behind[:-1]], axis=0), behind)
    before = jnp.where(first_place, jnp.concatenate(low_rows, axis=0), before)
    total = before + after + jnp.concatenate([x_low, main[:-rows_x]], axis=0)
    return total + jnp.concatenate([main[rows_x:], x_high], axis=0)


def z_message_kernel(size_x, size_y, turns_x, gas, *refs):
    xs, (ya, yb, rate, za, zb) = refs[:turns_x], refs[turns_x:]
    species = rate.shape[1]
    lines = size_x * size_y
    each = LANES // species
    rates = jnp.concatenate([rate[...]] * each, axis=1)
    keep = 1.0 - 6.0 * rates
    even_x, _, _ = place_on("gx")
    even_y, below_y, above_y = place_on("gy")
    even_z, _, _ = place_on("gz")

    def columns(ref):
        turned = [jnp.transpose(ref[i : i + each].reshape(LANES, LANES)) for i in range(0, ref.shape[0], each)]
        return [jnp.concatenate([t[z : z + 1] for t in turned], axis=0) for z in (0, 1, LANES - 1, LANES - 2)]

    main = columns(gas)
    x_sides = [columns(x) for x in xs]
    y_sides = [columns(y.at[:size_x]) for y in (ya, yb)]
    messages = []
    for side in range(2):
        own, inner = main[2 * side], main[2 * side + 1]
        from_x = [columns_of_x[2 * side] for columns_of_x in x_sides]
        from_y = [columns_of_y[2 * side] for columns_of_y in y_sides]
        x_low, x_high = low_high(even_x, from_x[0], from_x[1] if turns_x == 2 else None)
        y_low, y_high = low_high(even_y, from_y[0], second_round(even_y, below_y, above_y, from_y[1]))
        total = inner + beside_in_rows(size_x, size_y, own, x_low, x_high, y_low, y_high)
        parts = [own, keep * own + rates * total] + from_x + from_y
        filled = sum(part.shape[0] for part in parts)
        parts.append(jnp.zeros((za.shape[0] - filled, LANES), F32))
        messages.append(jnp.concatenate(parts, axis=0))
    low, high = messages
    za[...] = jnp.where(even_z, high, low)
    zb[...] = jnp.where(even_z, low, high)


def steps_kernel(size_x, size_y, turns_x, gas, *refs):
    xs, refs = refs[:turns_x], refs[turns_x:]
    xs_far, refs = refs[:turns_x], refs[turns_x:]
    ya, yb, rate, deposit, out, field, side_x, side_y = refs
    species = rate.shape[1]
    lines = size_x * size_y
    even_x, below_x, above_x = place_on("gx")
    even_y, below_y, above_y = place_on("gy")
    wide = wide_rates(rate, species)
    keep = 1.0 - 6.0 * wide

    def step(source, x_halos, y_halos, store):
        planes = [[plane_at(source, x * size_y + y) for y in range(size_y)] for x in range(size_x)]

        def from_x(side, y):
            return low_high(even_x, x_halos[0][y], x_halos[1][y] if turns_x == 2 else None)[side]

        def from_y(side, x):
            return low_high(even_y, y_halos[0][x], second_round(even_y, below_y, above_y, y_halos[1][x]))[side]

        for x in range(size_x):
            for y in range(size_y):
                own = source[x * size_y + y]
                total = beside_xy(
                    planes,
                    x,
                    y,
                    functools.partial(from_x, 0),
                    functools.partial(from_x, 1),
                    functools.partial(from_y, 0),
                    functools.partial(from_y, 1),
                )
                store(x * size_y + y, keep * own + wide * (total + beside_z(own)))

    def store_field(line, value):
        field[line] = value

    step(gas, xs, (ya, yb), store_field)
    for turn, ref in enumerate(xs):
        up = even_x == (turn == 0)
        exists = jnp.where(up, above_x, below_x)
        inner = jnp.where(up, lines - size_y, 0)
        for y in range(size_y):
            own = ref[y]
            total = xs_far[turn][y] + exists * gas[inner + y]
            if y > 0:
                total = total + ref[y - 1]
            if y < size_y - 1:
                total = total + ref[y + 1]
            side_x[turn, y] = keep * own + wide * (total + beside_z(own))

    for turn, ref in enumerate((ya, yb)):
        up = even_y == (turn == 0)
        exists = jnp.where(up, above_y, below_y)
        inner = jnp.where(up, size_y - 1, 0)
        for x in range(size_x):
            own = ref[x]
            total = ref[size_x + x] + exists * gas[x * size_y + inner]
            if x > 0:
                total = total + ref[x - 1]
            if x < size_x - 1:
                total = total + ref[x + 1]
            side_y[turn, x] = keep * own + wide * (total + beside_z(own))

    def store_result(line, value):
        out[line] = value + deposit[line]

    step(field, [side_x.at[turn] for turn in range(turns_x)], [side_y.at[turn] for turn in range(2)], store_result)


def close_kernel(size_x, size_y, turns_x, partial, *refs):
    corners, (za, zb, za_in, zb_in, rate, out, result, sems) = refs[:turns_x], refs[turns_x:]
    species = rate.shape[1]
    lines = size_x * size_y
    each = LANES // species
    count, rows_x, rows_y = lines // each, size_y // each, size_x // each
    even_x, _, _ = place_on("gx")
    even_y, below_y, above_y = place_on("gy")
    even, below, above = place_on("gz")
    rates = jnp.concatenate([rate[...]] * each, axis=1)
    keep = 1.0 - 6.0 * rates
    incoming = low_high(even, za_in[...], zb_in[...])
    leaving = low_high(even, za[...], zb[...])
    outer, inner = [], []
    for column, own, exists in zip(incoming, leaving, (below, above), strict=True):
        column = rates * jnp.where(exists > 0.0, column, 0.0)
        main, partly = column[:count], column[count : 2 * count]
        at = 2 * count
        sides = [column[at + i * rows_x : at + (i + 1) * rows_x] for i in range(turns_x)]
        x_low, x_high = low_high(even_x, sides[0], sides[1] if turns_x == 2 else None)
        at = at + turns_x * rows_x
        sides = [column[at + i * rows_y : at + (i + 1) * rows_y] for i in range(2)]
        y_low, y_high = low_high(even_y, sides[0], second_round(even_y, below_y, above_y, sides[1]))
        total = beside_in_rows(size_x, size_y, main, x_low, x_high, y_low, y_high)
        outer.append(keep * main + rates * total + partly + exists * rates * rates * own[:count])
        inner.append(rates * main)

    wide = wide_rates(rate, species)
    twice = 2.0 * wide * wide
    edge = {}
    for i, y in enumerate((0, size_y - 1)):
        planes = low_high(even_x, corners[0][i], corners[1][i] if turns_x == 2 else None)
        edge[y], edge[lines - size_y + y] = planes
    turned = iota((LANES, LANES), 0)
    saves = []
    for i in range(count):
        at = slice(i, i + 1)
        block = jnp.where(turned == 0, outer[0][at], jnp.where(turned == 1, inner[0][at], 0.0))
        block = jnp.where(turned == LANES - 2, inner[1][at], block)
        block = jnp.transpose(jnp.where(turned == LANES - 1, outer[1][at], block))
        for part in range(each):
            line = i * each + part
            total = partial[line] + block[part * species : (part + 1) * species]
            if line in edge:
                total = total + twice * edge[line]
            result[line] = total
            saves.append(pltpu.make_async_copy(result.at[line], out.at[:, line, :], sems.at[line]))
            saves[-1].start()
    for save in saves:
        save.wait()


def full(shape):
    return pl.BlockSpec(shape, lambda *_: (0,) * len(shape))


def lasts(microseconds):
    return pl.CostEstimate(flops=0, bytes_accessed=int(3.69e6 * microseconds), transcendentals=0)


def in_hbm(array):
    return pltpu.with_memory_space_constraint(array, pltpu.HBM)


def in_vmem(array):
    return pltpu.with_memory_space_constraint(array, pltpu.VMEM)


def exchange(rows, group):
    width = rows.shape[1]
    chunks = rows.reshape(group, -1, width)
    chunks = lax.all_to_all(chunks, ("gy", "gz"), split_axis=0, concat_axis=0, tiled=True)
    return chunks.reshape(-1, width)


def on_device(gas, droplet, owner, cells, weights, mass, liquid_rate, surface_rate, gas_rate):
    group = lax.axis_size("gy") * lax.axis_size("gz")
    nodes, species, parcels = droplet.shape
    cap = 2 * parcels // group
    slots = group * cap
    packed = cap % 16 == 0
    lines = gas.shape[1] * gas.shape[2]
    flat = gas.reshape(species, lines, LANES)
    planes = (lines, species, LANES)
    liquid = liquid_rate.reshape(1, species)
    surface = surface_rate.reshape(1, species)
    rate_spec = full((1, species))
    size_x, size_y = gas.shape[1], gas.shape[2]
    rate = gas_rate.reshape(1, species)
    vmem = pl.BlockSpec(memory_space=pltpu.VMEM)
    hbm = pl.BlockSpec(memory_space=pl.ANY)
    whole = pl.BlockSpec()
    turns_x = len(swaps("gx"))
    x_shape = (size_y, species, LANES)
    y_shape = (2 * size_x, species, LANES)

    send, slot, near_gas, *x_faces = pl.pallas_call(
        functools.partial(pack_kernel, cap, size_x, size_y, turns_x),
        out_shape=[
            pltpu.VMEM((slots, LANES), F32),
            pltpu.VMEM((1, parcels), jnp.int32),
            pltpu.VMEM(planes, F32),
        ]
        + [pltpu.VMEM(x_shape, F32)] * (2 * turns_x),
        in_specs=[hbm] * 8,
        out_specs=[vmem] * (3 + 2 * turns_x),
        scratch_shapes=[
            pltpu.VMEM((1, parcels), jnp.int32),
            pltpu.VMEM((STENCIL, parcels), jnp.int32),
            pltpu.VMEM((STENCIL, parcels), F32),
            pltpu.VMEM((1, parcels), F32),
            pltpu.VMEM((1, species), F32),
            pltpu.VMEM((1, species), F32),
            pltpu.VMEM((DROP_STEPS, species, parcels), F32),
            pltpu.SemaphoreType.DMA((7 + lines,)),
        ],
        compiler_params=pltpu.CompilerParams(vmem_limit_bytes=8 * MIB),
        cost_estimate=lasts(2.5),
        name="pack",
    )(
        in_hbm(droplet),
        in_hbm(flat),
        in_hbm(owner.reshape(1, parcels)),
        in_hbm(cells),
        in_hbm(weights),
        in_hbm(mass.reshape(1, parcels)),
        in_hbm(liquid),
        in_hbm(surface),
    )
    rows = exchange(send, group)

    y_faces = pl.pallas_call(
        functools.partial(y_faces_kernel, size_x, size_y),
        out_shape=[pltpu.VMEM(y_shape, F32)] * 2,
        in_specs=[vmem],
        out_specs=[vmem] * 2,
        compiler_params=pltpu.CompilerParams(vmem_limit_bytes=4 * MIB),
        cost_estimate=lasts(0.6),
        name="y_faces",
    )(near_gas)
    y_halo = swap_all(y_faces, "gy", closed=True, spare="gz")
    x_near = swap_all(x_faces[:turns_x], "gx")
    x_far = swap_all(x_faces[turns_x:], "gx")

    corners = pl.pallas_call(
        functools.partial(corner_kernel, size_x),
        out_shape=[jax.ShapeDtypeStruct((2, species, LANES), F32)] * turns_x,
        in_specs=[vmem] * 2,
        out_specs=[vmem] * turns_x,
        compiler_params=pltpu.CompilerParams(vmem_limit_bytes=4 * MIB),
        cost_estimate=lasts(0.3),
        name="corner_planes",
    )(*y_halo)
    corners = swap_all(corners, "gx")

    back_rows = slots // 2 if packed else slots
    w_shape = (lines, LANES, slots)
    back, deposit = pl.pallas_call(
        functools.partial(couple_kernel, cap, packed),
        out_shape=[jax.ShapeDtypeStruct((back_rows, LANES), F32), pltpu.VMEM(planes, F32)],
        in_specs=[vmem] * 2 + [whole] * 2,
        out_specs=[hbm, vmem],
        scratch_shapes=[
            pltpu.VMEM(w_shape, BF16),
            pltpu.VMEM(w_shape, BF16),
            pltpu.VMEM((back_rows, LANES), F32),
            pltpu.SemaphoreType.DMA((1,)),
        ],
        compiler_params=pltpu.CompilerParams(vmem_limit_bytes=10 * MIB),
        cost_estimate=lasts(7.0),
        name="couple_gas",
    )(rows, near_gas, liquid, surface)

    returned = exchange(back, group)

    z_shape = (48, LANES)
    x_near, x_far, y_halo = [[in_vmem(halo) for halo in halos] for halos in (x_near, x_far, y_halo)]
    z_sends = pl.pallas_call(
        functools.partial(z_message_kernel, size_x, size_y, turns_x),
        out_shape=[jax.ShapeDtypeStruct(z_shape, F32)] * 2,
        in_specs=[vmem] * (turns_x + 3) + [whole],
        compiler_params=pltpu.CompilerParams(vmem_limit_bytes=4 * MIB),
        cost_estimate=lasts(0.6),
        name="z_message",
    )(near_gas, *x_near, *y_halo, rate)
    z_halo = swap_all(z_sends, "gz", closed=True)
    partial = pl.pallas_call(
        functools.partial(steps_kernel, size_x, size_y, turns_x),
        out_shape=pltpu.VMEM(planes, F32),
        in_specs=[vmem] * (2 * turns_x + 3) + [whole, vmem],
        out_specs=vmem,
        scratch_shapes=[
            pltpu.VMEM(planes, F32),
            pltpu.VMEM((turns_x, size_y, species, LANES), F32),
            pltpu.VMEM((2, size_x, species, LANES), F32),
        ],
        compiler_params=pltpu.CompilerParams(vmem_limit_bytes=6 * MIB),
        cost_estimate=lasts(2.2),
        name="gas_steps",
    )(near_gas, *x_near, *x_far, *y_halo, rate, in_vmem(deposit))
    gas_next = pl.pallas_call(
        functools.partial(close_kernel, size_x, size_y, turns_x),
        out_shape=jax.ShapeDtypeStruct(flat.shape, F32),
        in_specs=[vmem] * (1 + turns_x) + [whole] * 5,
        out_specs=hbm,
        scratch_shapes=[pltpu.VMEM(planes, F32), pltpu.SemaphoreType.DMA((lines,))],
        compiler_params=pltpu.CompilerParams(vmem_limit_bytes=6 * MIB),
        cost_estimate=lasts(1.5),
        name="close_gas_step",
    )(in_vmem(partial), *corners, *z_sends, *z_halo, rate)
    droplet_next = pl.pallas_call(
        functools.partial(droplet_kernel, cap, packed),
        out_shape=jax.ShapeDtypeStruct(droplet.shape, F32),
        in_specs=[whole] * 5 + [hbm],
        out_specs=hbm,
        scratch_shapes=[
            pltpu.VMEM(droplet.shape, F32),
            pltpu.VMEM((species, parcels), F32),
            pltpu.SemaphoreType.DMA((species // 8,)),
        ],
        compiler_params=pltpu.CompilerParams(vmem_limit_bytes=8 * MIB),
        cost_estimate=lasts(2.5),
        name="droplets",
    )(droplet, returned, slot, liquid, surface, in_hbm(gas_next))
    return (gas_next.reshape(gas.shape), droplet_next)


def solution(mesh):
    return jax.shard_map(
        on_device,
        mesh=mesh,
        in_specs=(
            P(None, "gx", "gy", "gz"),
            P(None, None, ("gx", "gy", "gz")),
            P(("gx", "gy", "gz"), None),
            P(None, ("gx", "gy", "gz")),
            P(None, ("gx", "gy", "gz")),
            P(("gx", "gy", "gz")),
            P(),
            P(),
            P(),
        ),
        out_specs=(P(None, "gx", "gy", "gz"), P(None, None, ("gx", "gy", "gz"))),
        check_vma=False,
    )
```

```python
import functools

import jax
import jax.numpy as jnp
from jax import lax
from jax.experimental import pallas as pl
from jax.experimental.pallas import tpu as pltpu
from jax.sharding import PartitionSpec as P

STENCIL = 8
DROP_STEPS = 4
GAS_STEPS = 2
LANES = 128
MIB = 1 << 20
NT = (((1,), (1,)), ((), ()))
HIGH = lax.Precision.HIGHEST
F32 = jnp.float32
BF16 = jnp.bfloat16


def iota(shape, dim):
    return lax.broadcasted_iota(jnp.int32, shape, dim)


def as_column(row):
    n = row.shape[1]
    return jnp.sum(jnp.where(iota((n, n), 0) == iota((n, n), 1), row, 0.0), axis=1, keepdims=True)


def leading(value):
    scaled = value * 65537.0
    return scaled - (scaled - value)


def split(value):
    high = leading(value)
    return high.astype(BF16), (value - high).astype(BF16)


def split_all(value):
    high = leading(value)
    rest = value - high
    middle = leading(rest)
    return high.astype(BF16), middle.astype(BF16), (rest - middle).astype(BF16)


def one_hot(hit):
    return jnp.where(hit, 1.0, 0.0).astype(BF16)


def surface_steps(nodes, gas_at, liquid, surface):
    emitted = None
    for step in range(DROP_STEPS):
        last = nodes[-1]
        flux = surface * (last - gas_at)
        emitted = flux if emitted is None else emitted + flux
        inner = [
            nodes[i] + liquid * (nodes[i + 1] - 2.0 * nodes[i] + nodes[i - 1])
            for i in range(1, len(nodes) - 1)
        ]
        if len(nodes) > 1:
            nodes = inner + [last + liquid * (nodes[-2] - last) - flux]
    return emitted


def surface_response(liquid, surface):
    return surface_steps([jnp.zeros_like(liquid)] * DROP_STEPS, 1.0, liquid, surface)


def pack_kernel(cap, size_x, size_y, turns_x, droplet, gas, *refs):
    sources, (send, slots, near_gas), refs = refs[:6], refs[6:9], refs[9:]
    x_sends, refs = refs[: 2 * turns_x], refs[2 * turns_x :]
    (owner, cells, weights, mass, liquid, surface), (tail, sems) = refs[:6], refs[6:]
    parcels = owner.shape[1]
    nodes, species = droplet.shape[0], droplet.shape[1]
    lines = gas.shape[1]
    pairs = list(zip(sources, refs[:6], strict=True))
    pairs.append((droplet.at[pl.ds(nodes - DROP_STEPS, DROP_STEPS)], tail))
    small = len(pairs)
    pairs += [(gas.at[:, line, :], near_gas.at[line]) for line in range(lines)]
    loads = [pltpu.make_async_copy(source, here, sems.at[i]) for i, (source, here) in enumerate(pairs)]
    for load in loads:
        load.start()
    for load in loads[: small - 1]:
        load.wait()
    wts = weights[...]
    norm = wts / jnp.sum(wts, axis=0, keepdims=True)
    mine = owner[...]
    column = jnp.transpose(jnp.broadcast_to(mine.astype(F32), (parcels, parcels)))
    earlier = (column == mine.astype(F32)) & (iota((parcels, parcels), 0) < iota((parcels, parcels), 1))
    rank = jnp.sum(jnp.where(earlier, 1.0, 0.0), axis=0, keepdims=True).astype(jnp.int32)
    slot = mine * cap + rank
    slots[...] = slot
    place = one_hot(iota((send.shape[0], parcels), 0) == slot)
    rest = jnp.zeros((LANES - species - 2 * STENCIL - 8, parcels), F32)
    liquid_col, surface_col = as_column(liquid[...]), as_column(surface[...])
    loads[small - 1].wait()
    emitted = surface_steps([tail[i] for i in range(DROP_STEPS)], 0.0, liquid_col, surface_col)
    values = jnp.concatenate(
        [
            mass[...] * emitted,
            cells[...].astype(F32),
            norm,
            jnp.broadcast_to(mass[...], (8, parcels)),
            rest,
        ],
        axis=0,
    )
    parts = jnp.concatenate(split_all(values), axis=0)
    placed = lax.dot_general(place, parts, NT, preferred_element_type=F32)
    send[...] = placed[:, :LANES] + placed[:, LANES : 2 * LANES] + placed[:, 2 * LANES :]
    for load in loads[small:]:
        load.wait()
    even_x, _, _ = place_on("gx")
    for turn in range(turns_x):
        up = even_x == (turn == 0)
        near = jnp.where(up, size_x - 1, 0) * size_y
        far = jnp.where(up, size_x - 2, 1) * size_y
        for y in range(size_y):
            x_sends[turn][y] = near_gas[near + y]
            x_sends[turns_x + turn][y] = near_gas[far + y]


def y_faces_kernel(size_x, size_y, near_gas, ya, yb):
    even_y, _, _ = place_on("gy")
    for turn, y_send in enumerate((ya, yb)):
        up = even_y == (turn == 0)
        near = jnp.where(up, size_y - 1, 0)
        far = jnp.where(up, size_y - 2, 1)
        for x in range(size_x):
            y_send[x] = near_gas[x * size_y + near]
            y_send[size_x + x] = near_gas[x * size_y + far]


def corner_kernel(size_x, ya, yb, *sends):
    even_x, _, _ = place_on("gx")
    even_y, below_y, above_y = place_on("gy")
    for turn, send in enumerate(sends):
        x = jnp.where(even_x == (turn == 0), size_x - 1, 0)
        send[0], send[1] = low_high(even_y, ya[x], second_round(even_y, below_y, above_y, yb[x]))


def couple_kernel(cap, packed, rows, gas, liquid, surface, back_out, deposit, w_high, w_low, back, sems):
    slots = rows.shape[0]
    species = liquid.shape[1]
    lines = gas.shape[0]
    table = jnp.transpose(rows[...])
    first = species
    cell = table[first : first + STENCIL]
    wts = table[first + STENCIL : first + 2 * STENCIL]
    mass = table[first + 2 * STENCIL : first + 2 * STENCIL + 1]
    whole = wts
    for shift in range(1, STENCIL):
        same = cell == pltpu.roll(cell, shift, 0)
        whole = whole + jnp.where(same, pltpu.roll(wts, shift, 0), 0.0)
    tile = 16
    cell = cell.astype(jnp.int32)
    high_rows, low_rows = split(whole)
    named = [jnp.broadcast_to(cell[k : k + 1], (tile, slots)).astype(jnp.int16) for k in range(STENCIL)]
    first_cells = iota((tile, slots), 0).astype(jnp.int16)
    highs = [jnp.broadcast_to(high_rows[k : k + 1], (tile, slots)) for k in range(STENCIL)]
    lows = [jnp.broadcast_to(low_rows[k : k + 1], (tile, slots)) for k in range(STENCIL)]

    def pair(ref, line):
        return ref[line : line + 2].reshape(2 * LANES, slots)

    gathered = jnp.zeros((species, slots), F32)
    for line in range(0, lines, 2):
        for part in range(2):
            for z in range(0, LANES, tile):
                along = first_cells + jnp.int16((line + part) * LANES + z)
                high = jnp.zeros((tile, slots), BF16)
                low = jnp.zeros((tile, slots), BF16)
                for k in range(STENCIL):
                    hit = named[k] == along
                    high = jnp.where(hit, highs[k], high)
                    low = jnp.where(hit, lows[k], low)
                w_high[line + part, z : z + tile] = high
                w_low[line + part, z : z + tile] = low
        t_high, t_low = split(jnp.concatenate([gas[line], gas[line + 1]], axis=1))
        t_all = jnp.concatenate([t_high, t_low], axis=0)
        both = jnp.dot(t_all, pair(w_high, line), preferred_element_type=F32)
        extra = jnp.dot(t_high, pair(w_low, line), preferred_element_type=F32)
        gathered = gathered + both[:species] + both[species:] + extra
    gas_rows = jnp.transpose(gathered)
    if packed:
        gas_rows = gas_rows.reshape(slots // cap, cap, species)
        gas_rows = jnp.concatenate([gas_rows[:, : cap // 2], gas_rows[:, cap // 2 :]], axis=2)
        back[...] = gas_rows.reshape(slots // 2, 2 * species)
    else:
        back[...] = jnp.concatenate([gas_rows, jnp.zeros((slots, LANES - species), F32)], axis=1)
    save = pltpu.make_async_copy(back, back_out, sems.at[0])
    save.start()
    response = surface_response(as_column(liquid[...]), as_column(surface[...]))
    s_high, s_low = split(table[:species] + mass * (response * gathered))
    s_all = jnp.concatenate([s_high, s_low], axis=0)
    s_only = jnp.concatenate([s_high, jnp.zeros_like(s_low)], axis=0)
    for line in range(0, lines, 2):
        both = lax.dot_general(pair(w_high, line), s_all, NT, preferred_element_type=F32)
        both = both + lax.dot_general(pair(w_low, line), s_only, NT, preferred_element_type=F32)
        for i in range(2):
            turned = jnp.transpose(both[i * LANES : (i + 1) * LANES])
            deposit[line + i] = turned[:species] + turned[species:]
    save.wait()


def droplet_kernel(
    cap, packed, state_in, rows, slots, liquid, surface, _, state_out, state_next, gas_at, sems
):
    nodes, species, parcels = state_in.shape
    block = 8

    table = jnp.transpose(rows[...])
    count = rows.shape[0]
    at = iota((count, parcels), 0)
    slot = slots[...]
    if packed:
        half = cap // 2
        at = at // half * cap + at % half
        pairs = [(table[:species], at), (table[species:], at + half)]
    else:
        pairs = [(table[:species], at)]
    total = jnp.zeros((species, parcels), F32)
    for values, index in pairs:
        parts = jnp.concatenate(split_all(values), axis=0)
        placed = jnp.dot(parts, one_hot(index == slot), preferred_element_type=F32)
        total = total + placed[:species] + placed[species : 2 * species] + placed[2 * species :]
    gas_at[...] = total

    def save(i):
        at = pl.ds(i * block, block)
        return pltpu.make_async_copy(state_next.at[:, at], state_out.at[:, at], sems.at[i])

    @pl.loop(0, species // block, unroll=8)
    def _(i):
        at = pl.ds(pl.multiple_of(i * block, block), block)
        pick = i * block + iota((block, species), 0) == iota((block, species), 1)
        liquid_col = jnp.sum(jnp.where(pick, liquid[...], 0.0), axis=1, keepdims=True)
        surface_col = jnp.sum(jnp.where(pick, surface[...], 0.0), axis=1, keepdims=True)
        rate = jnp.broadcast_to(liquid_col, (block, parcels))
        keep = 1.0 - 2.0 * rate
        last_keep = jnp.broadcast_to(1.0 - liquid_col - surface_col, (block, parcels))
        from_gas = surface_col * gas_at[at, :]
        state = [state_in[node, at] for node in range(nodes)]
        for step in range(DROP_STEPS):
            state = (
                [keep * state[0] + (rate + rate) * state[1]]
                + [keep * state[n] + rate * (state[n - 1] + state[n + 1]) for n in range(1, nodes - 1)]
                + [last_keep * state[-1] + rate * state[-2] + from_gas]
            )
        for node in range(nodes):
            state_next[node, at] = state[node]
        save(i).start()

    for i in range(species // block):
        save(i).wait()


def place_on(axis):
    index, count = lax.axis_index(axis), lax.axis_size(axis)
    even = lax.rem(index, 2) == 0
    below = jnp.where(index > 0, 1.0, 0.0).astype(F32)
    above = jnp.where(index < count - 1, 1.0, 0.0).astype(F32)
    return even, below, above


def swaps(axis, closed=False, spare=None):
    count = lax.axis_size(axis)
    across = 1 if spare is None else lax.axis_size(spare)
    rounds = []
    for first in range(2):
        pairs = [(i * across + j, (i + 1) * across + j) for i in range(first, count - 1, 2) for j in range(across)]
        if closed and first == 1 and count > 2 and count % 2 == 0:
            if spare is None:
                pairs.append((count - 1, 0))
            elif across % 2 == 0:
                pairs += [(i * across + j, i * across + j + 1) for i in (0, count - 1) for j in range(0, across, 2)]
        if pairs:
            rounds.append(pairs + [(j, i) for i, j in pairs])
    return rounds


def swap_all(messages, axis, closed=False, spare=None):
    axes = axis if spare is None else (axis, spare)
    return [lax.ppermute(m, axes, pairs) for m, pairs in zip(messages, swaps(axis, closed, spare), strict=True)]


def second_round(even, below, above, block):
    return jnp.where(jnp.where(even, below, above) > 0.0, block, 0.0)


def low_high(even, first, second):
    if second is None:
        second = jnp.zeros_like(first)
    return jnp.where(even, second, first), jnp.where(even, first, second)


def beside_z(block):
    axis = block.ndim - 1
    lane = iota(block.shape, axis)
    before = jnp.where(lane == 0, 0.0, pltpu.roll(block, 1, axis))
    after = jnp.where(lane == LANES - 1, 0.0, pltpu.roll(block, LANES - 1, axis))
    return before + after


def beside_xy(planes, x, y, x_low, x_high, y_low, y_high):
    size_x, size_y = len(planes), len(planes[0])
    total = planes[x - 1][y]() if x > 0 else x_low(y)
    total = total + (planes[x + 1][y]() if x < size_x - 1 else x_high(y))
    total = total + (planes[x][y - 1]() if y > 0 else y_low(x))
    return total + (planes[x][y + 1]() if y < size_y - 1 else y_high(x))


def plane_at(ref, index):
    return lambda: ref[index]


def wide_rates(rate, rows):
    column = as_column(rate[...])
    column = jnp.concatenate([column] * (rows // column.shape[0]), axis=0)
    return jnp.broadcast_to(column, (rows, LANES))


def beside_in_rows(size_x, size_y, main, x_low, x_high, y_low, y_high):
    count = main.shape[0]
    each = size_x * size_y // count
    species = LANES // each
    rows_x = size_y // each
    row, lane = iota((count, LANES), 0), iota((count, LANES), 1)
    first_place = (lane < species) & (row % rows_x == 0)
    last_place = (lane >= LANES - species) & (row % rows_x == rows_x - 1)
    blank = jnp.zeros((rows_x - 1, LANES), F32)
    low_rows, high_rows = [], []
    for x in range(size_x):
        i, part = x // each, x % each
        low_row, high_row = y_low[i : i + 1], y_high[i : i + 1]
        if part > 0:
            low_row = pltpu.roll(low_row, LANES - part * species, 1)
        if part < each - 1:
            high_row = pltpu.roll(high_row, (each - 1 - part) * species, 1)
        low_rows += [low_row, blank]
        high_rows += [blank, high_row]
    ahead = pltpu.roll(main, LANES - species, 1)
    after = jnp.where(lane >= LANES - species, jnp.concatenate([ahead[1:], ahead[-1:]], axis=0), ahead)
    after = jnp.where(last_place, jnp.concatenate(high_rows, axis=0), after)
    behind = pltpu.roll(main, species, 1)
    before = jnp.where(lane < species, jnp.concatenate([behind[:1], behind[:-1]], axis=0), behind)
    before = jnp.where(first_place, jnp.concatenate(low_rows, axis=0), before)
    total = before + after + jnp.concatenate([x_low, main[:-rows_x]], axis=0)
    return total + jnp.concatenate([main[rows_x:], x_high], axis=0)


def z_message_kernel(size_x, size_y, turns_x, gas, *refs):
    xs, (ya, yb, rate, za, zb) = refs[:turns_x], refs[turns_x:]
    species = rate.shape[1]
    lines = size_x * size_y
    each = LANES // species
    rates = jnp.concatenate([rate[...]] * each, axis=1)
    keep = 1.0 - 6.0 * rates
    even_x, _, _ = place_on("gx")
    even_y, below_y, above_y = place_on("gy")
    even_z, _, _ = place_on("gz")

    def columns(ref):
        turned = [jnp.transpose(ref[i : i + each].reshape(LANES, LANES)) for i in range(0, ref.shape[0], each)]
        return [jnp.concatenate([t[z : z + 1] for t in turned], axis=0) for z in (0, 1, LANES - 1, LANES - 2)]

    main = columns(gas)
    x_sides = [columns(x) for x in xs]
    y_sides = [columns(y.at[:size_x]) for y in (ya, yb)]
    messages = []
    for side in range(2):
        own, inner = main[2 * side], main[2 * side + 1]
        from_x = [columns_of_x[2 * side] for columns_of_x in x_sides]
        from_y = [columns_of_y[2 * side] for columns_of_y in y_sides]
        x_low, x_high = low_high(even_x, from_x[0], from_x[1] if turns_x == 2 else None)
        y_low, y_high = low_high(even_y, from_y[0], second_round(even_y, below_y, above_y, from_y[1]))
        total = inner + beside_in_rows(size_x, size_y, own, x_low, x_high, y_low, y_high)
        parts = [own, keep * own + rates * total] + from_x + from_y
        filled = sum(part.shape[0] for part in parts)
        parts.append(jnp.zeros((za.shape[0] - filled, LANES), F32))
        messages.append(jnp.concatenate(parts, axis=0))
    low, high = messages
    za[...] = jnp.where(even_z, high, low)
    zb[...] = jnp.where(even_z, low, high)


def steps_kernel(size_x, size_y, turns_x, gas, *refs):
    xs, refs = refs[:turns_x], refs[turns_x:]
    xs_far, refs = refs[:turns_x], refs[turns_x:]
    ya, yb, rate, deposit, out, field, side_x, side_y = refs
    species = rate.shape[1]
    lines = size_x * size_y
    even_x, below_x, above_x = place_on("gx")
    even_y, below_y, above_y = place_on("gy")
    wide = wide_rates(rate, species)
    keep = 1.0 - 6.0 * wide

    def step(source, x_halos, y_halos, store):
        planes = [[plane_at(source, x * size_y + y) for y in range(size_y)] for x in range(size_x)]

        def from_x(side, y):
            return low_high(even_x, x_halos[0][y], x_halos[1][y] if turns_x == 2 else None)[side]

        def from_y(side, x):
            return low_high(even_y, y_halos[0][x], second_round(even_y, below_y, above_y, y_halos[1][x]))[side]

        for x in range(size_x):
            for y in range(size_y):
                own = source[x * size_y + y]
                total = beside_xy(
                    planes,
                    x,
                    y,
                    functools.partial(from_x, 0),
                    functools.partial(from_x, 1),
                    functools.partial(from_y, 0),
                    functools.partial(from_y, 1),
                )
                store(x * size_y + y, keep * own + wide * (total + beside_z(own)))

    def store_field(line, value):
        field[line] = value

    step(gas, xs, (ya, yb), store_field)
    for turn, ref in enumerate(xs):
        up = even_x == (turn == 0)
        exists = jnp.where(up, above_x, below_x)
        inner = jnp.where(up, lines - size_y, 0)
        for y in range(size_y):
            own = ref[y]
            total = xs_far[turn][y] + exists * gas[inner + y]
            if y > 0:
                total = total + ref[y - 1]
            if y < size_y - 1:
                total = total + ref[y + 1]
            side_x[turn, y] = keep * own + wide * (total + beside_z(own))

    for turn, ref in enumerate((ya, yb)):
        up = even_y == (turn == 0)
        exists = jnp.where(up, above_y, below_y)
        inner = jnp.where(up, size_y - 1, 0)
        for x in range(size_x):
            own = ref[x]
            total = ref[size_x + x] + exists * gas[x * size_y + inner]
            if x > 0:
                total = total + ref[x - 1]
            if x < size_x - 1:
                total = total + ref[x + 1]
            side_y[turn, x] = keep * own + wide * (total + beside_z(own))

    def store_result(line, value):
        out[line] = value + deposit[line]

    step(field, [side_x.at[turn] for turn in range(turns_x)], [side_y.at[turn] for turn in range(2)], store_result)


def close_kernel(size_x, size_y, turns_x, partial, *refs):
    corners, (za, zb, za_in, zb_in, rate, out, result, sems) = refs[:turns_x], refs[turns_x:]
    species = rate.shape[1]
    lines = size_x * size_y
    each = LANES // species
    count, rows_x, rows_y = lines // each, size_y // each, size_x // each
    even_x, _, _ = place_on("gx")
    even_y, below_y, above_y = place_on("gy")
    even, below, above = place_on("gz")
    rates = jnp.concatenate([rate[...]] * each, axis=1)
    keep = 1.0 - 6.0 * rates
    incoming = low_high(even, za_in[...], zb_in[...])
    leaving = low_high(even, za[...], zb[...])
    outer, inner = [], []
    for column, own, exists in zip(incoming, leaving, (below, above), strict=True):
        column = rates * jnp.where(exists > 0.0, column, 0.0)
        main, partly = column[:count], column[count : 2 * count]
        at = 2 * count
        sides = [column[at + i * rows_x : at + (i + 1) * rows_x] for i in range(turns_x)]
        x_low, x_high = low_high(even_x, sides[0], sides[1] if turns_x == 2 else None)
        at = at + turns_x * rows_x
        sides = [column[at + i * rows_y : at + (i + 1) * rows_y] for i in range(2)]
        y_low, y_high = low_high(even_y, sides[0], second_round(even_y, below_y, above_y, sides[1]))
        total = beside_in_rows(size_x, size_y, main, x_low, x_high, y_low, y_high)
        outer.append(keep * main + rates * total + partly + exists * rates * rates * own[:count])
        inner.append(rates * main)

    wide = wide_rates(rate, species)
    twice = 2.0 * wide * wide
    edge = {}
    for i, y in enumerate((0, size_y - 1)):
        planes = low_high(even_x, corners[0][i], corners[1][i] if turns_x == 2 else None)
        edge[y], edge[lines - size_y + y] = planes
    turned = iota((LANES, LANES), 0)
    saves = []
    for i in range(count):
        at = slice(i, i + 1)
        block = jnp.where(turned == 0, outer[0][at], jnp.where(turned == 1, inner[0][at], 0.0))
        block = jnp.where(turned == LANES - 2, inner[1][at], block)
        block = jnp.transpose(jnp.where(turned == LANES - 1, outer[1][at], block))
        for part in range(each):
            line = i * each + part
            total = partial[line] + block[part * species : (part + 1) * species]
            if line in edge:
                total = total + twice * edge[line]
            result[line] = total
            saves.append(pltpu.make_async_copy(result.at[line], out.at[:, line, :], sems.at[line]))
            saves[-1].start()
    for save in saves:
        save.wait()


def full(shape):
    return pl.BlockSpec(shape, lambda *_: (0,) * len(shape))


def lasts(microseconds):
    return pl.CostEstimate(flops=0, bytes_accessed=int(3.69e6 * microseconds), transcendentals=0)


def in_hbm(array):
    return pltpu.with_memory_space_constraint(array, pltpu.HBM)


def in_vmem(array):
    return pltpu.with_memory_space_constraint(array, pltpu.VMEM)


def exchange(rows, group):
    width = rows.shape[1]
    chunks = rows.reshape(group, -1, width)
    chunks = lax.all_to_all(chunks, ("gy", "gz"), split_axis=0, concat_axis=0, tiled=True)
    return chunks.reshape(-1, width)


def on_device(gas, droplet, owner, cells, weights, mass, liquid_rate, surface_rate, gas_rate):
    group = lax.axis_size("gy") * lax.axis_size("gz")
    nodes, species, parcels = droplet.shape
    cap = 2 * parcels // group
    slots = group * cap
    packed = cap % 16 == 0
    lines = gas.shape[1] * gas.shape[2]
    flat = gas.reshape(species, lines, LANES)
    planes = (lines, species, LANES)
    liquid = liquid_rate.reshape(1, species)
    surface = surface_rate.reshape(1, species)
    rate_spec = full((1, species))
    size_x, size_y = gas.shape[1], gas.shape[2]
    rate = gas_rate.reshape(1, species)
    vmem = pl.BlockSpec(memory_space=pltpu.VMEM)
    hbm = pl.BlockSpec(memory_space=pl.ANY)
    whole = pl.BlockSpec()
    turns_x = len(swaps("gx"))
    x_shape = (size_y, species, LANES)
    y_shape = (2 * size_x, species, LANES)

    send, slot, near_gas, *x_faces = pl.pallas_call(
        functools.partial(pack_kernel, cap, size_x, size_y, turns_x),
        out_shape=[
            pltpu.VMEM((slots, LANES), F32),
            pltpu.VMEM((1, parcels), jnp.int32),
            pltpu.VMEM(planes, F32),
        ]
        + [pltpu.VMEM(x_shape, F32)] * (2 * turns_x),
        in_specs=[hbm] * 8,
        out_specs=[vmem] * (3 + 2 * turns_x),
        scratch_shapes=[
            pltpu.VMEM((1, parcels), jnp.int32),
            pltpu.VMEM((STENCIL, parcels), jnp.int32),
            pltpu.VMEM((STENCIL, parcels), F32),
            pltpu.VMEM((1, parcels), F32),
            pltpu.VMEM((1, species), F32),
            pltpu.VMEM((1, species), F32),
            pltpu.VMEM((DROP_STEPS, species, parcels), F32),
            pltpu.SemaphoreType.DMA((7 + lines,)),
        ],
        compiler_params=pltpu.CompilerParams(vmem_limit_bytes=8 * MIB),
        cost_estimate=lasts(2.5),
        name="pack",
    )(
        in_hbm(droplet),
        in_hbm(flat),
        in_hbm(owner.reshape(1, parcels)),
        in_hbm(cells),
        in_hbm(weights),
        in_hbm(mass.reshape(1, parcels)),
        in_hbm(liquid),
        in_hbm(surface),
    )
    rows = exchange(send, group)

    y_faces = pl.pallas_call(
        functools.partial(y_faces_kernel, size_x, size_y),
        out_shape=[pltpu.VMEM(y_shape, F32)] * 2,
        in_specs=[vmem],
        out_specs=[vmem] * 2,
        compiler_params=pltpu.CompilerParams(vmem_limit_bytes=4 * MIB),
        cost_estimate=lasts(0.6),
        name="y_faces",
    )(near_gas)
    y_halo = swap_all(y_faces, "gy", closed=True, spare="gz")
    x_near = swap_all(x_faces[:turns_x], "gx")
    x_far = swap_all(x_faces[turns_x:], "gx")

    corners = pl.pallas_call(
        functools.partial(corner_kernel, size_x),
        out_shape=[jax.ShapeDtypeStruct((2, species, LANES), F32)] * turns_x,
        in_specs=[vmem] * 2,
        out_specs=[vmem] * turns_x,
        compiler_params=pltpu.CompilerParams(vmem_limit_bytes=4 * MIB),
        cost_estimate=lasts(0.3),
        name="corner_planes",
    )(*y_halo)
    corners = swap_all(corners, "gx")

    back_rows = slots // 2 if packed else slots
    w_shape = (lines, LANES, slots)
    back, deposit = pl.pallas_call(
        functools.partial(couple_kernel, cap, packed),
        out_shape=[jax.ShapeDtypeStruct((back_rows, LANES), F32), pltpu.VMEM(planes, F32)],
        in_specs=[vmem] * 2 + [whole] * 2,
        out_specs=[hbm, vmem],
        scratch_shapes=[
            pltpu.VMEM(w_shape, BF16),
            pltpu.VMEM(w_shape, BF16),
            pltpu.VMEM((back_rows, LANES), F32),
            pltpu.SemaphoreType.DMA((1,)),
        ],
        compiler_params=pltpu.CompilerParams(vmem_limit_bytes=10 * MIB),
        cost_estimate=lasts(7.0),
        name="couple_gas",
    )(rows, near_gas, liquid, surface)

    returned = exchange(back, group)

    z_shape = (48, LANES)
    x_near, x_far, y_halo = [[in_vmem(halo) for halo in halos] for halos in (x_near, x_far, y_halo)]
    z_sends = pl.pallas_call(
        functools.partial(z_message_kernel, size_x, size_y, turns_x),
        out_shape=[jax.ShapeDtypeStruct(z_shape, F32)] * 2,
        in_specs=[vmem] * (turns_x + 3) + [whole],
        compiler_params=pltpu.CompilerParams(vmem_limit_bytes=4 * MIB),
        cost_estimate=lasts(0.6),
        name="z_message",
    )(near_gas, *x_near, *y_halo, rate)
    z_halo = swap_all(z_sends, "gz", closed=True)
    partial = pl.pallas_call(
        functools.partial(steps_kernel, size_x, size_y, turns_x),
        out_shape=pltpu.VMEM(planes, F32),
        in_specs=[vmem] * (2 * turns_x + 3) + [whole, vmem],
        out_specs=vmem,
        scratch_shapes=[
            pltpu.VMEM(planes, F32),
            pltpu.VMEM((turns_x, size_y, species, LANES), F32),
            pltpu.VMEM((2, size_x, species, LANES), F32),
        ],
        compiler_params=pltpu.CompilerParams(vmem_limit_bytes=6 * MIB),
        cost_estimate=lasts(2.2),
        name="gas_steps",
    )(near_gas, *x_near, *x_far, *y_halo, rate, in_vmem(deposit))
    gas_next = pl.pallas_call(
        functools.partial(close_kernel, size_x, size_y, turns_x),
        out_shape=jax.ShapeDtypeStruct(flat.shape, F32),
        in_specs=[vmem] * (1 + turns_x) + [whole] * 5,
        out_specs=hbm,
        scratch_shapes=[pltpu.VMEM(planes, F32), pltpu.SemaphoreType.DMA((lines,))],
        compiler_params=pltpu.CompilerParams(vmem_limit_bytes=6 * MIB),
        cost_estimate=lasts(1.5),
        name="close_gas_step",
    )(in_vmem(partial), *corners, *z_sends, *z_halo, rate)
    droplet_next = pl.pallas_call(
        functools.partial(droplet_kernel, cap, packed),
        out_shape=jax.ShapeDtypeStruct(droplet.shape, F32),
        in_specs=[whole] * 5 + [hbm],
        out_specs=hbm,
        scratch_shapes=[
            pltpu.VMEM(droplet.shape, F32),
            pltpu.VMEM((species, parcels), F32),
            pltpu.SemaphoreType.DMA((species // 8,)),
        ],
        compiler_params=pltpu.CompilerParams(vmem_limit_bytes=8 * MIB),
        cost_estimate=lasts(2.5),
        name="droplets",
    )(droplet, returned, slot, liquid, surface, in_hbm(gas_next))
    return (gas_next.reshape(gas.shape), droplet_next)


def solution(mesh):
    return jax.shard_map(
        on_device,
        mesh=mesh,
        in_specs=(
            P(None, "gx", "gy", "gz"),
            P(None, None, ("gx", "gy", "gz")),
            P(("gx", "gy", "gz"), None),
            P(None, ("gx", "gy", "gz")),
            P(None, ("gx", "gy", "gz")),
            P(("gx", "gy", "gz")),
            P(),
            P(),
            P(),
        ),
        out_specs=(P(None, "gx", "gy", "gz"), P(None, None, ("gx", "gy", "gz"))),
        check_vma=False,
    )
```
